32 devices in a mesh: dp: 2 (over y), fsdp: 16 (over z, x, core).
Axes of the slice: x: 2, y: 2, z: 4, core: 2. Of those that a mesh axis runs over, the one named last changes fastest.
Arguments:
- field_five: bfloat16 [192, 5, 5, 512], P(('dp', 'fsdp')), may hold values from -6 to 6
- field_seven: bfloat16 [64, 7, 7, 512], P(('dp', 'fsdp')), may hold values from -6 to 6
- field_nine: bfloat16 [64, 9, 9, 512], P(('dp', 'fsdp')), may hold values from -6 to 6
- mask_five: int32 [192, 5, 5], P(('dp', 'fsdp')), may hold values from 0 to 1, as said below
- mask_seven: int32 [64, 7, 7], P(('dp', 'fsdp')), may hold values from 0 to 1, as said below
- mask_nine: int32 [64, 9, 9], P(('dp', 'fsdp')), may hold values from 0 to 1, as said below
- back_five: bfloat16 [192, 5, 5, 512], P(('dp', 'fsdp')), may hold values from -6 to 6
- back_seven: bfloat16 [64, 7, 7, 512], P(('dp', 'fsdp')), may hold values from -6 to 6
- back_nine: bfloat16 [64, 9, 9, 512], P(('dp', 'fsdp')), may hold values from -6 to 6
- kernels: float32 [2, 3, 3, 512, 512], P(None, None, None, None, 'fsdp'), may hold values from -0.09375 to 0.09375
- norm_params: float32 [4, 512], P(None, 'fsdp'), may hold values from 0.4 to 1.6
- kernel_first: float32 [2, 3, 3, 512, 512], P(None, None, None, None, 'fsdp'), may hold values from -320 to 320
- kernel_second: float32 [2, 3, 3, 512, 512], P(None, None, None, None, 'fsdp'), may hold values from 2624 to 10496
- norm_first: float32 [4, 512], P(None, 'fsdp'), may hold values from -320 to 320
- norm_second: float32 [4, 512], P(None, 'fsdp'), may hold values from 2624 to 10496
Outputs:
- out_five: bfloat16 [192, 5, 5, 512], P(('dp', 'fsdp'))
- out_seven: bfloat16 [64, 7, 7, 512], P(('dp', 'fsdp'))
- out_nine: bfloat16 [64, 9, 9, 512], P(('dp', 'fsdp'))
- grad_five: float32 [192, 5, 5, 512], P(('dp', 'fsdp'))
- grad_seven: float32 [64, 7, 7, 512], P(('dp', 'fsdp'))
- grad_nine: float32 [64, 9, 9, 512], P(('dp', 'fsdp'))
- kernels_next: float32 [2, 3, 3, 512, 512], P(None, None, None, None, 'fsdp')
- kernel_first_next: float32 [2, 3, 3, 512, 512], P(None, None, None, None, 'fsdp')
- kernel_second_next: float32 [2, 3, 3, 512, 512], P(None, None, None, None, 'fsdp')
- norm_next: float32 [4, 512], P(None, 'fsdp')
- norm_first_next: float32 [4, 512], P(None, 'fsdp')
- norm_second_next: float32 [4, 512], P(None, 'fsdp')
The draws below stay inside these ranges and needn't reach their ends.
Inputs may be any that keep to these rules, and one draw needn't show every extreme that they name: `mask_five`: 1 marks a valid pixel; the valid pixels of an image form a rectangle at its top-left corner, which may be empty. `mask_seven`: 1 marks a valid pixel; the valid pixels of an image form a rectangle at its top-left corner, which may be empty. `mask_nine`: 1 marks a valid pixel; the valid pixels of an image form a rectangle at its top-left corner, which may be empty.
All inputs are finite; a program needn't handle non-finite values.
Results may differ from the reference program's by a relative error of at most 0.0097.
Values may be sent and summed in bfloat16 or wider, within the bound.
No kernel may reach another device: no remote copies, remote signals or barrier semaphores. Data moves between devices by JAX's collectives and lax.ppermute only.
A program may use at most 128 MiB of HBM per device.

```python
import math
import jax
import jax.numpy as jnp
from jax import lax

C = 512
S5 = 6
S7 = 2
S9 = 2
STEP = 5
IMG5 = 192
IMG7 = 64
IMG9 = 64
PIXELS = 13120
N_DP = 2
N_FSDP = 16


def mask_draw(key, slots, edge):
    devices = N_DP * N_FSDP
    images = devices * slots
    owner_index = jnp.arange(images, dtype=jnp.int32) // slots
    slot_index = jnp.arange(images, dtype=jnp.int32) % slots
    across = owner_index // N_FSDP * (N_FSDP - 1) + owner_index % N_FSDP * (N_DP - 1)
    extent = max(2 * (N_DP - 1) * (N_FSDP - 1), 1)
    remain = extent - across
    live_slots = slots - slots // 2 * remain // extent
    row_key, col_key = jax.random.split(key)
    height = jnp.clip(edge - (edge - 2) * remain // extent - jax.random.randint(row_key, (images,), 0, 2), 1, edge)
    span_cols = jnp.clip(edge - (edge - 2) * remain // extent - jax.random.randint(col_key, (images,), 0, 2), 1, edge)
    positions = jnp.arange(edge, dtype=jnp.int32)
    inside = (slot_index < live_slots)[:, None, None] & (positions[None, :, None] < height[:, None, None]) & (positions[None, None, :] < span_cols[:, None, None])
    return inside.astype(jnp.int32)


def draw_mask_five(key, part):
    key = jax.random.fold_in(key, 5)
    return mask_draw(key, S5, 5)


def draw_mask_seven(key, part):
    key = jax.random.fold_in(key, 7)
    return mask_draw(key, S7, 7)


def draw_mask_nine(key, part):
    key = jax.random.fold_in(key, 9)
    return mask_draw(key, S9, 9)


def levels(key, shape, cuts, low, top_value):
    def one(axis_at, shards_of):
        draws = jax.random.uniform(jax.random.fold_in(jax.random.fold_in(key, 6), axis_at), (shards_of,), jnp.float32, low / len(cuts), top_value / len(cuts))
        return jnp.repeat(jnp.exp(draws), shape[axis_at] // shards_of).reshape((-1,) + (1,) * (len(shape) - axis_at - 1))

    loudness = one(*cuts[0])
    for cut in cuts[1:]:
        loudness = loudness * one(*cut)
    return loudness


def centred(stream_key, dims, scale, most, cuts=(), kind=jnp.bfloat16):
    result = scale * jax.random.normal(stream_key, dims, jnp.float32)
    if cuts:
        result = result * levels(stream_key, dims, cuts, -0.22, 0.18)
    return jnp.clip(result, -most, most).astype(kind)


def setup_inputs(seed: int = 0) -> dict:
    key_of = jax.random.split(jax.random.key(seed), 16)
    field_five = centred(key_of[0], (IMG5, 5, 5, C), 1.0, 6.0, ((0, 32),))
    field_seven = centred(key_of[1], (IMG7, 7, 7, C), 1.0, 6.0, ((0, 32),))
    field_nine = centred(key_of[2], (IMG9, 9, 9, C), 1.0, 6.0, ((0, 32),))
    mask_five = draw_mask_five(jax.random.fold_in(key_of[15], 71), 0)
    mask_seven = draw_mask_seven(jax.random.fold_in(key_of[15], 71), 0)
    mask_nine = draw_mask_nine(jax.random.fold_in(key_of[15], 71), 0)
    back_five = centred(key_of[6], (IMG5, 5, 5, C), 1.0, 6.0, ((0, 32),))
    back_seven = centred(key_of[7], (IMG7, 7, 7, C), 1.0, 6.0, ((0, 32),))
    back_nine = centred(key_of[8], (IMG9, 9, 9, C), 1.0, 6.0, ((0, 32),))
    kernels = centred(key_of[9], (2, 3, 3, C, C), (9 * C) ** -0.5, 0.09375, ((4, 16),), jnp.float32)
    norm_params = jnp.clip(1.0 + 0.12 * jax.random.normal(key_of[10], (4, C), jnp.float32), 0.4, 1.6)
    kernel_first = centred(key_of[11], (2, 3, 3, C, C), ((PIXELS // 5) ** 0.5), 320.0, ((4, 16),), jnp.float32)
    kernel_second = jnp.clip(jnp.exp(math.log(10496.0) - 1.3862944 * jax.random.uniform(key_of[12], (2, 3, 3, C, C), jnp.float32) ** levels(key_of[12], (2, 3, 3, C, C), ((4, 16),), -0.2, 0.2)), 2624.0, 10496.0)
    norm_first = centred(key_of[13], (4, C), ((PIXELS // 5) ** 0.5), 320.0, ((1, 16),), jnp.float32)
    norm_second = jnp.clip(jnp.exp(math.log(10496.0) - 1.3862944 * jax.random.uniform(key_of[14], (4, C), jnp.float32) ** levels(key_of[14], (4, C), ((1, 16),), -0.2, 0.2)), 2624.0, 10496.0)
    return dict(field_five=field_five, field_seven=field_seven, field_nine=field_nine, mask_five=mask_five, mask_seven=mask_seven, mask_nine=mask_nine, back_five=back_five, back_seven=back_seven, back_nine=back_nine, kernels=kernels, norm_params=norm_params, kernel_first=kernel_first, kernel_second=kernel_second, norm_first=norm_first, norm_second=norm_second)


@jax.custom_vjp
def low(v):
    return lax.optimization_barrier(v.astype(jnp.bfloat16)).astype(jnp.float32)

@jax.custom_vjp
def low_back(v):
    return v

def low_keep(v):
    return (low(v), None)

def low_pass(kept, grad):
    return (grad,)

def back_keep(v):
    return (v, None)

def back_low(kept, grad):
    return (low(grad),)
low.defvjp(low_keep, low_pass)
low_back.defvjp(back_keep, back_low)
NORM_EPS = 1e-05
BETA_ONE = 0.5
BETA_TWO = 0.5
KERNEL_RATE = 0.03
NORM_RATE = 0.4
KERNEL_DECAY = 0.01
ADAM_EPS = 1e-08

def swish(value):
    return value * jax.nn.sigmoid(value)

def convolve(field, kernel):
    return lax.conv_general_dilated(field, kernel, (1, 1), ((1, 1), (1, 1)), dimension_numbers=('NHWC', 'HWIO', 'NHWC'), precision=lax.Precision.HIGHEST)

def normalize(hidden, expanded, total, gain, shift):
    centre = sum((lax.optimization_barrier(jnp.sum(feature * weight, axis=(0, 1, 2))) for feature, weight in zip(hidden, expanded))) / total
    spread = sum((lax.optimization_barrier(jnp.sum(jnp.square(feature - centre) * weight, axis=(0, 1, 2))) for feature, weight in zip(hidden, expanded))) / total
    inv_std = lax.rsqrt(spread + NORM_EPS)
    return [(feature - centre) * inv_std * gain + shift for feature in hidden]

def forward(fields, expanded, kernels, norm_params):
    kernel_low = low(kernels)
    params_low = low(norm_params)
    total = sum((jnp.sum(weight) for weight in expanded))
    sources = [field * weight for field, weight in zip(fields, expanded)]
    first = [low_back(convolve(source, kernel_low[0])) for source in sources]
    normal_one = normalize(first, expanded, total, params_low[0], params_low[1])
    actives = [low(swish(value) * weight) for value, weight in zip(normal_one, expanded)]
    second = [low_back(convolve(active, kernel_low[1])) for active in actives]
    normal_two = normalize(second, expanded, total, params_low[2], params_low[3])
    return [swish(value + field) * weight for value, field, weight in zip(normal_two, fields, expanded)]

def adamw(param, grad, first, second, rate, decay):
    first_new = BETA_ONE * first + (1.0 - BETA_ONE) * grad
    second_new = BETA_TWO * second + (1.0 - BETA_TWO) * grad * grad
    first_hat = first_new / (1.0 - BETA_ONE ** STEP)
    second_hat = second_new / (1.0 - BETA_TWO ** STEP)
    update = first_hat / (jnp.sqrt(second_hat) + ADAM_EPS)
    return (param - rate * (update + decay * param), first_new, second_new)

def reference(field_five, field_seven, field_nine, mask_five, mask_seven, mask_nine, back_five, back_seven, back_nine, kernels, norm_params, kernel_first, kernel_second, norm_first, norm_second):
    fields = [field.astype(jnp.float32) for field in (field_five, field_seven, field_nine)]
    expanded = [mask.astype(jnp.float32)[..., None] for mask in (mask_five, mask_seven, mask_nine)]
    backs = [cotangent.astype(jnp.float32) for cotangent in (back_five, back_seven, back_nine)]

    def apply(fields_in, kernels_in, params_in):
        return forward(fields_in, expanded, kernels_in, params_in)
    outputs, pull = jax.vjp(apply, fields, kernels, norm_params)
    grad_fields, grad_kernels, grad_params = pull(backs)
    kernels_next, kernel_first_next, kernel_second_next = adamw(kernels, grad_kernels, kernel_first, kernel_second, KERNEL_RATE, KERNEL_DECAY)
    norm_next, norm_first_next, norm_second_next = adamw(norm_params, grad_params, norm_first, norm_second, NORM_RATE, 0.0)
    return (outputs[0].astype(jnp.bfloat16), outputs[1].astype(jnp.bfloat16), outputs[2].astype(jnp.bfloat16), grad_fields[0], grad_fields[1], grad_fields[2], kernels_next, kernel_first_next, kernel_second_next, norm_next, norm_first_next, norm_second_next)
```

```python
import functools

import jax
import jax.numpy as jnp
from jax import lax
from jax.experimental import pallas as pl
from jax.experimental.pallas import tpu as pltpu
from jax.sharding import PartitionSpec as P

STEP = 5
NORM_EPS = 1e-05
BETA_ONE = 0.5
BETA_TWO = 0.5
KERNEL_RATE = 0.03
NORM_RATE = 0.4
KERNEL_DECAY = 0.01
ADAM_EPS = 1e-08
AXES = ("dp", "fsdp")
TAPS = 9
LANES = 128
VMEM_BYTES = 56 * 1024 * 1024


def round_up(value, step):
    return (value + step - 1) // step * step


class Geometry:
    def __init__(self, shapes):
        self.shapes = shapes
        self.groups = []
        row, offset = 0, 0
        for count, side in shapes:
            down, right = (side + 1) * count, count
            rows = round_up(side * down, 8)
            halo = round_up(down + right, 8)
            offset = offset + halo
            self.groups.append((row, rows, offset, down, right))
            row += rows
            offset += rows + halo
        self.rows = row
        self.padded_rows = offset

    def flatten(self, arrays):
        pieces = []
        for array, (count, side), (_, rows, _, down, _) in zip(arrays, self.shapes, self.groups):
            moved = jnp.transpose(array, (1, 2, 0, 3))
            moved = jnp.pad(moved, ((0, 0), (0, 1), (0, 0), (0, 0)))
            moved = moved.reshape(side * down, array.shape[3])
            pieces.append(jnp.pad(moved, ((0, rows - side * down), (0, 0))))
        return jnp.concatenate(pieces, axis=0)

    def unflatten(self, flat):
        results = []
        for (count, side), (row, _, _, down, _) in zip(self.shapes, self.groups):
            piece = flat[row : row + side * down].reshape(side, side + 1, count, flat.shape[1])
            results.append(jnp.transpose(piece[:, :side], (2, 0, 1, 3)))
        return results

    def place(self, buffer, value):
        buffer[...] = jnp.zeros_like(buffer)
        for row, rows, offset, _, _ in self.groups:
            buffer[offset : offset + rows, :] = value[row : row + rows]

    def shifted(self, buffer, tap, sign):
        pieces = []
        for _, rows, offset, down, right in self.groups:
            start = offset + sign * ((tap // 3 - 1) * down + (tap % 3 - 1) * right)
            pieces.append(buffer[start : start + rows, :])
        return jnp.concatenate(pieces, axis=0).astype(jnp.bfloat16)


def wide(mask_ref, channels):
    return jnp.concatenate([mask_ref[...]] * (channels // LANES), axis=1)


def fetch(weight_hbm, weight_vmem, sems):
    copies = [
        pltpu.make_async_copy(weight_hbm.at[tap], weight_vmem.at[tap], sems.at[tap])
        for tap in range(TAPS)
    ]
    for copy in copies:
        copy.start()
    return copies


def multiply(left, right, left_dim, right_dim):
    return lax.dot_general(
        left, right, (((left_dim,), (right_dim,)), ((), ())), preferred_element_type=jnp.float32
    )


def column_sum(value):
    return jnp.sum(value, axis=0, keepdims=True)


def spread_rows(rows, ref):
    ref[...] = jnp.broadcast_to(jnp.concatenate(rows, axis=0)[None], ref.shape)


def local_statistics(hidden, valid, ref):
    count = column_sum(valid)
    total = column_sum(hidden * valid)
    centre = total / jnp.maximum(count, 1.0)
    squares = column_sum(jnp.square(hidden - centre) * valid)
    spread_rows([total, squares, count, centre], ref)


def global_statistics(gathered):
    totals, squares, counts, centres = (gathered[:, row, :] for row in range(4))
    total = column_sum(counts)
    centre = column_sum(totals) / total
    between = column_sum(counts * jnp.square(centres - centre))
    spread = (column_sum(squares) + between) / total
    return centre, lax.rsqrt(spread + NORM_EPS), total


def sigmoid(value):
    return 1.0 / (1.0 + jnp.exp(-value))


def swish_slope(value):
    logistic = sigmoid(value)
    return logistic * (1.0 + value * (1.0 - logistic))


def forward_one(geo, x_ref, mask_ref, weight_hbm, hidden_ref, stats_ref, buffer, weight, sems):
    copies = fetch(weight_hbm, weight, sems)
    valid = wide(mask_ref, x_ref.shape[1])
    geo.place(buffer, x_ref[...].astype(jnp.float32) * valid)
    for tap in range(TAPS):
        part = geo.shifted(buffer, tap, 1)
        copies[tap].wait()
        product = multiply(part, weight[tap], 1, 1)
        hidden_ref[...] = product if tap == 0 else hidden_ref[...] + product
    local_statistics(hidden_ref[...], valid, stats_ref)


def forward_two(
    geo,
    hidden_ref,
    gathered_ref,
    param_ref,
    mask_ref,
    weight_hbm,
    active_ref,
    second_ref,
    norm_ref,
    stats_ref,
    buffer,
    weight,
    sems,
):
    copies = fetch(weight_hbm, weight, sems)
    valid = wide(mask_ref, hidden_ref.shape[1])
    centre, inv, total = global_statistics(gathered_ref)
    norm_ref[...] = jnp.concatenate([centre, inv, total, total], axis=0)
    value = (hidden_ref[...] - centre) * inv * param_ref[0:1, :] + param_ref[1:2, :]
    active = value * sigmoid(value) * valid
    active_ref[...] = active.astype(jnp.bfloat16)
    geo.place(buffer, active)
    for tap in range(TAPS):
        part = geo.shifted(buffer, tap, 1)
        copies[tap].wait()
        product = multiply(part, weight[tap], 1, 1)
        second_ref[...] = product if tap == 0 else second_ref[...] + product
    local_statistics(second_ref[...], valid, stats_ref)


def turn(
    second_ref,
    gathered_ref,
    param_ref,
    mask_ref,
    x_ref,
    back_ref,
    result_ref,
    grad_ref,
    norm_ref,
    stats_ref,
):
    valid = wide(mask_ref, second_ref.shape[1])
    centre, inv, total = global_statistics(gathered_ref)
    norm_ref[...] = jnp.concatenate([centre, inv, total, total], axis=0)
    normed = (second_ref[...] - centre) * inv
    summed = normed * param_ref[2:3, :] + param_ref[3:4, :] + x_ref[...].astype(jnp.float32)
    logistic = sigmoid(summed)
    result_ref[...] = (summed * logistic * valid).astype(jnp.bfloat16)
    slope = logistic * (1.0 + summed * (1.0 - logistic))
    grad = back_ref[...].astype(jnp.float32) * valid * slope
    grad_ref[...] = grad
    spread_rows([column_sum(grad), column_sum(grad * normed)], stats_ref)


def norm_back(grad_ref, hidden_ref, norm_ref, gathered_ref, gain, valid, sums_ref):
    shift_grad = column_sum(gathered_ref[:, 0, :])
    gain_grad = column_sum(gathered_ref[:, 1, :])
    sums_ref[...] = jnp.concatenate([gain_grad, shift_grad], axis=0)
    centre, inv, total = norm_ref[0:1, :], norm_ref[1:2, :], norm_ref[2:3, :]
    normed = (hidden_ref[...] - centre) * inv
    grad = grad_ref[...] - shift_grad / total - normed * (gain_grad / total)
    return (valid * (gain * inv) * grad).astype(jnp.bfloat16)


def kernel_grad(geo, buffer, grad_in, out_ref):
    turned = jnp.transpose(grad_in.astype(jnp.float32)).astype(jnp.bfloat16)
    for tap in range(TAPS):
        product = multiply(turned, geo.shifted(buffer, tap, 1), 1, 0).astype(out_ref.dtype)
        if len(out_ref.shape) == 4:
            out_ref[:, tap, :, :] = product.reshape(
                out_ref.shape[0], out_ref.shape[2], out_ref.shape[3]
            )
        else:
            out_ref[tap] = product


def backward_two(
    geo,
    grad_ref,
    second_ref,
    norm_ref,
    gathered_ref,
    param_ref,
    mask_ref,
    active_ref,
    inner_ref,
    kernel_grad_ref,
    sums_ref,
    buffer,
):
    valid = wide(mask_ref, grad_ref.shape[1])
    inner = norm_back(
        grad_ref, second_ref, norm_ref, gathered_ref, param_ref[2:3, :], valid, sums_ref
    )
    inner_ref[...] = inner
    geo.place(buffer, active_ref[...].astype(jnp.float32))
    kernel_grad(geo, buffer, inner, kernel_grad_ref)


def backward_middle(
    geo,
    inner_ref,
    hidden_ref,
    norm_ref,
    param_ref,
    mask_ref,
    weight_hbm,
    grad_ref,
    stats_ref,
    buffer,
    weight,
    sems,
):
    copies = fetch(weight_hbm, weight, sems)
    valid = wide(mask_ref, hidden_ref.shape[1])
    geo.place(buffer, inner_ref[...].astype(jnp.float32))
    for tap in range(TAPS):
        part = geo.shifted(buffer, tap, -1)
        copies[tap].wait()
        product = multiply(part, weight[tap], 1, 0)
        grad_ref[...] = product if tap == 0 else grad_ref[...] + product
    normed = (hidden_ref[...] - norm_ref[0:1, :]) * norm_ref[1:2, :]
    value = normed * param_ref[0:1, :] + param_ref[1:2, :]
    grad = grad_ref[...] * valid * swish_slope(value)
    grad_ref[...] = grad
    spread_rows([column_sum(grad), column_sum(grad * normed)], stats_ref)


def backward_one(
    geo,
    grad_ref,
    hidden_ref,
    norm_ref,
    gathered_ref,
    param_ref,
    mask_ref,
    x_ref,
    inner_ref,
    kernel_grad_ref,
    sums_ref,
    buffer,
):
    valid = wide(mask_ref, grad_ref.shape[1])
    inner = norm_back(
        grad_ref, hidden_ref, norm_ref, gathered_ref, param_ref[0:1, :], valid, sums_ref
    )
    inner_ref[...] = inner
    geo.place(buffer, x_ref[...].astype(jnp.float32) * valid)
    kernel_grad(geo, buffer, inner, kernel_grad_ref)


def backward_input(
    geo, inner_ref, residual_ref, mask_ref, weight_hbm, grad_ref, buffer, weight, sems
):
    copies = fetch(weight_hbm, weight, sems)
    geo.place(buffer, inner_ref[...].astype(jnp.float32))
    for tap in range(TAPS):
        part = geo.shifted(buffer, tap, -1)
        copies[tap].wait()
        product = multiply(part, weight[tap], 1, 0)
        grad_ref[...] = product if tap == 0 else grad_ref[...] + product
    grad_ref[...] = residual_ref[...] + wide(mask_ref, grad_ref.shape[1]) * grad_ref[...]


def call(body, inputs, outputs, scratch=(), weights=()):
    whole = pl.BlockSpec(memory_space=pltpu.VMEM)
    return pl.pallas_call(
        body,
        out_shape=[jax.ShapeDtypeStruct(shape, dtype) for shape, dtype in outputs],
        in_specs=[whole] * len(inputs) + [pl.BlockSpec(memory_space=pl.ANY)] * len(weights),
        out_specs=[whole] * len(outputs),
        scratch_shapes=list(scratch),
        compiler_params=pltpu.CompilerParams(vmem_limit_bytes=VMEM_BYTES),
    )(*inputs, *weights)


def adamw(param, grad, first, second, rate, decay):
    first_new = BETA_ONE * first + (1.0 - BETA_ONE) * grad
    second_new = BETA_TWO * second + (1.0 - BETA_TWO) * grad * grad
    first_hat = first_new / (1.0 - BETA_ONE**STEP)
    second_hat = second_new / (1.0 - BETA_TWO**STEP)
    update = first_hat / (jnp.sqrt(second_hat) + ADAM_EPS)
    return (param - rate * (update + decay * param), first_new, second_new)


def exchange(spread):
    return lax.all_to_all(spread, AXES, 0, 0, tiled=True)


def local(
    devices,
    field_five,
    field_seven,
    field_nine,
    mask_five,
    mask_seven,
    mask_nine,
    back_five,
    back_seven,
    back_nine,
    kernels,
    norm_params,
    kernel_first,
    kernel_second,
    norm_first,
    norm_second,
):
    copies, shards = devices
    fields = (field_five, field_seven, field_nine)
    masks = (mask_five, mask_seven, mask_nine)
    backs = (back_five, back_seven, back_nine)
    channels = field_five.shape[3]
    width = kernels.shape[4]
    geo = Geometry([(field.shape[0], field.shape[1]) for field in fields])
    rows = geo.rows
    count = copies * shards
    f32, bf16 = jnp.float32, jnp.bfloat16

    def turned(kernel):
        return jnp.transpose(kernel, (0, 1, 2, 4, 3)).reshape(2, TAPS, width, channels)

    kernels_turned = turned(kernels)
    low = kernels_turned.astype(bf16)
    weight_one = lax.all_gather(low[0], "fsdp", axis=1, tiled=True)
    weight_two = lax.all_gather(low[1], "fsdp", axis=1, tiled=True)
    param_spread = jnp.broadcast_to(
        norm_params.astype(bf16).astype(f32)[None], (shards, 4, width)
    )
    params = lax.all_to_all(param_spread, "fsdp", 0, 0, tiled=True)
    params = jnp.transpose(params, (1, 0, 2)).reshape(4, channels)

    x = geo.flatten(fields)
    back = geo.flatten(backs)
    mask = geo.flatten([mask.astype(f32)[..., None] for mask in masks])
    mask = jnp.broadcast_to(mask, (rows, LANES))

    buffer = pltpu.VMEM((geo.padded_rows, channels), f32)
    weighted = (
        buffer,
        pltpu.VMEM((TAPS, channels, channels), bf16),
        pltpu.SemaphoreType.DMA((TAPS,)),
    )
    flat32 = ((rows, channels), f32)
    flat16 = ((rows, channels), bf16)
    four = ((count, 4, channels), f32)
    two = ((count, 2, channels), f32)
    norm = ((4, channels), f32)
    sums = ((2, channels), f32)
    if width % 16 == 0:
        grad_shape = ((shards, TAPS, width, channels), bf16)
    else:
        grad_shape = ((TAPS, channels, channels), bf16)

    def bind(body):
        return functools.partial(body, geo)

    hidden, stats = call(bind(forward_one), (x, mask), (flat32, four), weighted, (weight_one,))
    gathered = exchange(stats)
    active, second, norm_one, stats = call(
        bind(forward_two),
        (hidden, gathered, params, mask),
        (flat16, flat32, norm, four),
        weighted,
        (weight_two,),
    )
    gathered = exchange(stats)
    result, grad_sum, norm_two, stats = call(
        turn, (second, gathered, params, mask, x, back), (flat16, flat32, norm, two)
    )
    gathered = exchange(stats)
    inner_two, kernel_grad_two, sums_two = call(
        bind(backward_two),
        (grad_sum, second, norm_two, gathered, params, mask, active),
        (flat16, grad_shape, sums),
        (buffer,),
    )
    grad_hidden, stats = call(
        bind(backward_middle),
        (inner_two, hidden, norm_one, params, mask),
        (flat32, two),
        weighted,
        (weight_two,),
    )
    gathered = exchange(stats)
    inner_one, kernel_grad_one, sums_one = call(
        bind(backward_one),
        (grad_hidden, hidden, norm_one, gathered, params, mask, x),
        (flat16, grad_shape, sums),
        (buffer,),
    )
    (grad_input,) = call(
        bind(backward_input), (inner_one, grad_sum, mask), (flat32,), weighted, (weight_one,)
    )

    def reduced(value):
        if len(value.shape) == 3:
            value = jnp.transpose(
                value.reshape(TAPS, shards, width, channels), (1, 0, 2, 3)
            )
        owned = lax.psum_scatter(value, "fsdp", scatter_dimension=0, tiled=False)
        return lax.psum(owned, "dp").astype(f32)

    owned = jnp.stack([reduced(kernel_grad_one), reduced(kernel_grad_two)])
    results = adamw(
        kernels_turned,
        owned,
        turned(kernel_first),
        turned(kernel_second),
        KERNEL_RATE,
        KERNEL_DECAY,
    )
    kernel_results = [
        jnp.transpose(value.reshape(2, 3, 3, width, channels), (0, 1, 2, 4, 3))
        for value in results
    ]
    norm_full = jnp.concatenate([sums_one, sums_two], axis=0)
    norm_grads = lax.dynamic_slice_in_dim(norm_full, lax.axis_index("fsdp") * width, width, 1)
    norm_results = adamw(norm_params, norm_grads, norm_first, norm_second, NORM_RATE, 0.0)
    return (
        *geo.unflatten(result),
        *geo.unflatten(grad_input),
        *kernel_results,
        *norm_results,
    )


def solution(mesh):
    images = P(AXES, None, None, None)
    maps = P(AXES, None, None)
    weights = P(None, None, None, None, "fsdp")
    norms = P(None, "fsdp")
    in_specs = (
        (images,) * 3 + (maps,) * 3 + (images,) * 3 + (weights, norms, weights, weights, norms, norms)
    )
    out_specs = (images,) * 6 + (weights,) * 3 + (norms,) * 3
    body = functools.partial(local, (mesh.shape["dp"], mesh.shape["fsdp"]))
    return jax.shard_map(body, mesh=mesh, in_specs=in_specs, out_specs=out_specs, check_vma=False)
```

```python
import functools

import jax
import jax.numpy as jnp
from jax import lax
from jax.experimental import pallas as pl
from jax.experimental.pallas import tpu as pltpu
from jax.sharding import Mesh, PartitionSpec as P

STEP = 5
NORM_EPS = 1e-05
BETA_ONE = 0.5
BETA_TWO = 0.5
KERNEL_RATE = 0.03
NORM_RATE = 0.4
KERNEL_DECAY = 0.01
ADAM_EPS = 1e-08
TAPS = 9
LANES = 128
CELL = 2
VMEM_BYTES = 56 * 1024 * 1024
F32, BF16 = jnp.float32, jnp.bfloat16


def round_up(value, step):
    return (value + step - 1) // step * step


class Canvas:
    def __init__(self, shapes):
        self.shapes = shapes
        cells = [
            (side, group, first)
            for group, (count, side) in enumerate(shapes)
            for first in range(0, count, CELL)
        ]
        limit = max(
            sum(side + 1 for side, group, _ in cells if group == wanted)
            for wanted in range(len(shapes))
        )
        self.bands = []
        for side, group, first in sorted(cells, reverse=True):
            used = sum(cell[0] + 1 for cell in self.bands[-1]) if self.bands else limit
            if used + side + 1 > limit:
                self.bands.append([])
            self.bands[-1].append((side, group, first))
        self.width = limit
        self.right = CELL
        self.down = limit * CELL
        self.heights = [band[0][0] for band in self.bands]
        used_rows = (sum(self.heights) + len(self.bands) - 1) * self.down
        self.rows = round_up(used_rows, 16)
        self.halo = round_up(self.down + self.right, 8)
        self.lanes = round_up(self.rows + self.down + self.right, LANES)
        self.padded_rows = self.rows + 2 * self.halo

    def flatten(self, arrays):
        bands = []
        for band, height in zip(self.bands, self.heights):
            pieces = []
            for side, group, first in band:
                piece = jnp.transpose(arrays[group][first : first + CELL], (1, 2, 0, 3))
                piece = jnp.pad(piece, ((0, height + 1 - side), (0, 1), (0, 0), (0, 0)))
                pieces.append(piece)
            pieces = jnp.concatenate(pieces, axis=1)
            pieces = jnp.pad(pieces, ((0, 0), (0, self.width - pieces.shape[1]), (0, 0), (0, 0)))
            bands.append(pieces.reshape(-1, pieces.shape[3]))
        flat = jnp.concatenate(bands, axis=0)[: self.rows]
        return jnp.pad(flat, ((0, self.rows - flat.shape[0]), (0, 0)))

    def unflatten(self, flat):
        parts = [[] for _ in self.shapes]
        start = 0
        for band, height in zip(self.bands, self.heights):
            rows = flat[start : start + height * self.down]
            rows = rows.reshape(height, self.width, CELL, flat.shape[1])
            column = 0
            for side, group, first in band:
                piece = rows[:side, column : column + side]
                parts[group].append((first, jnp.transpose(piece, (2, 0, 1, 3))))
                column += side + 1
            start += (height + 1) * self.down
        return [
            jnp.concatenate([piece for _, piece in sorted(part, key=lambda item: item[0])], axis=0)
            for part in parts
        ]

    def shift(self, tap):
        return (tap // 3 - 1) * self.down + (tap % 3 - 1) * self.right

    def place(self, buffer, value):
        edge = jnp.zeros((self.halo, value.shape[1]), F32)
        buffer[0 : self.halo, :] = edge
        buffer[self.halo : self.halo + self.rows, :] = value
        buffer[self.halo + self.rows :, :] = edge

    def shifted(self, buffer, tap, sign):
        start = self.halo + sign * self.shift(tap)
        return buffer[start : start + self.rows, :].astype(BF16)


def wide(mask_ref, channels):
    return jnp.concatenate([mask_ref[...]] * (channels // LANES), axis=1)


def multiply(left, right, left_dim, right_dim):
    return lax.dot_general(
        left, right, (((left_dim,), (right_dim,)), ((), ())), preferred_element_type=F32
    )


def column_sum(value):
    return jnp.sum(value, axis=0, keepdims=True)


def spread_rows(rows, ref):
    ref[...] = jnp.broadcast_to(jnp.concatenate(rows, axis=0)[None], ref.shape)


def local_statistics(hidden, valid, ref):
    count = column_sum(valid)
    total = column_sum(hidden * valid)
    centre = total / jnp.maximum(count, 1.0)
    squares = column_sum(jnp.square(hidden - centre) * valid)
    spread_rows([total, squares, count, centre], ref)


def global_statistics(gathered):
    totals, squares, counts, centres = (gathered[:, row, :] for row in range(4))
    total = column_sum(counts)
    centre = column_sum(totals) / total
    between = column_sum(counts * jnp.square(centres - centre))
    spread = (column_sum(squares) + between) / total
    return centre, lax.rsqrt(spread + NORM_EPS), total


def sigmoid(value):
    return 1.0 / (1.0 + jnp.exp(-value))


def swish_slope(value):
    logistic = sigmoid(value)
    return logistic * (1.0 + value * (1.0 - logistic))


class Whole:
    def __init__(self, array):
        self.arrays = [array]

    @staticmethod
    def start(refs, weight, sem):
        copies = [pltpu.make_async_copy(refs[0], weight, sem)]
        copies[0].start()
        return copies


class Pieces:
    def __init__(self, pieces):
        self.arrays = [array for array, _ in pieces]
        self.slots = [slots for _, slots in pieces]

    def start(self, refs, weight, sem):
        y, z, x, c = (lax.axis_index(name) for name in ("y", "z", "x", "c"))
        copies = []
        for ref, slots in zip(refs, self.slots):
            _, _, width, half = ref.shape
            for slot, (dy, dz, dx, dc) in enumerate(slots):
                shard = ((z ^ dz) * 2 + (x ^ dx)) * 2 + (c ^ dc)
                row = pl.multiple_of(shard * width, width)
                lane = pl.multiple_of((y ^ dy) * half, half)
                copies.append(
                    pltpu.make_async_copy(
                        ref.at[slot], weight.at[:, pl.ds(row, width), pl.ds(lane, half)], sem
                    )
                )
        for copy in copies:
            copy.start()
        return copies


def convolve(canvas, value, source, refs, buffer, weight, sem, out_ref, sign, prepare=None):
    copies = source.start(refs, weight, sem)
    canvas.place(buffer, value() if callable(value) else value)
    for copy in copies:
        copy.wait()
    for tap in range(TAPS):
        part = canvas.shifted(buffer, tap, sign)
        product = multiply(part, weight[tap], 1, 1 if sign > 0 else 0)
        out_ref[...] = product if tap == 0 else out_ref[...] + product


def forward_one(canvas, source, x_ref, mask_ref, *refs):
    *weights, hidden_ref, stats_ref, buffer, weight, sem = refs
    convolve(
        canvas, lambda: x_ref[...].astype(F32), source, weights, buffer, weight, sem, hidden_ref, 1
    )
    local_statistics(hidden_ref[...], wide(mask_ref, x_ref.shape[1]), stats_ref)


def forward_two(canvas, source, hidden_ref, gathered_ref, param_ref, mask_ref, *refs):
    *weights, active_ref, second_ref, norm_ref, stats_ref, buffer, weight, sem = refs
    valid = wide(mask_ref, hidden_ref.shape[1])

    def active():
        centre, inv, total = global_statistics(gathered_ref)
        norm_ref[...] = jnp.concatenate([centre, inv, total, total], axis=0)
        value = (hidden_ref[...] - centre) * inv * param_ref[0:1, :] + param_ref[1:2, :]
        value = value * sigmoid(value) * valid
        active_ref[...] = value.astype(BF16)
        return value

    convolve(canvas, active, source, weights, buffer, weight, sem, second_ref, 1)
    local_statistics(second_ref[...], valid, stats_ref)


def turn(
    second_ref,
    gathered_ref,
    param_ref,
    mask_ref,
    x_ref,
    back_ref,
    result_ref,
    grad_ref,
    norm_ref,
    stats_ref,
):
    valid = wide(mask_ref, second_ref.shape[1])
    centre, inv, total = global_statistics(gathered_ref)
    norm_ref[...] = jnp.concatenate([centre, inv, total, total], axis=0)
    normed = (second_ref[...] - centre) * inv
    summed = normed * param_ref[2:3, :] + param_ref[3:4, :] + x_ref[...].astype(F32)
    logistic = sigmoid(summed)
    result_ref[...] = (summed * logistic * valid).astype(BF16)
    slope = logistic * (1.0 + summed * (1.0 - logistic))
    grad = back_ref[...].astype(F32) * valid * slope
    grad_ref[...] = grad
    spread_rows([column_sum(grad), column_sum(grad * normed)], stats_ref)


def norm_back(
    row,
    grad_ref,
    hidden_ref,
    norm_ref,
    gathered_ref,
    param_ref,
    mask_ref,
    inner_ref,
    sums_ref,
    turned_ref,
):
    valid = wide(mask_ref, grad_ref.shape[1])
    shift_grad = column_sum(gathered_ref[:, 0, :])
    gain_grad = column_sum(gathered_ref[:, 1, :])
    sums_ref[...] = jnp.concatenate([gain_grad, shift_grad], axis=0)
    centre, inv, total = norm_ref[0:1, :], norm_ref[1:2, :], norm_ref[2:3, :]
    normed = (hidden_ref[...] - centre) * inv
    grad = grad_ref[...] - shift_grad / total - normed * (gain_grad / total)
    inner = valid * (param_ref[row : row + 1, :] * inv) * grad
    inner_ref[...] = inner.astype(BF16)
    turned = jnp.transpose(inner).astype(BF16)
    rows, channels = inner.shape
    if len(turned_ref.shape) == 2:
        turned_ref[...] = turned
        return
    lanes = turned_ref.shape[-1]
    turned = jnp.concatenate([turned, jnp.zeros((channels, lanes - rows), BF16)], axis=1)
    half = channels // 32
    for shard in range(16):
        z, x, c = shard // 4, shard // 2 % 2, shard % 2
        for y in range(2):
            start = (shard * 2 + y) * half
            turned_ref[y, x, c, z * half : (z + 1) * half, :] = turned[start : start + half]


def backward_middle(canvas, source, inner_ref, hidden_ref, norm_ref, param_ref, mask_ref, *refs):
    *weights, grad_ref, stats_ref, buffer, weight, sem = refs
    valid = wide(mask_ref, hidden_ref.shape[1])
    convolve(
        canvas,
        lambda: inner_ref[...].astype(F32),
        source,
        weights,
        buffer,
        weight,
        sem,
        grad_ref,
        -1,
    )
    normed = (hidden_ref[...] - norm_ref[0:1, :]) * norm_ref[1:2, :]
    value = normed * param_ref[0:1, :] + param_ref[1:2, :]
    grad = grad_ref[...] * valid * swish_slope(value)
    grad_ref[...] = grad
    spread_rows([column_sum(grad), column_sum(grad * normed)], stats_ref)


def backward_input(canvas, source, inner_ref, residual_ref, mask_ref, *refs):
    *weights, grad_ref, buffer, weight, sem = refs
    convolve(
        canvas,
        lambda: inner_ref[...].astype(F32),
        source,
        weights,
        buffer,
        weight,
        sem,
        grad_ref,
        -1,
    )
    grad_ref[...] = residual_ref[...] + wide(mask_ref, grad_ref.shape[1]) * grad_ref[...]


def kernel_grad_whole(canvas, turned_ref, active_ref, out_ref, buffer):
    canvas.place(buffer, active_ref[...].astype(F32))
    for tap in range(TAPS):
        product = multiply(turned_ref[...], canvas.shifted(buffer, tap, 1), 1, 0)
        out_ref[tap] = product.astype(out_ref.dtype)


def kernel_grad_layer(canvas, turned_ref, *refs):
    *active_refs, send_ref, keep_ref, left, total = refs
    y, x, c = lax.axis_index("y"), lax.axis_index("x"), lax.axis_index("c")
    part = turned_ref.shape[3]
    for index, active_ref in enumerate(active_refs):
        block_y, block_x = y ^ (index // 2), x ^ (index % 2)
        for core in range(2):
            turned = turned_ref[block_y, block_x, c ^ core].astype(F32)
            for tap in range(TAPS):
                shift = canvas.shift(tap) % canvas.lanes
                moved = pltpu.roll(turned, shift, 1) if shift else turned
                row = (core * TAPS + tap) * part
                left[row : row + part, :] = moved[:, : canvas.rows].astype(BF16)
        product = multiply(left[...], active_ref[...], 1, 0)
        total[...] = product if index == 0 else total[...] + product
    half = part // 4
    for core, out_ref in enumerate((keep_ref, send_ref)):
        for tap in range(TAPS):
            for z in range(4):
                row = (core * TAPS + tap) * part + z * half
                out_ref[z, tap] = total[row : row + half, :].astype(out_ref.dtype)


def call(body, inputs, outputs, scratch=(), weights=()):
    whole = pl.BlockSpec(memory_space=pltpu.VMEM)
    return pl.pallas_call(
        body,
        out_shape=[jax.ShapeDtypeStruct(shape, dtype) for shape, dtype in outputs],
        in_specs=[whole] * len(inputs) + [pl.BlockSpec(memory_space=pl.ANY)] * len(weights),
        out_specs=[whole] * len(outputs),
        scratch_shapes=list(scratch),
        compiler_params=pltpu.CompilerParams(vmem_limit_bytes=VMEM_BYTES),
    )(*inputs, *weights)


def adamw(param, grad, first, second, rate, decay):
    first_new = BETA_ONE * first + (1.0 - BETA_ONE) * grad
    second_new = BETA_TWO * second + (1.0 - BETA_TWO) * grad * grad
    first_hat = first_new / (1.0 - BETA_ONE**STEP)
    second_hat = second_new / (1.0 - BETA_TWO**STEP)
    update = first_hat / (jnp.sqrt(second_hat) + ADAM_EPS)
    return (param - rate * (update + decay * param), first_new, second_new)


def flip(value, axis, bit, size):
    return lax.ppermute(value, axis, [(place, place ^ bit) for place in range(size)])


def diagonal(value):
    return lax.ppermute(value, ("y", "x"), [(place, place ^ 3) for place in range(4)])


class Grid:
    axes = ("y", "z", "x", "c")
    shard_axes = ("z", "x", "c")

    def weights(self, low):
        half = low.shape[2] // 2
        start = lax.axis_index("y") * half
        own = lax.dynamic_slice_in_dim(low, start, half, 2)[None]
        line = jnp.concatenate([own, flip(own, "z", 2, 4)], axis=0)
        line = jnp.concatenate([line, flip(line, "z", 1, 4)], axis=0)
        deep = (0, 2, 1, 3)
        over_x, over_y = flip(line, "x", 1, 2), flip(line, "y", 1, 2)
        last_x = flip(over_y[:2], "x", 1, 2)
        last_y = flip(over_x[2:], "y", 1, 2)
        pieces = [
            (line, [(0, dz, 0) for dz in deep]),
            (over_x, [(0, dz, 1) for dz in deep]),
            (over_y, [(1, dz, 0) for dz in deep]),
            (last_x, [(1, dz, 1) for dz in deep[:2]]),
            (last_y, [(1, dz, 1) for dz in deep[2:]]),
        ]
        found = []
        for array, slots in pieces:
            found.append((array, [slot + (0,) for slot in slots]))
            found.append((flip(array, "c", 1, 2), [slot + (1,) for slot in slots]))
        return Pieces(found)

    def layer(self, value):
        return [value, flip(value, "x", 1, 2), flip(value, "y", 1, 2), diagonal(value)]

    def turned_shape(self, canvas, channels):
        return ((2, 2, 2, channels // 8, canvas.lanes), BF16)

    def kernel_grad(self, canvas, turned, layer, channels):
        shape = turned.shape
        moved = lax.all_to_all(turned.reshape(4, *shape[2:]), ("y", "x"), 0, 0, tiled=True)
        half = channels // 32
        out = (4, TAPS, half, channels)
        send, keep = call(
            functools.partial(kernel_grad_layer, canvas),
            (moved.reshape(shape), *layer),
            ((out, BF16), (out, F32)),
            (
                pltpu.VMEM((2 * TAPS * shape[3], canvas.rows), BF16),
                pltpu.VMEM((2 * TAPS * shape[3], channels), F32),
            ),
        )
        chip = (keep + flip(send, "c", 1, 2).astype(F32)).astype(BF16)
        line = lax.all_to_all(chip, "z", 0, 0, tiled=True)
        own = jnp.sum(line.astype(F32), axis=0).astype(BF16)
        other = flip(own, "y", 1, 2)
        first = lax.axis_index("y") == 0
        halves = [jnp.where(first, own, other), jnp.where(first, other, own)]
        return jnp.concatenate(halves, axis=1).astype(F32)


class Plain:
    axes = ("dp", "fsdp")
    shard_axes = ("fsdp",)

    def weights(self, low):
        return Whole(lax.all_gather(low, "fsdp", axis=1, tiled=True))

    def layer(self, value):
        return [value]

    def turned_shape(self, canvas, channels):
        return ((channels, canvas.rows), BF16)

    def kernel_grad(self, canvas, turned, layer, channels):
        (full,) = call(
            functools.partial(kernel_grad_whole, canvas),
            (turned, layer[0]),
            (((TAPS, channels, channels), BF16),),
            (pltpu.VMEM((canvas.padded_rows, channels), F32),),
        )
        owned = lax.psum_scatter(full, "fsdp", scatter_dimension=1, tiled=True)
        return lax.psum(owned, "dp").astype(F32)


def local(
    ways,
    sizes,
    field_five,
    field_seven,
    field_nine,
    mask_five,
    mask_seven,
    mask_nine,
    back_five,
    back_seven,
    back_nine,
    kernels,
    norm_params,
    kernel_first,
    kernel_second,
    norm_first,
    norm_second,
):
    copies, shards = sizes
    fields = (field_five, field_seven, field_nine)
    masks = (mask_five, mask_seven, mask_nine)
    backs = (back_five, back_seven, back_nine)
    channels = field_five.shape[3]
    width = kernels.shape[4]
    canvas = Canvas([(field.shape[0], field.shape[1]) for field in fields])
    rows = canvas.rows
    count = copies * shards

    def turned(kernel):
        return jnp.transpose(kernel, (0, 1, 2, 4, 3)).reshape(2, TAPS, width, channels)

    def exchange(spread):
        return lax.all_to_all(spread, ways.axes, 0, 0, tiled=True)

    kernels_turned = turned(kernels)
    low = kernels_turned.astype(BF16)
    weight_one = ways.weights(low[0])
    weight_two = ways.weights(low[1])
    params = jnp.broadcast_to(norm_params.astype(BF16).astype(F32)[None], (shards, 4, width))
    params = lax.all_to_all(params, ways.shard_axes, 0, 0, tiled=True)
    params = jnp.transpose(params, (1, 0, 2)).reshape(4, channels)

    x = canvas.flatten([field * mask[..., None].astype(BF16) for field, mask in zip(fields, masks)])
    back = canvas.flatten(backs)
    mask = canvas.flatten([mask.astype(F32)[..., None] for mask in masks])
    mask = jnp.broadcast_to(mask, (rows, LANES))

    weighted = (
        pltpu.VMEM((canvas.padded_rows, channels), F32),
        pltpu.VMEM((TAPS, channels, channels), BF16),
        pltpu.SemaphoreType.DMA,
    )
    flat32 = ((rows, channels), F32)
    flat16 = ((rows, channels), BF16)
    four = ((count, 4, channels), F32)
    two = ((count, 2, channels), F32)
    norm = ((4, channels), F32)
    sums = ((2, channels), F32)
    turned_shape = ways.turned_shape(canvas, channels)

    def conv_call(body, source, inputs, outputs):
        return call(
            functools.partial(body, canvas, source), inputs, outputs, weighted, source.arrays
        )

    hidden, stats = conv_call(forward_one, weight_one, (x, mask), (flat32, four))
    gathered = exchange(stats)
    active, second, norm_one, stats = conv_call(
        forward_two, weight_two, (hidden, gathered, params, mask), (flat16, flat32, norm, four)
    )
    layer_active = ways.layer(active)
    layer_x = ways.layer(x)
    gathered = exchange(stats)
    result, grad_sum, norm_two, stats = call(
        turn, (second, gathered, params, mask, x, back), (flat16, flat32, norm, two)
    )
    gathered = exchange(stats)
    inner_two, sums_two, turned_two = call(
        functools.partial(norm_back, 2),
        (grad_sum, second, norm_two, gathered, params, mask),
        (flat16, sums, turned_shape),
    )
    grad_hidden, stats = conv_call(
        backward_middle, weight_two, (inner_two, hidden, norm_one, params, mask), (flat32, two)
    )
    gathered = exchange(stats)
    owned_two = ways.kernel_grad(canvas, turned_two, layer_active, channels)
    inner_one, sums_one, turned_one = call(
        functools.partial(norm_back, 0),
        (grad_hidden, hidden, norm_one, gathered, params, mask),
        (flat16, sums, turned_shape),
    )
    owned_one = ways.kernel_grad(canvas, turned_one, layer_x, channels)
    (grad_input,) = conv_call(backward_input, weight_one, (inner_one, grad_sum, mask), (flat32,))

    results = adamw(
        kernels_turned,
        jnp.stack([owned_one, owned_two]),
        turned(kernel_first),
        turned(kernel_second),
        KERNEL_RATE,
        KERNEL_DECAY,
    )
    kernel_results = [
        jnp.transpose(value.reshape(2, 3, 3, width, channels), (0, 1, 2, 4, 3))
        for value in results
    ]
    norm_full = jnp.concatenate([sums_one, sums_two], axis=0)
    place = lax.axis_index(ways.shard_axes) * width
    norm_grads = lax.dynamic_slice_in_dim(norm_full, place, width, 1)
    norm_results = adamw(norm_params, norm_grads, norm_first, norm_second, NORM_RATE, 0.0)
    return (
        *canvas.unflatten(result),
        *canvas.unflatten(grad_input),
        *kernel_results,
        *norm_results,
    )


def solution(mesh):
    sizes = (mesh.shape["dp"], mesh.shape["fsdp"])
    if sizes == (2, 16):
        ways = Grid()
        mesh = Mesh(mesh.devices.reshape(2, 4, 2, 2), ways.axes)
    else:
        ways = Plain()
    images = P(ways.axes, None, None, None)
    maps = P(ways.axes, None, None)
    weights = P(None, None, None, None, ways.shard_axes)
    norms = P(None, ways.shard_axes)
    in_specs = (
        (images,) * 3 + (maps,) * 3 + (images,) * 3 + (weights, norms, weights, weights, norms, norms)
    )
    out_specs = (images,) * 6 + (weights,) * 3 + (norms,) * 3
    body = functools.partial(local, ways, sizes)
    return jax.shard_map(body, mesh=mesh, in_specs=in_specs, out_specs=out_specs, check_vma=False)
```

```python
import functools

import jax
import jax.numpy as jnp
from jax import lax
from jax.experimental import pallas as pl
from jax.experimental.pallas import tpu as pltpu
from jax.sharding import Mesh, PartitionSpec as P

STEP = 5
NORM_EPS = 1e-05
BETA_ONE = 0.5
BETA_TWO = 0.5
KERNEL_RATE = 0.03
NORM_RATE = 0.4
KERNEL_DECAY = 0.01
ADAM_EPS = 1e-08
TAPS = 9
LANES = 128
CELL = 2
VMEM_BYTES = 54 * 1024 * 1024
F32, BF16 = jnp.float32, jnp.bfloat16


def round_up(value, step):
    return (value + step - 1) // step * step


class Canvas:
    def __init__(self, shapes):
        self.shapes = shapes
        cells = [
            (side, group, first)
            for group, (count, side) in enumerate(shapes)
            for first in range(0, count, CELL)
        ]
        limit = max(
            sum(side + 1 for side, group, _ in cells if group == wanted)
            for wanted in range(len(shapes))
        )
        self.bands = []
        for side, group, first in sorted(cells, reverse=True):
            used = sum(cell[0] + 1 for cell in self.bands[-1]) if self.bands else limit
            if used + side + 1 > limit:
                self.bands.append([])
            self.bands[-1].append((side, group, first))
        self.width = limit
        self.right = CELL
        self.down = limit * CELL
        self.heights = [band[0][0] for band in self.bands]
        used_rows = (sum(self.heights) + len(self.bands) - 1) * self.down
        self.rows = round_up(used_rows, 16)
        self.halo = round_up(self.down + self.right, 8)
        self.lanes = round_up(self.rows + self.down + self.right, LANES)
        self.padded_rows = self.rows + 2 * self.halo
        self.sent_rows = self.rows + 16

    def cells(self):
        start = 0
        for band, height in zip(self.bands, self.heights):
            column = 0
            for side, group, first in band:
                yield side, group, first, start * self.down + column * CELL
                column += side + 1
            start += height + 1

    def unflatten(self, flat):
        parts = [[] for _ in self.shapes]
        start = 0
        for band, height in zip(self.bands, self.heights):
            rows = flat[start : start + height * self.down]
            rows = rows.reshape(height, self.width, CELL, flat.shape[1])
            column = 0
            for side, group, first in band:
                piece = rows[:side, column : column + side]
                parts[group].append((first, jnp.transpose(piece, (2, 0, 1, 3))))
                column += side + 1
            start += (height + 1) * self.down
        return [
            jnp.concatenate([piece for _, piece in sorted(part, key=lambda item: item[0])], axis=0)
            for part in parts
        ]

    def shift(self, tap):
        return (tap // 3 - 1) * self.down + (tap % 3 - 1) * self.right

    def place(self, buffer, value):
        edge = jnp.zeros((self.halo, value.shape[1]), F32)
        buffer[0 : self.halo, :] = edge
        buffer[self.halo : self.halo + self.rows, :] = value
        buffer[self.halo + self.rows :, :] = edge

    def shifted(self, buffer, tap, sign):
        start = self.halo + sign * self.shift(tap)
        return buffer[start : start + self.rows, :].astype(BF16)


def wide(mask_ref, channels):
    return jnp.concatenate([mask_ref[...]] * (channels // LANES), axis=1)


def multiply(left, right, left_dim, right_dim):
    return lax.dot_general(
        left, right, (((left_dim,), (right_dim,)), ((), ())), preferred_element_type=F32
    )


def column_sum(value):
    return jnp.sum(value, axis=0, keepdims=True)


def spread_rows(rows, ref):
    ref[...] = jnp.broadcast_to(jnp.concatenate(rows, axis=0)[None], ref.shape)


def local_statistics(hidden, valid, *refs):
    total = column_sum(hidden * valid)
    centre = total / jnp.maximum(column_sum(valid), 1.0)
    squares = column_sum(jnp.square(hidden - centre) * valid)
    rows = jnp.concatenate([total, squares], axis=0)
    *info, ref = [ref[...] for ref in refs[:-1]] + [refs[-1]]
    rows = jnp.concatenate([rows, *info], axis=1)
    ref[...] = jnp.broadcast_to(rows[None], ref.shape)


def global_statistics(gathered, counts):
    channels = counts.shape[1]
    totals, squares = gathered[:, 0, :channels], gathered[:, 1, :channels]
    total = column_sum(counts)
    centre = column_sum(totals) / total
    between = column_sum(counts * jnp.square(totals / jnp.maximum(counts, 1.0) - centre))
    spread = (column_sum(squares) + between) / total
    return centre, lax.rsqrt(spread + NORM_EPS), total


def lay_out(canvas, field_refs, buffer):
    buffer[...] = jnp.zeros_like(buffer)
    for side, group, first, start in canvas.cells():
        for down in range(side):
            for right in range(side):
                row = start + down * canvas.down + right * CELL
                pair = field_refs[group][down, right, first : first + CELL, :]
                buffer[row : row + CELL, :] = pair.astype(F32)


def prepare(canvas, *refs):
    *field_refs, param_ref = refs[:4]
    mask_refs = refs[4:7]
    x_ref, mask_ref, info_ref, buffer = refs[7:]
    rows, channels = buffer.shape
    mask_ref[...] = jnp.zeros_like(mask_ref)
    for side, group, first, start in canvas.cells():
        for down in range(side):
            for right in range(side):
                for image in range(CELL):
                    row = start + down * canvas.down + right * CELL + image
                    value = mask_refs[group][first + image, down, right].astype(F32)
                    mask_ref[row : row + 1, :] = jnp.full((1, LANES), value, F32)
    lay_out(canvas, field_refs, buffer)
    x_ref[0:rows, :] = (buffer[...] * wide(mask_ref, channels)).astype(BF16)
    line = jnp.transpose(mask_ref[...])[0:1]
    rest = jnp.zeros((1, channels * 2 - rows), F32)
    lines = [line[:, :channels], jnp.concatenate([line[:, channels:], rest], axis=1)]
    lines.append(jnp.zeros((14, channels), F32))
    x_ref[rows:, :] = jnp.concatenate(lines, axis=0).astype(BF16)
    params = param_ref[...].astype(BF16).astype(F32)
    rows = [params[index : index + 1] for index in range(4)]
    if params.size < LANES:
        rows.append(jnp.zeros((1, LANES - params.size), F32))
    row = jnp.concatenate(rows, axis=1)
    info_ref[...] = jnp.concatenate([row, column_sum(mask_ref[...])], axis=0)


def sent_pixels(canvas, refs):
    whole = jnp.concatenate([ref[...] for ref in refs], axis=0).astype(F32)
    return whole[: canvas.rows]


def sent_mask(canvas, refs):
    channels = refs[0].shape[1]
    turned = jnp.transpose(refs[-1][refs[-1].shape[0] - 16 :, :].astype(F32))
    column = jnp.concatenate([turned[:, 0:1], turned[: canvas.rows - channels, 1:2]], axis=0)
    return jnp.broadcast_to(column, (canvas.rows, channels))


def prepare_back(canvas, *refs):
    *field_refs, back_ref, buffer = refs
    lay_out(canvas, field_refs, buffer)
    back_ref[...] = buffer[...].astype(BF16)


def sigmoid(value):
    return 1.0 / (1.0 + jnp.exp(-value))


def swish_slope(value):
    logistic = sigmoid(value)
    return logistic * (1.0 + value * (1.0 - logistic))


class Whole:
    def __init__(self, array, width):
        self.arrays = self.last = [array]
        self.width = width

    @staticmethod
    def copies(refs, weight, taps, sem):
        return [pltpu.make_async_copy(refs[0].at[taps], weight.at[taps], sem)]


class Pieces:
    width = 32

    def __init__(self, pieces):
        self.arrays = [array for array, _, _ in pieces]
        self.last = self.arrays[-4:]
        self.places = [(slots, first) for _, slots, first in pieces]

    def copies(self, refs, weight, taps, sem):
        y, z, x, c = (lax.axis_index(name) for name in ("y", "z", "x", "c"))
        copies = []
        for ref, (slots, first) in zip(refs, self.places):
            _, _, rows, lanes = ref.shape
            for slot, (dy, dz, dx, dc) in enumerate(slots):
                shard = ((z ^ dz) * 2 + (x ^ dx)) * 2 + (c ^ dc)
                row = pl.multiple_of(shard * self.width + first, 16)
                lane = 0 if dy is None else pl.multiple_of((y ^ dy) * lanes, lanes)
                target = weight.at[taps, pl.ds(row, rows), pl.ds(lane, lanes)]
                copies.append(pltpu.make_async_copy(ref.at[slot, taps], target, sem))
        return copies


def convolve(canvas, value, source, refs, buffer, weight, sems, out_ref, sign):
    parts = [
        source.copies(refs, weight, pl.ds(3 * part, 3), sems.at[part]) for part in range(3)
    ]
    for copies in parts:
        for copy in copies:
            copy.start()
    canvas.place(buffer, value())
    for tap in range(TAPS):
        if tap % 3 == 0:
            for copy in parts[tap // 3]:
                copy.wait()
        part = canvas.shifted(buffer, tap, sign)
        product = multiply(part, weight[tap], 1, 1 if sign > 0 else 0)
        out_ref[...] = product if tap == 0 else out_ref[...] + product


def activate(hidden, norm_ref, param_ref, valid):
    normed = (hidden - norm_ref[0:1, :]) * norm_ref[1:2, :]
    value = normed * param_ref[0:1, :] + param_ref[1:2, :]
    return value * sigmoid(value) * valid


def side_hidden(canvas, source, sent_ref, *refs):
    *weights, hidden_ref, buffer, weight, sems = refs
    pixels = functools.partial(sent_pixels, canvas, [sent_ref])
    convolve(canvas, pixels, source, weights, buffer, weight, sems, hidden_ref, 1)


def side_active(canvas, source, known, parts, *refs):
    hidden_refs, refs = refs[:known], refs[known:]
    hidden_sent, refs = refs[:known], refs[known:]
    sent_refs, refs = refs[:parts], refs[parts:]
    norm_ref, param_ref, *weights = refs[: 2 + len(source.arrays)]
    *active_refs, buffer, weight, sems, hidden = refs[2 + len(source.arrays) :]
    for hidden_ref, sent_ref, active_ref in zip(hidden_refs, hidden_sent, active_refs[1:]):
        valid = sent_mask(canvas, [sent_ref])
        active_ref[...] = activate(hidden_ref[...], norm_ref, param_ref, valid).astype(BF16)
    pixels = functools.partial(sent_pixels, canvas, sent_refs)
    convolve(canvas, pixels, source, weights, buffer, weight, sems, hidden, 1)
    valid = sent_mask(canvas, sent_refs)
    active_refs[0][...] = activate(hidden[...], norm_ref, param_ref, valid).astype(BF16)


def forward_one(canvas, source, x_ref, mask_ref, info_ref, *refs):
    *weights, hidden_ref, stats_ref, buffer, weight, sem = refs
    convolve(
        canvas,
        functools.partial(sent_pixels, canvas, [x_ref]),
        source,
        weights,
        buffer,
        weight,
        sem,
        hidden_ref,
        1,
    )
    local_statistics(hidden_ref[...], wide(mask_ref, x_ref.shape[1]), info_ref, stats_ref)


def forward_two(canvas, source, hidden_ref, gathered_ref, mask_ref, *refs):
    *weights, active_ref, second_ref, norm_ref, param_ref, count_ref, stats_ref = refs[:-3]
    buffer, weight, sem = refs[-3:]
    channels = hidden_ref.shape[1]
    valid = wide(mask_ref, channels)
    width = source.width
    rows = []
    for index in range(4):
        start = channels + index * width
        rows.append(
            jnp.concatenate(
                [gathered_ref[shard, 0:1, start : start + width] for shard in range(channels // width)],
                axis=1,
            )
        )
    param_ref[...] = jnp.concatenate(rows, axis=0)
    counts = gathered_ref[:, 1, channels : channels + LANES]
    count_ref[...] = jnp.concatenate([counts] * (channels // LANES), axis=1)

    def active():
        centre, inv, total = global_statistics(gathered_ref, count_ref[...])
        norm_ref[...] = jnp.concatenate([centre, inv, total, total], axis=0)
        value = activate(hidden_ref[...], norm_ref, param_ref, valid)
        active_ref[...] = value.astype(BF16)
        return value

    convolve(canvas, active, source, weights, buffer, weight, sem, second_ref, 1)
    local_statistics(second_ref[...], valid, stats_ref)


def turn(
    second_ref,
    gathered_ref,
    count_ref,
    param_ref,
    mask_ref,
    x_ref,
    back_ref,
    result_ref,
    grad_ref,
    norm_ref,
    stats_ref,
):
    valid = wide(mask_ref, second_ref.shape[1])
    centre, inv, total = global_statistics(gathered_ref, count_ref[...])
    norm_ref[...] = jnp.concatenate([centre, inv, total, total], axis=0)
    normed = (second_ref[...] - centre) * inv
    rows = second_ref.shape[0]
    summed = normed * param_ref[2:3, :] + param_ref[3:4, :] + x_ref[0:rows, :].astype(F32)
    logistic = sigmoid(summed)
    result_ref[...] = (summed * logistic * valid).astype(BF16)
    slope = logistic * (1.0 + summed * (1.0 - logistic))
    grad = back_ref[...].astype(F32) * valid * slope
    grad_ref[...] = grad
    spread_rows([column_sum(grad), column_sum(grad * normed)], stats_ref)


def norm_back(
    row,
    grad_ref,
    hidden_ref,
    norm_ref,
    gathered_ref,
    param_ref,
    mask_ref,
    inner_ref,
    sums_ref,
    turned_ref,
):
    valid = wide(mask_ref, grad_ref.shape[1])
    shift_grad = column_sum(gathered_ref[:, 0, :])
    gain_grad = column_sum(gathered_ref[:, 1, :])
    sums_ref[...] = jnp.concatenate([gain_grad, shift_grad], axis=0)
    centre, inv, total = norm_ref[0:1, :], norm_ref[1:2, :], norm_ref[2:3, :]
    normed = (hidden_ref[...] - centre) * inv
    grad = grad_ref[...] - shift_grad / total - normed * (gain_grad / total)
    inner = valid * (param_ref[row : row + 1, :] * inv) * grad
    inner_ref[...] = inner.astype(BF16)
    turned = jnp.transpose(inner).astype(BF16)
    rows, channels = inner.shape
    if len(turned_ref.shape) == 2:
        turned_ref[...] = turned
        return
    lanes = turned_ref.shape[-1]
    turned = jnp.concatenate([turned, jnp.zeros((channels, lanes - rows), BF16)], axis=1)
    half = channels // 32
    for shard in range(16):
        z, x, c = shard // 4, shard // 2 % 2, shard % 2
        for y in range(2):
            start = (shard * 2 + y) * half
            turned_ref[y, x, c, z * half : (z + 1) * half, :] = turned[start : start + half]


def backward_middle(canvas, source, inner_ref, hidden_ref, norm_ref, param_ref, mask_ref, *refs):
    *weights, grad_ref, stats_ref, buffer, weight, sem = refs
    valid = wide(mask_ref, hidden_ref.shape[1])
    convolve(
        canvas,
        lambda: inner_ref[...].astype(F32),
        source,
        weights,
        buffer,
        weight,
        sem,
        grad_ref,
        -1,
    )
    normed = (hidden_ref[...] - norm_ref[0:1, :]) * norm_ref[1:2, :]
    value = normed * param_ref[0:1, :] + param_ref[1:2, :]
    grad = grad_ref[...] * valid * swish_slope(value)
    grad_ref[...] = grad
    spread_rows([column_sum(grad), column_sum(grad * normed)], stats_ref)


def backward_input(canvas, source, inner_ref, residual_ref, mask_ref, *refs):
    *weights, grad_ref, buffer, weight, sem = refs
    convolve(
        canvas,
        lambda: inner_ref[...].astype(F32),
        source,
        weights,
        buffer,
        weight,
        sem,
        grad_ref,
        -1,
    )
    grad_ref[...] = residual_ref[...] + wide(mask_ref, grad_ref.shape[1]) * grad_ref[...]


def kernel_grad_whole(canvas, turned_ref, active_ref, out_ref, buffer):
    canvas.place(buffer, active_ref[0 : canvas.rows, :].astype(F32))
    for tap in range(TAPS):
        product = multiply(turned_ref[...], canvas.shifted(buffer, tap, 1), 1, 0)
        out_ref[tap] = product.astype(out_ref.dtype)


def kernel_grad_layer(canvas, turned_ref, *refs):
    *active_refs, send_ref, keep_ref, left, total = refs
    y, x, c = lax.axis_index("y"), lax.axis_index("x"), lax.axis_index("c")
    part = turned_ref.shape[3]
    for index in range(4):
        block_y, block_x = y ^ (index // 2), x ^ (index % 2)
        for core in range(2):
            turned = turned_ref[block_y, block_x, c ^ core].astype(F32)
            for tap in range(TAPS):
                shift = canvas.shift(tap) % canvas.lanes
                moved = pltpu.roll(turned, shift, 1) if shift else turned
                row = (core * TAPS + tap) * part
                left[row : row + part, :] = moved[:, : canvas.rows].astype(BF16)
        start = 0
        for part_ref in active_refs[index : index + 1] if index < 3 else active_refs[3:]:
            rows = min(part_ref.shape[0], canvas.rows - start)
            product = multiply(left[:, start : start + rows], part_ref[0:rows, :], 1, 0)
            total[...] = product if index + start == 0 else total[...] + product
            start += rows
    half = part // 4
    for core, out_ref in enumerate((keep_ref, send_ref)):
        for tap in range(TAPS):
            for z in range(4):
                row = (core * TAPS + tap) * part + (lax.axis_index("z") ^ z) * half
                out_ref[z, tap] = total[pl.ds(row, half), :].astype(out_ref.dtype)


def call(body, inputs, outputs, scratch=(), weights=(), after=(), scalars=()):
    whole = pl.BlockSpec(memory_space=pltpu.VMEM)
    anywhere = pl.BlockSpec(memory_space=pltpu.HBM)
    read = len(inputs) + len(scalars) + len(weights)

    def kernel(*refs):
        body(*refs[:read], *refs[read + len(after) :])

    return pl.pallas_call(
        kernel,
        out_shape=[jax.ShapeDtypeStruct(shape, dtype) for shape, dtype in outputs],
        in_specs=[whole] * len(inputs)
        + [pl.BlockSpec(memory_space=pltpu.SMEM)] * len(scalars)
        + [anywhere] * (len(weights) + len(after)),
        out_specs=[whole] * len(outputs),
        scratch_shapes=list(scratch),
        compiler_params=pltpu.CompilerParams(vmem_limit_bytes=VMEM_BYTES),
    )(*inputs, *scalars, *weights, *after)


def adamw(param, grad, first, second, rate, decay):
    first_new = BETA_ONE * first + (1.0 - BETA_ONE) * grad
    second_new = BETA_TWO * second + (1.0 - BETA_TWO) * grad * grad
    first_hat = first_new / (1.0 - BETA_ONE**STEP)
    second_hat = second_new / (1.0 - BETA_TWO**STEP)
    update = first_hat / (jnp.sqrt(second_hat) + ADAM_EPS)
    return (param - rate * (update + decay * param), first_new, second_new)


def flip(value, axis, bit, size):
    return lax.ppermute(value, axis, [(place, place ^ bit) for place in range(size)])


def behind(value, others):
    return lax.optimization_barrier((value, *others))[0] if others else value


class Gather:
    def __init__(self, shard, half):
        self.shard, self.half = shard[None], half[None]

    def along_two(self, *others):
        self.second = flip(behind(self.half, others), "z", 2, 4)

    def beside(self, *others):
        self.nearest = flip(behind(self.shard, others), "x", 1, 2)

    def along_one(self, *others):
        both = jnp.concatenate([self.half, self.second], axis=0)
        self.line = flip(behind(both, others), "z", 1, 4)

    def across(self, *others):
        self.rest = jnp.concatenate([self.second, self.line], axis=0)
        rest = behind(self.rest, others)
        self.over = flip(rest, "x", 1, 2), flip(rest, "y", 1, 2)

    def corner(self, *others):
        rows = self.shard.shape[2] // 2
        over_x, over_y = self.over
        self.corners = (
            flip(behind(over_y[:, :, :rows], others), "x", 1, 2),
            flip(behind(over_x[:, :, rows:], others), "y", 1, 2),
        )

    def cores(self, *others):
        rows = self.shard.shape[2] // 2
        deep = (2, 1, 3)
        pieces = [
            (self.shard, [(None, 0, 0)], 0),
            (self.nearest, [(None, 0, 1)], 0),
            (self.rest, [(0, dz, 0) for dz in deep], 0),
            (self.over[0], [(0, dz, 1) for dz in deep], 0),
            (self.over[1], [(1, dz, 0) for dz in deep], 0),
            (self.corners[0], [(1, dz, 1) for dz in deep], 0),
            (self.corners[1], [(1, dz, 1) for dz in deep], rows),
        ]
        self.found = []
        for index, (array, slots, first) in enumerate(pieces):
            late = others if index > 2 else ()
            other = flip(behind(array, late), "c", 1, 2)
            self.found.append((array, [slot + (0,) for slot in slots], first))
            self.found.append((other, [slot + (1,) for slot in slots], first))


class Grid:
    axes = ("y", "z", "x", "c")
    shard_axes = ("z", "x", "c")

    def weights(self, low, x, back):
        half = low.shape[3] // 2
        first, second = lax.dynamic_slice_in_dim(low, lax.axis_index("y") * half, half, 3)
        one, two = Gather(low[0], first), Gather(low[1], second)
        one.along_two()
        one.beside()
        self.sides = flip(x, "x", 1, 2), flip(x, "y", 1, 2)
        one.along_one(x, one.nearest)
        two.along_two(one.line)
        one.across()
        two.along_one(*one.over)
        one.corner(back)
        one.cores()
        two.beside(*one.corners)
        two.across(*one.corners)
        self.second = two
        return Pieces(one.found)

    def second_weights(self, hidden, gathered):
        over_x, over_y = self.sides
        rows = round_up(over_x.shape[0] // 2, 16)
        self.second.corner(*hidden)
        self.second.cores(*hidden)
        self.corners = (
            flip(behind(over_y[:rows], (gathered,)), "x", 1, 2),
            flip(behind(over_x[rows:], (gathered,)), "y", 1, 2),
        )
        return Pieces(self.second.found)

    def turned_shape(self, canvas, channels):
        return ((2, 2, 2, channels // 8, canvas.lanes), BF16)

    def send(self, turned):
        shape = turned.shape
        moved = lax.all_to_all(turned.reshape(4, *shape[2:]), ("y", "x"), 0, 0, tiled=True)
        return moved.reshape(shape)

    def chip_sum(self, canvas, moved, layer, channels, after):
        out = (4, TAPS, channels // 32, channels)
        part = moved.shape[3]
        send, keep = call(
            functools.partial(kernel_grad_layer, canvas),
            (moved, *layer),
            ((out, BF16), (out, F32)),
            (
                pltpu.VMEM((2 * TAPS * part, canvas.rows), BF16),
                pltpu.VMEM((2 * TAPS * part, channels), F32),
            ),
            after=after,
        )
        return send, keep

    def core_sum(self, chip, *others):
        send, keep = chip
        other = flip(behind(send, others), "c", 1, 2)
        near, far = (keep[part::2] + other[part::2].astype(F32) for part in range(2))
        return near, far.astype(BF16)

    def pair_sum(self, parts, *others):
        near, far = parts
        return near + flip(behind(far, others), "z", 1, 4).astype(F32)

    def line_sum(self, near):
        return near[0] + flip(near[1].astype(BF16), "z", 2, 4).astype(F32)

    def owned(self, line):
        own = line.astype(BF16)
        other = flip(own, "y", 1, 2)
        first = lax.axis_index("y") == 0
        halves = [jnp.where(first, own, other), jnp.where(first, other, own)]
        return jnp.concatenate(halves, axis=1).astype(F32)


class Plain:
    axes = ("dp", "fsdp")
    shard_axes = ("fsdp",)

    sides = corners = ()

    def weights(self, low, x, back):
        full = lax.all_gather(low, "fsdp", axis=2, tiled=True)
        first, self.second = [Whole(array, low.shape[2]) for array in full]
        return first

    def second_weights(self, hidden, gathered):
        return self.second

    def turned_shape(self, canvas, channels):
        return ((channels, canvas.rows), BF16)

    def send(self, turned):
        return turned

    def chip_sum(self, canvas, turned, layer, channels, after):
        (full,) = call(
            functools.partial(kernel_grad_whole, canvas),
            (turned, layer[0]),
            (((TAPS, channels, channels), BF16),),
            (pltpu.VMEM((canvas.padded_rows, channels), F32),),
            after=after,
        )
        return (full,)

    def core_sum(self, chip, *others):
        return chip

    def pair_sum(self, parts, *others):
        return parts[0]

    def line_sum(self, full):
        return lax.psum_scatter(full, "fsdp", scatter_dimension=1, tiled=True)

    def owned(self, line):
        return lax.psum(line, "dp").astype(F32)


def local(
    ways,
    sizes,
    field_five,
    field_seven,
    field_nine,
    mask_five,
    mask_seven,
    mask_nine,
    back_five,
    back_seven,
    back_nine,
    kernels,
    norm_params,
    kernel_first,
    kernel_second,
    norm_first,
    norm_second,
):
    copies, shards = sizes
    fields = (field_five, field_seven, field_nine)
    masks = (mask_five, mask_seven, mask_nine)
    backs = (back_five, back_seven, back_nine)
    channels = field_five.shape[3]
    width = kernels.shape[4]
    canvas = Canvas([(field.shape[0], field.shape[1]) for field in fields])
    rows = canvas.rows
    count = copies * shards

    def turned(kernel):
        return jnp.transpose(kernel, (0, 1, 2, 4, 3)).reshape(2, TAPS, width, channels)

    def exchange(spread):
        return lax.all_to_all(spread, ways.axes, 0, 0, tiled=True)

    kernels_turned = turned(kernels)
    low = kernels_turned.astype(BF16)

    buffer = pltpu.VMEM((rows, channels), F32)
    weighted = (
        pltpu.VMEM((canvas.padded_rows, channels), F32),
        pltpu.VMEM((TAPS, channels, channels), BF16),
        pltpu.SemaphoreType.DMA((3,)),
    )
    flat32 = ((rows, channels), F32)
    flat16 = ((rows, channels), BF16)
    two = ((count, 2, channels), F32)
    norm = ((4, channels), F32)
    sums = ((2, channels), F32)
    turned_shape = ways.turned_shape(canvas, channels)

    def conv_call(body, source, inputs, outputs, after=()):
        return call(
            functools.partial(body, canvas, source),
            inputs,
            outputs,
            weighted,
            source.arrays,
            after,
        )

    x, mask, info = call(
        functools.partial(prepare, canvas),
        (*[jnp.transpose(field, (1, 2, 0, 3)) for field in fields], norm_params),
        (((canvas.sent_rows, channels), BF16), ((rows, LANES), F32), ((2, LANES), F32)),
        (buffer,),
        scalars=masks,
    )
    (back,) = call(
        functools.partial(prepare_back, canvas),
        [jnp.transpose(field, (1, 2, 0, 3)) for field in backs],
        (flat16,),
        (buffer,),
    )
    weight_one = ways.weights(low, x, back)
    sides = ways.sides
    hidden, stats = conv_call(
        forward_one,
        weight_one,
        (x, mask, info),
        (flat32, ((count, 2, channels + LANES), F32)),
        after=sides,
    )
    gathered = exchange(stats)
    side = ()
    if sides:
        side = conv_call(side_hidden, weight_one, sides[1:], (flat32,), after=(stats,))
    weight_two = ways.second_weights(side, gathered)
    active, second, norm_one, params, counts, stats = conv_call(
        forward_two,
        weight_two,
        (hidden, gathered, mask),
        (flat16, flat32, norm, norm, ((count, channels), F32), two),
        after=side,
    )
    gathered = exchange(stats)
    actives = (active,)

    def side_call(hidden, hidden_sent, sent, after):
        return call(
            functools.partial(side_active, canvas, weight_one, len(hidden), len(sent)),
            (*hidden, *hidden_sent, *sent, norm_one, params),
            (flat16,) * (1 + len(hidden)),
            (*weighted, pltpu.VMEM((rows, channels), F32)),
            weight_one.arrays,
            after,
        )

    if sides:
        actives += tuple(side_call(side, sides[1:], sides[:1], (stats,)))
    result, grad_sum, norm_two, stats = call(
        turn,
        (second, gathered, counts, params, mask, x, back),
        (flat16, flat32, norm, two),
        after=actives[1:],
    )
    gathered = exchange(stats)
    if sides:
        actives += tuple(side_call((), (), ways.corners, (stats,)))
    inner_two, sums_two, turned_two = call(
        functools.partial(norm_back, 2),
        (grad_sum, second, norm_two, gathered, params, mask),
        (flat16, sums, turned_shape),
        after=actives[3:],
    )
    moved_two = ways.send(turned_two)
    grad_hidden, stats = conv_call(
        backward_middle, weight_two, (inner_two, hidden, norm_one, params, mask), (flat32, two)
    )
    gathered = exchange(stats)
    chip_two = ways.chip_sum(canvas, moved_two, actives, channels, (grad_hidden,))
    layer_x = (x, *sides, *ways.corners)
    inner_one, sums_one, turned_one = call(
        functools.partial(norm_back, 0),
        (grad_hidden, hidden, norm_one, gathered, params, mask),
        (flat16, sums, turned_shape),
        after=chip_two,
    )
    moved_one = ways.send(turned_one)
    core_two = ways.core_sum(chip_two, gathered)
    line_two = ways.line_sum(ways.pair_sum(core_two))
    (grad_input,) = conv_call(
        backward_input, weight_one, (inner_one, grad_sum, mask), (flat32,), after=core_two
    )
    chip_one = ways.chip_sum(canvas, moved_one, layer_x, channels, (grad_input,))
    pair_one = ways.pair_sum(ways.core_sum(chip_one), line_two)
    owned_two = ways.owned(line_two)
    owned_one = ways.owned(ways.line_sum(pair_one))

    results = adamw(
        kernels_turned,
        jnp.stack([owned_one, owned_two]),
        turned(kernel_first),
        turned(kernel_second),
        KERNEL_RATE,
        KERNEL_DECAY,
    )
    kernel_results = [
        jnp.transpose(value.reshape(2, 3, 3, width, channels), (0, 1, 2, 4, 3))
        for value in results
    ]
    norm_full = jnp.concatenate([sums_one, sums_two], axis=0)
    place = lax.axis_index(ways.shard_axes) * width
    norm_grads = lax.dynamic_slice_in_dim(norm_full, place, width, 1)
    norm_results = adamw(norm_params, norm_grads, norm_first, norm_second, NORM_RATE, 0.0)
    return (
        *canvas.unflatten(result),
        *canvas.unflatten(grad_input),
        *kernel_results,
        *norm_results,
    )


def solution(mesh):
    sizes = (mesh.shape["dp"], mesh.shape["fsdp"])
    if sizes == (2, 16):
        ways = Grid()
        mesh = Mesh(mesh.devices.reshape(2, 4, 2, 2), ways.axes)
    else:
        ways = Plain()
    images = P(ways.axes, None, None, None)
    maps = P(ways.axes, None, None)
    weights = P(None, None, None, None, ways.shard_axes)
    norms = P(None, ways.shard_axes)
    in_specs = (
        (images,) * 3 + (maps,) * 3 + (images,) * 3 + (weights, norms, weights, weights, norms, norms)
    )
    out_specs = (images,) * 6 + (weights,) * 3 + (norms,) * 3
    body = functools.partial(local, ways, sizes)
    return jax.shard_map(body, mesh=mesh, in_specs=in_specs, out_specs=out_specs, check_vma=False)
```

```python
import functools

import jax
import jax.numpy as jnp
from jax import lax
from jax.experimental import pallas as pl
from jax.experimental.pallas import tpu as pltpu
from jax.sharding import Mesh, PartitionSpec as P

STEP = 5
NORM_EPS = 1e-05
BETA_ONE = 0.5
BETA_TWO = 0.5
KERNEL_RATE = 0.03
NORM_RATE = 0.4
KERNEL_DECAY = 0.01
ADAM_EPS = 1e-08
TAPS = 9
LANES = 128
CELL = 2
VMEM_BYTES = 54 * 1024 * 1024
F32, BF16 = jnp.float32, jnp.bfloat16


def round_up(value, step):
    return (value + step - 1) // step * step


class Canvas:
    def __init__(self, shapes):
        self.shapes = shapes
        cells = [
            (side, group, first)
            for group, (count, side) in enumerate(shapes)
            for first in range(0, count, CELL)
        ]
        limit = max(
            sum(side + 1 for side, group, _ in cells if group == wanted)
            for wanted in range(len(shapes))
        )
        self.bands = []
        for side, group, first in sorted(cells, reverse=True):
            used = sum(cell[0] + 1 for cell in self.bands[-1]) if self.bands else limit
            if used + side + 1 > limit:
                self.bands.append([])
            self.bands[-1].append((side, group, first))
        self.width = limit
        self.right = CELL
        self.down = limit * CELL
        self.heights = [band[0][0] for band in self.bands]
        used_rows = (sum(self.heights) + len(self.bands) - 1) * self.down
        self.rows = round_up(used_rows, 16)
        self.halo = round_up(self.down + self.right, 8)
        self.lanes = round_up(self.rows + self.down + self.right, LANES)
        self.padded_rows = self.rows + 2 * self.halo
        self.sent_rows = self.rows + 16

    def cells(self):
        start = 0
        for band, height in zip(self.bands, self.heights):
            column = 0
            for side, group, first in band:
                yield side, group, first, start * self.down + column * CELL
                column += side + 1
            start += height + 1

    def unflatten(self, flat):
        parts = [[] for _ in self.shapes]
        start = 0
        for band, height in zip(self.bands, self.heights):
            rows = flat[start : start + height * self.down]
            rows = rows.reshape(height, self.width, CELL, flat.shape[1])
            column = 0
            for side, group, first in band:
                piece = rows[:side, column : column + side]
                parts[group].append((first, jnp.transpose(piece, (2, 0, 1, 3))))
                column += side + 1
            start += (height + 1) * self.down
        return [
            jnp.concatenate([piece for _, piece in sorted(part, key=lambda item: item[0])], axis=0)
            for part in parts
        ]

    def shift(self, tap):
        return (tap // 3 - 1) * self.down + (tap % 3 - 1) * self.right

    def place(self, buffer, value):
        edge = jnp.zeros((self.halo, value.shape[1]), F32)
        buffer[0 : self.halo, :] = edge
        buffer[self.halo : self.halo + self.rows, :] = value
        buffer[self.halo + self.rows :, :] = edge

    def shifted(self, buffer, tap, sign):
        start = self.halo + sign * self.shift(tap)
        return buffer[start : start + self.rows, :].astype(BF16)


def wide(mask_ref, channels):
    return jnp.concatenate([mask_ref[...]] * (channels // LANES), axis=1)


def multiply(left, right, left_dim, right_dim):
    return lax.dot_general(
        left, right, (((left_dim,), (right_dim,)), ((), ())), preferred_element_type=F32
    )


def column_sum(value):
    return jnp.sum(value, axis=0, keepdims=True)


def spread_rows(rows, ref):
    ref[...] = jnp.broadcast_to(jnp.concatenate(rows, axis=0)[None], ref.shape)


def local_statistics(hidden, valid, *refs):
    total = column_sum(hidden * valid)
    centre = total / jnp.maximum(column_sum(valid), 1.0)
    squares = column_sum(jnp.square(hidden - centre) * valid)
    rows = jnp.concatenate([total, squares], axis=0)
    *info, ref = [ref[...] for ref in refs[:-1]] + [refs[-1]]
    rows = jnp.concatenate([rows, *info], axis=1)
    ref[...] = jnp.broadcast_to(rows[None], ref.shape)


def global_statistics(gathered, counts):
    channels = counts.shape[1]
    totals, squares = gathered[:, 0, :channels], gathered[:, 1, :channels]
    total = column_sum(counts)
    centre = column_sum(totals) / total
    between = column_sum(counts * jnp.square(totals / jnp.maximum(counts, 1.0) - centre))
    spread = (column_sum(squares) + between) / total
    return centre, lax.rsqrt(spread + NORM_EPS), total


def lay_out(canvas, field_refs, buffer):
    buffer[...] = jnp.zeros_like(buffer)
    for side, group, first, start in canvas.cells():
        for down in range(side):
            for right in range(side):
                row = start + down * canvas.down + right * CELL
                pair = field_refs[group][down, right, first : first + CELL, :]
                buffer[row : row + CELL, :] = pair.astype(F32)


def prepare(canvas, *refs):
    *field_refs, param_ref = refs[:4]
    mask_refs = refs[4:7]
    x_ref, mask_ref, info_ref, buffer = refs[7:]
    rows, channels = buffer.shape
    mask_ref[...] = jnp.zeros_like(mask_ref)
    for side, group, first, start in canvas.cells():
        for down in range(side):
            for right in range(side):
                for image in range(CELL):
                    row = start + down * canvas.down + right * CELL + image
                    value = mask_refs[group][down, first + image, right].astype(F32)
                    mask_ref[row : row + 1, :] = jnp.full((1, LANES), value, F32)
    lay_out(canvas, field_refs, buffer)
    x_ref[0:rows, :] = (buffer[...] * wide(mask_ref, channels)).astype(BF16)
    line = jnp.transpose(mask_ref[...])[0:1]
    rest = jnp.zeros((1, channels * 2 - rows), F32)
    lines = [line[:, :channels], jnp.concatenate([line[:, channels:], rest], axis=1)]
    lines.append(jnp.zeros((14, channels), F32))
    x_ref[rows:, :] = jnp.concatenate(lines, axis=0).astype(BF16)
    params = param_ref[...].astype(BF16).astype(F32)
    rows = [params[index : index + 1] for index in range(4)]
    if params.size < LANES:
        rows.append(jnp.zeros((1, LANES - params.size), F32))
    row = jnp.concatenate(rows, axis=1)
    info_ref[...] = jnp.concatenate([row, column_sum(mask_ref[...])], axis=0)


def sent_pixels(canvas, refs):
    whole = jnp.concatenate([ref[...] for ref in refs], axis=0).astype(F32)
    return whole[: canvas.rows]


def sent_mask(canvas, refs):
    channels = refs[0].shape[1]
    turned = jnp.transpose(refs[-1][refs[-1].shape[0] - 16 :, :].astype(F32))
    column = jnp.concatenate([turned[:, 0:1], turned[: canvas.rows - channels, 1:2]], axis=0)
    return jnp.broadcast_to(column, (canvas.rows, channels))


def prepare_back(canvas, *refs):
    *field_refs, back_ref, buffer = refs
    lay_out(canvas, field_refs, buffer)
    back_ref[...] = buffer[...].astype(BF16)


def sigmoid(value):
    return 1.0 / (1.0 + jnp.exp(-value))


def swish_slope(value):
    logistic = sigmoid(value)
    return logistic * (1.0 + value * (1.0 - logistic))


class Whole:
    def __init__(self, array, width):
        self.arrays = self.last = [array]
        self.width = width

    @staticmethod
    def copies(refs, weight, taps, sem):
        return [pltpu.make_async_copy(refs[0].at[taps], weight.at[taps], sem)]


class Pieces:
    width = 32

    def __init__(self, pieces):
        self.arrays = [array for array, _, _ in pieces]
        self.last = self.arrays[-4:]
        self.places = [(slots, first) for _, slots, first in pieces]

    def copies(self, refs, weight, taps, sem):
        y, z, x, c = (lax.axis_index(name) for name in ("y", "z", "x", "c"))
        copies = []
        for ref, (slots, first) in zip(refs, self.places):
            _, _, rows, lanes = ref.shape
            for slot, (dy, dz, dx, dc) in enumerate(slots):
                shard = ((z ^ dz) * 2 + (x ^ dx)) * 2 + (c ^ dc)
                row = pl.multiple_of(shard * self.width + first, 16)
                lane = 0 if dy is None else pl.multiple_of((y ^ dy) * lanes, lanes)
                target = weight.at[taps, pl.ds(row, rows), pl.ds(lane, lanes)]
                copies.append(pltpu.make_async_copy(ref.at[slot, taps], target, sem))
        return copies


class Fetch:
    def __init__(self, source, refs, weight, sems):
        self.weight = weight
        self.parts = [
            source.copies(refs, weight, pl.ds(3 * part, 3), sems.at[part]) for part in range(3)
        ]
        for copies in self.parts:
            for copy in copies:
                copy.start()

    def ready(self, tap):
        if tap % 3 == 0 and self.parts:
            for copy in self.parts.pop(0):
                copy.wait()


def convolve(canvas, value, fetch, buffer, out_ref, sign):
    canvas.place(buffer, value)
    for tap in range(TAPS):
        part = canvas.shifted(buffer, tap, sign)
        fetch.ready(tap)
        product = multiply(part, fetch.weight[tap], 1, 1 if sign > 0 else 0)
        out_ref[...] = product if tap == 0 else out_ref[...] + product


def activate(hidden, norm_ref, param_ref, valid):
    normed = (hidden - norm_ref[0:1, :]) * norm_ref[1:2, :]
    value = normed * param_ref[0:1, :] + param_ref[1:2, :]
    return value * sigmoid(value) * valid


def side_active(canvas, source, parts, *refs):
    sent, refs = refs[: sum(parts)], refs[sum(parts) :]
    norm_ref, param_ref, *weights = refs[: 2 + len(source.arrays)]
    *active_refs, buffer, weight, sems, hidden = refs[2 + len(source.arrays) :]
    fetch = Fetch(source, weights, weight, sems)
    for count, active_ref in zip(parts, active_refs):
        pixels, sent = sent[:count], sent[count:]
        convolve(canvas, sent_pixels(canvas, pixels), fetch, buffer, hidden, 1)
        valid = sent_mask(canvas, pixels)
        active_ref[...] = activate(hidden[...], norm_ref, param_ref, valid).astype(BF16)


def forward_one(canvas, source, x_ref, mask_ref, info_ref, *refs):
    *weights, hidden_ref, stats_ref, buffer, weight, sem = refs
    fetch = Fetch(source, weights, weight, sem)
    convolve(canvas, sent_pixels(canvas, [x_ref]), fetch, buffer, hidden_ref, 1)
    local_statistics(hidden_ref[...], wide(mask_ref, x_ref.shape[1]), info_ref, stats_ref)


def forward_two(canvas, source, hidden_ref, gathered_ref, mask_ref, *refs):
    *weights, active_ref, second_ref, norm_ref, param_ref, count_ref, stats_ref = refs[:-3]
    buffer, weight, sem = refs[-3:]
    fetch = Fetch(source, weights, weight, sem)
    channels = hidden_ref.shape[1]
    valid = wide(mask_ref, channels)
    width = source.width
    rows = []
    for index in range(4):
        start = channels + index * width
        rows.append(
            jnp.concatenate(
                [gathered_ref[shard, 0:1, start : start + width] for shard in range(channels // width)],
                axis=1,
            )
        )
    param_ref[...] = jnp.concatenate(rows, axis=0)
    counts = gathered_ref[:, 1, channels : channels + LANES]
    count_ref[...] = jnp.concatenate([counts] * (channels // LANES), axis=1)

    centre, inv, total = global_statistics(gathered_ref, count_ref[...])
    norm_ref[...] = jnp.concatenate([centre, inv, total, total], axis=0)
    value = activate(hidden_ref[...], norm_ref, param_ref, valid)
    active_ref[...] = value.astype(BF16)
    convolve(canvas, value, fetch, buffer, second_ref, 1)
    local_statistics(second_ref[...], valid, stats_ref)


def turn(
    second_ref,
    gathered_ref,
    count_ref,
    param_ref,
    mask_ref,
    x_ref,
    back_ref,
    result_ref,
    grad_ref,
    norm_ref,
    stats_ref,
):
    valid = wide(mask_ref, second_ref.shape[1])
    centre, inv, total = global_statistics(gathered_ref, count_ref[...])
    norm_ref[...] = jnp.concatenate([centre, inv, total, total], axis=0)
    normed = (second_ref[...] - centre) * inv
    rows = second_ref.shape[0]
    summed = normed * param_ref[2:3, :] + param_ref[3:4, :] + x_ref[0:rows, :].astype(F32)
    logistic = sigmoid(summed)
    result_ref[...] = (summed * logistic * valid).astype(BF16)
    slope = logistic * (1.0 + summed * (1.0 - logistic))
    grad = back_ref[...].astype(F32) * valid * slope
    grad_ref[...] = grad
    spread_rows([column_sum(grad), column_sum(grad * normed)], stats_ref)


def norm_back(
    row,
    grad_ref,
    hidden_ref,
    norm_ref,
    gathered_ref,
    param_ref,
    mask_ref,
    inner_ref,
    sums_ref,
    turned_ref,
):
    valid = wide(mask_ref, grad_ref.shape[1])
    shift_grad = column_sum(gathered_ref[:, 0, :])
    gain_grad = column_sum(gathered_ref[:, 1, :])
    sums_ref[...] = jnp.concatenate([gain_grad, shift_grad], axis=0)
    centre, inv, total = norm_ref[0:1, :], norm_ref[1:2, :], norm_ref[2:3, :]
    normed = (hidden_ref[...] - centre) * inv
    grad = grad_ref[...] - shift_grad / total - normed * (gain_grad / total)
    inner = valid * (param_ref[row : row + 1, :] * inv) * grad
    inner_ref[...] = inner.astype(BF16)
    turned = jnp.transpose(inner).astype(BF16)
    rows, channels = inner.shape
    if len(turned_ref.shape) == 2:
        turned_ref[...] = turned
        return
    lanes = turned_ref.shape[-1]
    turned = jnp.concatenate([turned, jnp.zeros((channels, lanes - rows), BF16)], axis=1)
    half = channels // 32
    for shard in range(16):
        z, x, c = shard // 4, shard // 2 % 2, shard % 2
        for y in range(2):
            start = (shard * 2 + y) * half
            turned_ref[y, x, c, z * half : (z + 1) * half, :] = turned[start : start + half]


def backward_middle(canvas, source, inner_ref, hidden_ref, norm_ref, param_ref, mask_ref, *refs):
    *weights, grad_ref, stats_ref, buffer, weight, sem = refs
    valid = wide(mask_ref, hidden_ref.shape[1])
    fetch = Fetch(source, weights, weight, sem)
    convolve(canvas, inner_ref[...].astype(F32), fetch, buffer, grad_ref, -1)
    normed = (hidden_ref[...] - norm_ref[0:1, :]) * norm_ref[1:2, :]
    value = normed * param_ref[0:1, :] + param_ref[1:2, :]
    grad = grad_ref[...] * valid * swish_slope(value)
    grad_ref[...] = grad
    spread_rows([column_sum(grad), column_sum(grad * normed)], stats_ref)


def backward_input(canvas, source, inner_ref, residual_ref, mask_ref, *refs):
    *weights, grad_ref, buffer, weight, sem = refs
    fetch = Fetch(source, weights, weight, sem)
    convolve(canvas, inner_ref[...].astype(F32), fetch, buffer, grad_ref, -1)
    grad_ref[...] = residual_ref[...] + wide(mask_ref, grad_ref.shape[1]) * grad_ref[...]


def kernel_grad_whole(canvas, turned_ref, active_ref, out_ref, buffer):
    canvas.place(buffer, active_ref[0 : canvas.rows, :].astype(F32))
    for tap in range(TAPS):
        product = multiply(turned_ref[...], canvas.shifted(buffer, tap, 1), 1, 0)
        out_ref[tap] = product.astype(out_ref.dtype)


def kernel_grad_layer(canvas, turned_ref, *refs):
    *active_refs, send_ref, keep_ref, left, total = refs
    y, x, c = lax.axis_index("y"), lax.axis_index("x"), lax.axis_index("c")
    part = turned_ref.shape[3]
    for index in range(4):
        block_y, block_x = y ^ (index // 2), x ^ (index % 2)
        for core in range(2):
            turned = turned_ref[block_y, block_x, c ^ core].astype(F32)
            for tap in range(TAPS):
                shift = canvas.shift(tap) % canvas.lanes
                moved = pltpu.roll(turned, shift, 1) if shift else turned
                row = (core * TAPS + tap) * part
                left[row : row + part, :] = moved[:, : canvas.rows].astype(BF16)
        start = 0
        for part_ref in active_refs[index : index + 1] if index < 3 else active_refs[3:]:
            rows = min(part_ref.shape[0], canvas.rows - start)
            product = multiply(left[:, start : start + rows], part_ref[0:rows, :], 1, 0)
            total[...] = product if index + start == 0 else total[...] + product
            start += rows
    half = part // 4
    for core, out_ref in enumerate((keep_ref, send_ref)):
        for tap in range(TAPS):
            for z in range(4):
                row = (core * TAPS + tap) * part + (lax.axis_index("z") ^ z) * half
                out_ref[z, tap] = total[pl.ds(row, half), :].astype(out_ref.dtype)


def call(body, inputs, outputs, scratch=(), weights=(), after=(), scalars=()):
    whole = pl.BlockSpec(memory_space=pltpu.VMEM)
    anywhere = pl.BlockSpec(memory_space=pltpu.HBM)
    read = len(inputs) + len(scalars) + len(weights)

    def kernel(*refs):
        body(*refs[:read], *refs[read + len(after) :])

    return pl.pallas_call(
        kernel,
        out_shape=[jax.ShapeDtypeStruct(shape, dtype) for shape, dtype in outputs],
        in_specs=[whole] * len(inputs)
        + [pl.BlockSpec(memory_space=pltpu.SMEM)] * len(scalars)
        + [anywhere] * (len(weights) + len(after)),
        out_specs=[whole] * len(outputs),
        scratch_shapes=list(scratch),
        compiler_params=pltpu.CompilerParams(vmem_limit_bytes=VMEM_BYTES),
    )(*inputs, *scalars, *weights, *after)


def adamw(param, grad, first, second, rate, decay):
    first_new = BETA_ONE * first + (1.0 - BETA_ONE) * grad
    second_new = BETA_TWO * second + (1.0 - BETA_TWO) * grad * grad
    first_hat = first_new / (1.0 - BETA_ONE**STEP)
    second_hat = second_new / (1.0 - BETA_TWO**STEP)
    update = first_hat / (jnp.sqrt(second_hat) + ADAM_EPS)
    return (param - rate * (update + decay * param), first_new, second_new)


def flip(value, axis, bit, size):
    return lax.ppermute(value, axis, [(place, place ^ bit) for place in range(size)])


def behind(value, others):
    return lax.optimization_barrier((value, *others))[0] if others else value


class Gather:
    def __init__(self, shard, half):
        self.shard, self.half = shard[None], half[None]

    def along_two(self, *others):
        self.second = flip(behind(self.half, others), "z", 2, 4)

    def beside(self, *others):
        self.nearest = flip(behind(self.shard, others), "x", 1, 2)

    def along_one(self, *others):
        both = jnp.concatenate([self.half, self.second], axis=0)
        self.line = flip(behind(both, others), "z", 1, 4)

    def across(self, *others):
        self.rest = jnp.concatenate([self.second, self.line], axis=0)
        rest = behind(self.rest, others)
        self.over = flip(rest, "x", 1, 2), flip(rest, "y", 1, 2)

    def corner(self, *others):
        rows = self.shard.shape[2] // 2
        over_x, over_y = self.over
        self.corners = (
            flip(behind(over_y[:, :, :rows], others), "x", 1, 2),
            flip(behind(over_x[:, :, rows:], others), "y", 1, 2),
        )

    def cores(self, early=(), late=()):
        rows = self.shard.shape[2] // 2
        deep = (2, 1, 3)
        pieces = [
            (self.shard, [(None, 0, 0)], 0),
            (self.nearest, [(None, 0, 1)], 0),
            (self.rest, [(0, dz, 0) for dz in deep], 0),
            (self.over[0], [(0, dz, 1) for dz in deep], 0),
            (self.over[1], [(1, dz, 0) for dz in deep], 0),
            (self.corners[0], [(1, dz, 1) for dz in deep], 0),
            (self.corners[1], [(1, dz, 1) for dz in deep], rows),
        ]
        self.found = []
        for index, (array, slots, first) in enumerate(pieces):
            others = late if index > 4 else early if index > 2 else ()
            other = flip(behind(array, others), "c", 1, 2)
            self.found.append((array, [slot + (0,) for slot in slots], first))
            self.found.append((other, [slot + (1,) for slot in slots], first))


class Grid:
    axes = ("y", "z", "x", "c")
    shard_axes = ("z", "x", "c")

    def weights(self, low, x, back):
        half = low.shape[3] // 2
        first, second = lax.dynamic_slice_in_dim(low, lax.axis_index("y") * half, half, 3)
        one, two = Gather(low[0], first), Gather(low[1], second)
        one.along_two()
        one.beside()
        self.sides = flip(x, "x", 1, 2), flip(x, "y", 1, 2)
        one.along_one(x, one.nearest)
        two.along_two(one.line)
        one.across(*self.sides)
        two.along_one(*one.over)
        one.corner()
        one.cores()
        two.beside(*one.corners)
        two.across(back, *one.corners)
        self.second = two
        return Pieces(one.found)

    def second_weights(self, stats, gathered):
        over_x, over_y = self.sides
        rows = round_up(over_x.shape[0] // 2, 16)
        self.second.corner(stats)
        self.second.cores((stats,), (gathered,))
        self.corners = (
            flip(behind(over_y[:rows], (gathered,)), "x", 1, 2),
            flip(behind(over_x[rows:], (gathered,)), "y", 1, 2),
        )
        return Pieces(self.second.found)

    def turned_shape(self, canvas, channels):
        return ((2, 2, 2, channels // 8, canvas.lanes), BF16)

    def send(self, turned):
        shape = turned.shape
        moved = lax.all_to_all(turned.reshape(4, *shape[2:]), ("y", "x"), 0, 0, tiled=True)
        return moved.reshape(shape)

    def chip_sum(self, canvas, moved, layer, channels, after):
        out = (4, TAPS, channels // 32, channels)
        part = moved.shape[3]
        send, keep = call(
            functools.partial(kernel_grad_layer, canvas),
            (moved, *layer),
            ((out, BF16), (out, F32)),
            (
                pltpu.VMEM((2 * TAPS * part, canvas.rows), BF16),
                pltpu.VMEM((2 * TAPS * part, channels), F32),
            ),
            after=after,
        )
        return send, keep

    def core_sum(self, chip, *others):
        send, keep = chip
        other = flip(behind(send, others), "c", 1, 2)
        near, far = (keep[part::2] + other[part::2].astype(F32) for part in range(2))
        return near, far.astype(BF16)

    def pair_sum(self, parts, *others):
        near, far = parts
        return near + flip(behind(far, others), "z", 1, 4).astype(F32)

    def line_sum(self, near):
        return near[0] + flip(near[1].astype(BF16), "z", 2, 4).astype(F32)

    def owned(self, line):
        own = line.astype(BF16)
        other = flip(own, "y", 1, 2)
        first = lax.axis_index("y") == 0
        halves = [jnp.where(first, own, other), jnp.where(first, other, own)]
        return jnp.concatenate(halves, axis=1).astype(F32)


class Plain:
    axes = ("dp", "fsdp")
    shard_axes = ("fsdp",)

    sides = corners = ()

    def weights(self, low, x, back):
        full = lax.all_gather(low, "fsdp", axis=2, tiled=True)
        first, self.second = [Whole(array, low.shape[2]) for array in full]
        return first

    def second_weights(self, stats, gathered):
        return self.second

    def turned_shape(self, canvas, channels):
        return ((channels, canvas.rows), BF16)

    def send(self, turned):
        return turned

    def chip_sum(self, canvas, turned, layer, channels, after):
        (full,) = call(
            functools.partial(kernel_grad_whole, canvas),
            (turned, layer[0]),
            (((TAPS, channels, channels), BF16),),
            (pltpu.VMEM((canvas.padded_rows, channels), F32),),
            after=after,
        )
        return (full,)

    def core_sum(self, chip, *others):
        return chip

    def pair_sum(self, parts, *others):
        return parts[0]

    def line_sum(self, full):
        return lax.psum_scatter(full, "fsdp", scatter_dimension=1, tiled=True)

    def owned(self, line):
        return lax.psum(line, "dp").astype(F32)


def local(
    ways,
    sizes,
    field_five,
    field_seven,
    field_nine,
    mask_five,
    mask_seven,
    mask_nine,
    back_five,
    back_seven,
    back_nine,
    kernels,
    norm_params,
    kernel_first,
    kernel_second,
    norm_first,
    norm_second,
):
    copies, shards = sizes
    fields = (field_five, field_seven, field_nine)
    masks = (mask_five, mask_seven, mask_nine)
    backs = (back_five, back_seven, back_nine)
    channels = field_five.shape[3]
    width = kernels.shape[4]
    canvas = Canvas([(field.shape[0], field.shape[1]) for field in fields])
    rows = canvas.rows
    count = copies * shards

    def turned(kernel):
        return jnp.transpose(kernel, (0, 1, 2, 4, 3)).reshape(2, TAPS, width, channels)

    def exchange(spread):
        return lax.all_to_all(spread, ways.axes, 0, 0, tiled=True)

    kernels_turned = turned(kernels)
    low = kernels_turned.astype(BF16)

    buffer = pltpu.VMEM((rows, channels), F32)
    weighted = (
        pltpu.VMEM((canvas.padded_rows, channels), F32),
        pltpu.VMEM((TAPS, channels, channels), BF16),
        pltpu.SemaphoreType.DMA((3,)),
    )
    flat32 = ((rows, channels), F32)
    flat16 = ((rows, channels), BF16)
    two = ((count, 2, channels), F32)
    norm = ((4, channels), F32)
    sums = ((2, channels), F32)
    turned_shape = ways.turned_shape(canvas, channels)

    def conv_call(body, source, inputs, outputs, after=()):
        return call(
            functools.partial(body, canvas, source),
            inputs,
            outputs,
            weighted,
            source.arrays,
            after,
        )

    x, mask, info = call(
        functools.partial(prepare, canvas),
        (*[jnp.transpose(field, (1, 2, 0, 3)) for field in fields], norm_params),
        (((canvas.sent_rows, channels), BF16), ((rows, LANES), F32), ((2, LANES), F32)),
        (buffer,),
        scalars=[jnp.transpose(mask, (1, 0, 2)) for mask in masks],
    )
    (back,) = call(
        functools.partial(prepare_back, canvas),
        [jnp.transpose(field, (1, 2, 0, 3)) for field in backs],
        (flat16,),
        (buffer,),
    )
    weight_one = ways.weights(low, x, back)
    sides = ways.sides
    hidden, stats = conv_call(
        forward_one,
        weight_one,
        (x, mask, info),
        (flat32, ((count, 2, channels + LANES), F32)),
        after=sides,
    )
    gathered = exchange(stats)
    weight_two = ways.second_weights(stats, gathered)
    active, second, norm_one, params, counts, stats = conv_call(
        forward_two,
        weight_two,
        (hidden, gathered, mask),
        (flat16, flat32, norm, norm, ((count, channels), F32), two),
    )
    gathered = exchange(stats)
    actives = (active,)

    def side_call(images, after):
        return call(
            functools.partial(side_active, canvas, weight_one, [len(parts) for parts in images]),
            (*[part for parts in images for part in parts], norm_one, params),
            (flat16,) * len(images),
            (*weighted, pltpu.VMEM((rows, channels), F32)),
            weight_one.arrays,
            after,
        )

    if sides:
        actives += tuple(side_call([[part] for part in sides], (stats,)))
    result, grad_sum, norm_two, stats = call(
        turn,
        (second, gathered, counts, params, mask, x, back),
        (flat16, flat32, norm, two),
        after=actives[1:],
    )
    gathered = exchange(stats)
    if sides:
        actives += tuple(side_call([ways.corners], (stats,)))
    inner_two, sums_two, turned_two = call(
        functools.partial(norm_back, 2),
        (grad_sum, second, norm_two, gathered, params, mask),
        (flat16, sums, turned_shape),
        after=actives[3:],
    )
    moved_two = ways.send(turned_two)
    grad_hidden, stats = conv_call(
        backward_middle, weight_two, (inner_two, hidden, norm_one, params, mask), (flat32, two)
    )
    gathered = exchange(stats)
    chip_two = ways.chip_sum(canvas, moved_two, actives, channels, (grad_hidden,))
    layer_x = (x, *sides, *ways.corners)
    inner_one, sums_one, turned_one = call(
        functools.partial(norm_back, 0),
        (grad_hidden, hidden, norm_one, gathered, params, mask),
        (flat16, sums, turned_shape),
        after=chip_two,
    )
    moved_one = ways.send(turned_one)
    core_two = ways.core_sum(chip_two, gathered)
    line_two = ways.line_sum(ways.pair_sum(core_two))
    (grad_input,) = conv_call(
        backward_input, weight_one, (inner_one, grad_sum, mask), (flat32,), after=core_two
    )
    chip_one = ways.chip_sum(canvas, moved_one, layer_x, channels, (grad_input, line_two))
    pair_one = ways.pair_sum(ways.core_sum(chip_one))
    owned_two = ways.owned(line_two)
    owned_one = ways.owned(ways.line_sum(pair_one))

    results = adamw(
        kernels_turned,
        jnp.stack([owned_one, owned_two]),
        turned(kernel_first),
        turned(kernel_second),
        KERNEL_RATE,
        KERNEL_DECAY,
    )
    kernel_results = [
        jnp.transpose(value.reshape(2, 3, 3, width, channels), (0, 1, 2, 4, 3))
        for value in results
    ]
    norm_full = jnp.concatenate([sums_one, sums_two], axis=0)
    place = lax.axis_index(ways.shard_axes) * width
    norm_grads = lax.dynamic_slice_in_dim(norm_full, place, width, 1)
    norm_results = adamw(norm_params, norm_grads, norm_first, norm_second, NORM_RATE, 0.0)
    return (
        *canvas.unflatten(result),
        *canvas.unflatten(grad_input),
        *kernel_results,
        *norm_results,
    )


def solution(mesh):
    sizes = (mesh.shape["dp"], mesh.shape["fsdp"])
    if sizes == (2, 16):
        ways = Grid()
        mesh = Mesh(mesh.devices.reshape(2, 4, 2, 2), ways.axes)
    else:
        ways = Plain()
    images = P(ways.axes, None, None, None)
    maps = P(ways.axes, None, None)
    weights = P(None, None, None, None, ways.shard_axes)
    norms = P(None, ways.shard_axes)
    in_specs = (
        (images,) * 3 + (maps,) * 3 + (images,) * 3 + (weights, norms, weights, weights, norms, norms)
    )
    out_specs = (images,) * 6 + (weights,) * 3 + (norms,) * 3
    body = functools.partial(local, ways, sizes)
    return jax.shard_map(body, mesh=mesh, in_specs=in_specs, out_specs=out_specs, check_vma=False)
```

```python
import functools

import jax
import jax.numpy as jnp
from jax import lax
from jax.experimental import pallas as pl
from jax.experimental.pallas import tpu as pltpu
from jax.sharding import Mesh, PartitionSpec as P

STEP = 5
NORM_EPS = 1e-05
BETA_ONE = 0.5
BETA_TWO = 0.5
KERNEL_RATE = 0.03
NORM_RATE = 0.4
KERNEL_DECAY = 0.01
ADAM_EPS = 1e-08
TAPS = 9
LANES = 128
CELL = 2
VMEM_BYTES = 54 * 1024 * 1024
F32, BF16 = jnp.float32, jnp.bfloat16


def round_up(value, step):
    return (value + step - 1) // step * step


class Canvas:
    def __init__(self, shapes):
        self.shapes = shapes
        cells = [
            (side, group, first)
            for group, (count, side) in enumerate(shapes)
            for first in range(0, count, CELL)
        ]
        limit = max(
            sum(side + 1 for side, group, _ in cells if group == wanted)
            for wanted in range(len(shapes))
        )
        self.bands = []
        for side, group, first in sorted(cells, reverse=True):
            used = sum(cell[0] + 1 for cell in self.bands[-1]) if self.bands else limit
            if used + side + 1 > limit:
                self.bands.append([])
            self.bands[-1].append((side, group, first))
        self.width = limit
        self.right = CELL
        self.down = limit * CELL
        self.heights = [band[0][0] for band in self.bands]
        used_rows = (sum(self.heights) + len(self.bands) - 1) * self.down
        self.rows = round_up(used_rows, 16)
        self.halo = round_up(self.down + self.right, 8)
        self.lanes = round_up(self.rows + self.down + self.right, LANES)
        self.padded_rows = self.rows + 2 * self.halo
        self.sent_rows = self.rows + 16

    def cells(self):
        start = 0
        for band, height in zip(self.bands, self.heights):
            column = 0
            for side, group, first in band:
                yield side, group, first, start * self.down + column * CELL
                column += side + 1
            start += height + 1

    def unflatten(self, flat):
        parts = [[] for _ in self.shapes]
        start = 0
        for band, height in zip(self.bands, self.heights):
            rows = flat[start : start + height * self.down]
            rows = rows.reshape(height, self.width, CELL, flat.shape[1])
            column = 0
            for side, group, first in band:
                piece = rows[:side, column : column + side]
                parts[group].append((first, jnp.transpose(piece, (2, 0, 1, 3))))
                column += side + 1
            start += (height + 1) * self.down
        return [
            jnp.concatenate([piece for _, piece in sorted(part, key=lambda item: item[0])], axis=0)
            for part in parts
        ]

    def shift(self, tap):
        return (tap // 3 - 1) * self.down + (tap % 3 - 1) * self.right

    def place(self, buffer, value):
        edge = jnp.zeros((self.halo, value.shape[1]), F32)
        buffer[0 : self.halo, :] = edge
        buffer[self.halo : self.halo + self.rows, :] = value
        buffer[self.halo + self.rows :, :] = edge

    def shifted(self, buffer, tap, sign):
        start = self.halo + sign * self.shift(tap)
        return buffer[start : start + self.rows, :].astype(BF16)


def wide(mask_ref, channels):
    return jnp.concatenate([mask_ref[...]] * (channels // LANES), axis=1)


def multiply(left, right, left_dim, right_dim):
    return lax.dot_general(
        left, right, (((left_dim,), (right_dim,)), ((), ())), preferred_element_type=F32
    )


def column_sum(value):
    return jnp.sum(value, axis=0, keepdims=True)


def spread_rows(rows, ref):
    ref[...] = jnp.broadcast_to(jnp.concatenate(rows, axis=0)[None], ref.shape)


def local_statistics(hidden, valid, *refs):
    total = column_sum(hidden * valid)
    centre = total / jnp.maximum(column_sum(valid), 1.0)
    squares = column_sum(jnp.square(hidden - centre) * valid)
    rows = jnp.concatenate([total, squares], axis=0)
    *info, ref = [ref[...] for ref in refs[:-1]] + [refs[-1]]
    rows = jnp.concatenate([rows, *info], axis=1)
    ref[...] = jnp.broadcast_to(rows[None], ref.shape)


def global_statistics(gathered, counts):
    channels = counts.shape[1]
    totals, squares = gathered[:, 0, :channels], gathered[:, 1, :channels]
    total = column_sum(counts)
    centre = column_sum(totals) / total
    between = column_sum(counts * jnp.square(totals / jnp.maximum(counts, 1.0) - centre))
    spread = (column_sum(squares) + between) / total
    return centre, lax.rsqrt(spread + NORM_EPS), total


def lay_out(canvas, field_refs, buffer):
    buffer[...] = jnp.zeros_like(buffer)
    for side, group, first, start in canvas.cells():
        for down in range(side):
            for right in range(side):
                row = start + down * canvas.down + right * CELL
                pair = field_refs[group][down, right, first : first + CELL, :]
                buffer[row : row + CELL, :] = pair.astype(F32)


def prepare(canvas, *refs):
    *field_refs, param_ref = refs[:4]
    mask_refs = refs[4:7]
    x_ref, mask_ref, info_ref, buffer = refs[7:]
    rows, channels = buffer.shape
    mask_ref[...] = jnp.zeros_like(mask_ref)
    for side, group, first, start in canvas.cells():
        for down in range(side):
            for right in range(side):
                for image in range(CELL):
                    row = start + down * canvas.down + right * CELL + image
                    value = mask_refs[group][down, first + image, right].astype(F32)
                    mask_ref[row : row + 1, :] = jnp.full((1, LANES), value, F32)
    lay_out(canvas, field_refs, buffer)
    x_ref[0:rows, :] = (buffer[...] * wide(mask_ref, channels)).astype(BF16)
    line = jnp.transpose(mask_ref[...])[0:1]
    rest = jnp.zeros((1, channels * 2 - rows), F32)
    lines = [line[:, :channels], jnp.concatenate([line[:, channels:], rest], axis=1)]
    lines.append(jnp.zeros((14, channels), F32))
    x_ref[rows:, :] = jnp.concatenate(lines, axis=0).astype(BF16)
    params = param_ref[...].astype(BF16).astype(F32)
    rows = [params[index : index + 1] for index in range(4)]
    if params.size < LANES:
        rows.append(jnp.zeros((1, LANES - params.size), F32))
    row = jnp.concatenate(rows, axis=1)
    info_ref[...] = jnp.concatenate([row, column_sum(mask_ref[...])], axis=0)


def sent_mask(canvas, lines):
    channels = lines.shape[1]
    turned = jnp.transpose(lines)
    column = jnp.concatenate([turned[:, 0:1], turned[: canvas.rows - channels, 1:2]], axis=0)
    return jnp.broadcast_to(column, (canvas.rows, channels))


def prepare_back(canvas, *refs):
    *field_refs, back_ref, buffer = refs
    lay_out(canvas, field_refs, buffer)
    back_ref[...] = buffer[...].astype(BF16)


def sigmoid(value):
    return 1.0 / (1.0 + jnp.exp(-value))


def swish_slope(value):
    logistic = sigmoid(value)
    return logistic * (1.0 + value * (1.0 - logistic))


class Whole:
    def __init__(self, array, width):
        self.arrays = self.last = [array]
        self.width = width

    @staticmethod
    def copies(refs, weight, taps, sem):
        return [pltpu.make_async_copy(refs[0].at[taps], weight.at[taps], sem)]


class Pieces:
    width = 32

    def __init__(self, pieces):
        self.arrays = [array for array, _, _ in pieces]
        self.last = self.arrays[-4:]
        self.places = [(slots, first) for _, slots, first in pieces]

    def copies(self, refs, weight, taps, sem):
        y, z, x, c = (lax.axis_index(name) for name in ("y", "z", "x", "c"))
        copies = []
        for ref, (slots, first) in zip(refs, self.places):
            _, _, rows, lanes = ref.shape
            for slot, (dy, dz, dx, dc) in enumerate(slots):
                shard = ((z ^ dz) * 2 + (x ^ dx)) * 2 + (c ^ dc)
                row = pl.multiple_of(shard * self.width + first, 16)
                lane = 0 if dy is None else pl.multiple_of((y ^ dy) * lanes, lanes)
                target = weight.at[taps, pl.ds(row, rows), pl.ds(lane, lanes)]
                copies.append(pltpu.make_async_copy(ref.at[slot, taps], target, sem))
        return copies


class Fetch:
    def __init__(self, source, refs, weight, sems, target=None):
        self.weight, self.sems, self.target = weight, sems, target
        self.parts = [
            source.copies(refs, weight, pl.ds(3 * part, 3), sems.at[part]) for part in range(3)
        ]
        for copies in self.parts:
            for copy in copies:
                copy.start()

    def ready(self, tap):
        if tap % 3 == 0 and self.parts:
            for copy in self.parts.pop(0):
                copy.wait()
            if not self.parts and self.target is not None:
                self.store = pltpu.make_async_copy(self.weight, self.target, self.sems.at[0])
                self.store.start()


def convolve(canvas, value, fetch, buffer, out_ref, sign):
    canvas.place(buffer, value)
    for tap in range(TAPS):
        part = canvas.shifted(buffer, tap, sign)
        fetch.ready(tap)
        product = multiply(part, fetch.weight[tap], 1, 1 if sign > 0 else 0)
        out_ref[...] = product if tap == 0 else out_ref[...] + product


def activate(hidden, norm_ref, param_ref, valid):
    normed = (hidden - norm_ref[0:1, :]) * norm_ref[1:2, :]
    value = normed * param_ref[0:1, :] + param_ref[1:2, :]
    return value * sigmoid(value) * valid


def side_hidden(canvas, source, *refs):
    *weights, sent_hbm, hidden_ref, full_ref, buffer, weight, sems, sent, sent_sem = refs
    copy = pltpu.make_async_copy(sent_hbm, sent, sent_sem)
    copy.start()
    fetch = Fetch(source, weights, weight, sems, full_ref)
    copy.wait()
    convolve(canvas, sent[0 : canvas.rows, :].astype(F32), fetch, buffer, hidden_ref, 1)
    fetch.store.wait()


def side_active(canvas, source, known, *refs):
    norm_ref, param_ref, *refs = refs
    hidden_refs, refs = refs[:known], refs[known:]
    weights, refs = refs[: len(source.arrays)], refs[len(source.arrays) :]
    sent_hbm, refs = refs[: 1 + known], refs[1 + known :]
    active_refs, refs = refs[: 1 + known], refs[1 + known :]
    buffer, weight, sems, hidden, sent, lines, sent_sems = refs
    copies = [pltpu.make_async_copy(sent_hbm[0], sent, sent_sems.at[0])]
    for other in sent_hbm[1:]:
        tail = other.at[pl.ds(canvas.rows, 16)]
        copies.append(pltpu.make_async_copy(tail, lines, sent_sems.at[1]))
    for copy in copies:
        copy.start()
    fetch = Fetch(source, weights, weight, sems)
    for hidden_ref, active_ref in zip(hidden_refs, active_refs[1:]):
        copies[1].wait()
        valid = sent_mask(canvas, lines[...].astype(F32))
        active_ref[...] = activate(hidden_ref[...], norm_ref, param_ref, valid).astype(BF16)
    copies[0].wait()
    convolve(canvas, sent[0 : canvas.rows, :].astype(F32), fetch, buffer, hidden, 1)
    valid = sent_mask(canvas, sent[canvas.rows :, :].astype(F32))
    active_refs[0][...] = activate(hidden[...], norm_ref, param_ref, valid).astype(BF16)


def forward_one(canvas, source, x_ref, mask_ref, info_ref, *refs):
    *weights, hidden_ref, stats_ref, buffer, weight, sem = refs
    fetch = Fetch(source, weights, weight, sem)
    convolve(canvas, x_ref[0 : canvas.rows, :].astype(F32), fetch, buffer, hidden_ref, 1)
    local_statistics(hidden_ref[...], wide(mask_ref, x_ref.shape[1]), info_ref, stats_ref)


def forward_two(canvas, source, hidden_ref, gathered_ref, mask_ref, *refs):
    *weights, active_ref, second_ref, norm_ref, param_ref, count_ref, stats_ref = refs[:-3]
    buffer, weight, sem = refs[-3:]
    fetch = Fetch(source, weights, weight, sem)
    channels = hidden_ref.shape[1]
    valid = wide(mask_ref, channels)
    width = source.width
    rows = []
    for index in range(4):
        start = channels + index * width
        rows.append(
            jnp.concatenate(
                [gathered_ref[shard, 0:1, start : start + width] for shard in range(channels // width)],
                axis=1,
            )
        )
    param_ref[...] = jnp.concatenate(rows, axis=0)
    counts = gathered_ref[:, 1, channels : channels + LANES]
    count_ref[...] = jnp.concatenate([counts] * (channels // LANES), axis=1)

    centre, inv, total = global_statistics(gathered_ref, count_ref[...])
    norm_ref[...] = jnp.concatenate([centre, inv, total, total], axis=0)
    value = activate(hidden_ref[...], norm_ref, param_ref, valid)
    active_ref[...] = value.astype(BF16)
    convolve(canvas, value, fetch, buffer, second_ref, 1)
    local_statistics(second_ref[...], valid, stats_ref)


def turn(
    second_ref,
    gathered_ref,
    count_ref,
    param_ref,
    mask_ref,
    x_ref,
    back_ref,
    result_ref,
    grad_ref,
    norm_ref,
    stats_ref,
):
    valid = wide(mask_ref, second_ref.shape[1])
    centre, inv, total = global_statistics(gathered_ref, count_ref[...])
    norm_ref[...] = jnp.concatenate([centre, inv, total, total], axis=0)
    normed = (second_ref[...] - centre) * inv
    rows = second_ref.shape[0]
    summed = normed * param_ref[2:3, :] + param_ref[3:4, :] + x_ref[0:rows, :].astype(F32)
    logistic = sigmoid(summed)
    result_ref[...] = (summed * logistic * valid).astype(BF16)
    slope = logistic * (1.0 + summed * (1.0 - logistic))
    grad = back_ref[...].astype(F32) * valid * slope
    grad_ref[...] = grad
    spread_rows([column_sum(grad), column_sum(grad * normed)], stats_ref)


def norm_back(
    row,
    grad_ref,
    hidden_ref,
    norm_ref,
    gathered_ref,
    param_ref,
    mask_ref,
    inner_ref,
    sums_ref,
    turned_ref,
):
    valid = wide(mask_ref, grad_ref.shape[1])
    shift_grad = column_sum(gathered_ref[:, 0, :])
    gain_grad = column_sum(gathered_ref[:, 1, :])
    sums_ref[...] = jnp.concatenate([gain_grad, shift_grad], axis=0)
    centre, inv, total = norm_ref[0:1, :], norm_ref[1:2, :], norm_ref[2:3, :]
    normed = (hidden_ref[...] - centre) * inv
    grad = grad_ref[...] - shift_grad / total - normed * (gain_grad / total)
    inner = valid * (param_ref[row : row + 1, :] * inv) * grad
    inner_ref[...] = inner.astype(BF16)
    turned = jnp.transpose(inner).astype(BF16)
    rows, channels = inner.shape
    if len(turned_ref.shape) == 2:
        turned_ref[...] = turned
        return
    lanes = turned_ref.shape[-1]
    turned = jnp.concatenate([turned, jnp.zeros((channels, lanes - rows), BF16)], axis=1)
    half = channels // 32
    for shard in range(16):
        z, x, c = shard // 4, shard // 2 % 2, shard % 2
        for y in range(2):
            start = (shard * 2 + y) * half
            turned_ref[y, x, c, z * half : (z + 1) * half, :] = turned[start : start + half]


def backward_middle(canvas, source, inner_ref, hidden_ref, norm_ref, param_ref, mask_ref, *refs):
    *weights, grad_ref, stats_ref, buffer, weight, sem = refs
    valid = wide(mask_ref, hidden_ref.shape[1])
    fetch = Fetch(source, weights, weight, sem)
    convolve(canvas, inner_ref[...].astype(F32), fetch, buffer, grad_ref, -1)
    normed = (hidden_ref[...] - norm_ref[0:1, :]) * norm_ref[1:2, :]
    value = normed * param_ref[0:1, :] + param_ref[1:2, :]
    grad = grad_ref[...] * valid * swish_slope(value)
    grad_ref[...] = grad
    spread_rows([column_sum(grad), column_sum(grad * normed)], stats_ref)


def backward_input(canvas, source, inner_ref, residual_ref, mask_ref, *refs):
    *weights, grad_ref, buffer, weight, sem = refs
    fetch = Fetch(source, weights, weight, sem)
    convolve(canvas, inner_ref[...].astype(F32), fetch, buffer, grad_ref, -1)
    grad_ref[...] = residual_ref[...] + wide(mask_ref, grad_ref.shape[1]) * grad_ref[...]


def kernel_grad_whole(canvas, turned_ref, active_ref, out_ref, buffer):
    canvas.place(buffer, active_ref[0 : canvas.rows, :].astype(F32))
    for tap in range(TAPS):
        product = multiply(turned_ref[...], canvas.shifted(buffer, tap, 1), 1, 0)
        out_ref[tap] = product.astype(out_ref.dtype)


def kernel_grad_layer(canvas, turned_hbm, *refs):
    active_hbm, (send_hbm, keep_hbm) = refs[:4], refs[4:6]
    turned_ref, active_ref, left, total, send_ref, keep_ref, sems = refs[6:]
    y, z, x, c = (lax.axis_index(name) for name in ("y", "z", "x", "c"))
    rows, part = canvas.rows, turned_ref.shape[3]
    half = part // 4
    copies = [pltpu.make_async_copy(turned_hbm, turned_ref, sems.at[4])]
    for index, hbm in enumerate(active_hbm):
        target = active_ref.at[index, pl.ds(0, hbm.shape[0])]
        copies.append(pltpu.make_async_copy(hbm, target, sems.at[index]))
    for copy in copies:
        copy.start()
    copies.pop(0).wait()
    stores = []
    for core, ref, hbm in ((1, send_ref, send_hbm), (0, keep_ref, keep_hbm)):
        for index in range(4):
            slot = index % 2
            turned = turned_ref[y ^ (index // 2), x ^ (index % 2), c ^ core].astype(F32)
            for tap in range(TAPS):
                shift = canvas.shift(tap) % canvas.lanes
                moved = pltpu.roll(turned, shift, 1) if shift else turned
                left[slot, tap * part : (tap + 1) * part, :] = moved[:, :rows].astype(BF16)
            if core:
                copies[index].wait()
            product = multiply(left[slot], active_ref[index, 0:rows, :], 1, 0)
            total[...] = product if index == 0 else total[...] + product
        for tap in range(TAPS):
            for place in range(4):
                row = tap * part + (z ^ place) * half
                ref[place, tap] = total[pl.ds(row, half), :].astype(ref.dtype)
        stores.append(pltpu.make_async_copy(ref, hbm, sems.at[5 + core]))
        stores[-1].start()
    for store in stores:
        store.wait()


def call(body, inputs, outputs, scratch=(), weights=(), after=(), scalars=(), kept=()):
    whole = pl.BlockSpec(memory_space=pltpu.VMEM)
    anywhere = pl.BlockSpec(memory_space=pltpu.HBM)
    read = len(inputs) + len(scalars) + len(weights)

    def kernel(*refs):
        body(*refs[:read], *refs[read + len(after) :])

    return pl.pallas_call(
        kernel,
        out_shape=[jax.ShapeDtypeStruct(shape, dtype) for shape, dtype in (*outputs, *kept)],
        in_specs=[whole] * len(inputs)
        + [pl.BlockSpec(memory_space=pltpu.SMEM)] * len(scalars)
        + [anywhere] * (len(weights) + len(after)),
        out_specs=[whole] * len(outputs) + [anywhere] * len(kept),
        scratch_shapes=list(scratch),
        compiler_params=pltpu.CompilerParams(vmem_limit_bytes=VMEM_BYTES),
    )(*inputs, *scalars, *weights, *after)


def adamw(param, grad, first, second, rate, decay):
    first_new = BETA_ONE * first + (1.0 - BETA_ONE) * grad
    second_new = BETA_TWO * second + (1.0 - BETA_TWO) * grad * grad
    first_hat = first_new / (1.0 - BETA_ONE**STEP)
    second_hat = second_new / (1.0 - BETA_TWO**STEP)
    update = first_hat / (jnp.sqrt(second_hat) + ADAM_EPS)
    return (param - rate * (update + decay * param), first_new, second_new)


def flip(value, axis, bit, size):
    return lax.ppermute(value, axis, [(place, place ^ bit) for place in range(size)])


def behind(value, others):
    return lax.optimization_barrier((value, *others))[0] if others else value


class Gather:
    def __init__(self, shard, half):
        self.shard, self.half = shard[None], half[None]

    def along_two(self, *others):
        self.second = flip(behind(self.half, others), "z", 2, 4)

    def beside(self, *others):
        self.nearest = flip(behind(self.shard, others), "x", 1, 2)

    def along_one(self, *others):
        both = jnp.concatenate([self.half, self.second], axis=0)
        self.line = flip(behind(both, others), "z", 1, 4)

    def across(self, *others):
        self.rest = jnp.concatenate([self.second, self.line], axis=0)
        rest = behind(self.rest, others)
        self.over = flip(rest, "x", 1, 2), flip(rest, "y", 1, 2)

    def corner(self, *others):
        rows = self.shard.shape[2] // 2
        over_x, over_y = self.over
        self.corners = (
            flip(behind(over_y[:, :, :rows], others), "x", 1, 2),
            flip(behind(over_x[:, :, rows:], others), "y", 1, 2),
        )

    def cores(self, early=(), late=()):
        rows = self.shard.shape[2] // 2
        deep = (2, 1, 3)
        pieces = [
            (self.shard, [(None, 0, 0)], 0),
            (self.nearest, [(None, 0, 1)], 0),
            (self.rest, [(0, dz, 0) for dz in deep], 0),
            (self.over[0], [(0, dz, 1) for dz in deep], 0),
            (self.over[1], [(1, dz, 0) for dz in deep], 0),
            (self.corners[0], [(1, dz, 1) for dz in deep], 0),
            (self.corners[1], [(1, dz, 1) for dz in deep], rows),
        ]
        self.found = []
        for index, (array, slots, first) in enumerate(pieces):
            others = late if index > 4 else early if index > 2 else ()
            other = flip(behind(array, others), "c", 1, 2)
            self.found.append((array, [slot + (0,) for slot in slots], first))
            self.found.append((other, [slot + (1,) for slot in slots], first))


class Grid:
    axes = ("y", "z", "x", "c")
    shard_axes = ("z", "x", "c")

    def weights(self, low, x, back):
        half = low.shape[3] // 2
        first, second = lax.dynamic_slice_in_dim(low, lax.axis_index("y") * half, half, 3)
        one, two = Gather(low[0], first), Gather(low[1], second)
        one.along_two()
        one.beside()
        self.pixels = x
        self.sides = flip(x, "x", 1, 2), flip(x, "y", 1, 2)
        one.along_one(x, one.nearest)
        two.along_two(one.line)
        one.across(back, *self.sides)
        two.along_one(*one.over)
        one.corner()
        one.cores()
        two.beside(*one.corners)
        two.across(*one.corners)
        self.second = two
        return Pieces(one.found)

    def second_weights(self, stats, gathered, *others):
        self.second.corner(stats)
        self.second.cores((stats,), (gathered, *others))
        turn = [(place, place ^ 3) for place in range(4)]
        self.corners = (lax.ppermute(behind(self.pixels, (gathered, *others)), ("y", "x"), turn),)
        return Pieces(self.second.found)

    def turned_shape(self, canvas, channels):
        return ((2, 2, 2, channels // 8, canvas.lanes), BF16)

    def send(self, turned):
        shape = turned.shape
        moved = lax.all_to_all(turned.reshape(4, *shape[2:]), ("y", "x"), 0, 0, tiled=True)
        return moved.reshape(shape)

    def chip_sum(self, canvas, moved, layer, channels, after):
        out = (4, TAPS, channels // 32, channels)
        part = moved.shape[3]
        send, keep = call(
            functools.partial(kernel_grad_layer, canvas),
            (),
            (),
            (
                pltpu.VMEM(moved.shape, BF16),
                pltpu.VMEM((4, canvas.sent_rows, channels), BF16),
                pltpu.VMEM((2, TAPS * part, canvas.rows), BF16),
                pltpu.VMEM((TAPS * part, channels), F32),
                pltpu.VMEM(out, BF16),
                pltpu.VMEM(out, F32),
                pltpu.SemaphoreType.DMA((7,)),
            ),
            (moved, *layer),
            after,
            kept=((out, BF16), (out, F32)),
        )
        return send, keep

    def core_sum(self, chip, *others):
        send, keep = chip
        chip = keep + flip(behind(send, others), "c", 1, 2).astype(F32)
        return chip[0], *[chip[place].astype(BF16) for place in range(1, 4)]

    def line_sum(self, parts, *others):
        own, *rest = parts
        found = [flip(part, "z", place, 4) for place, part in enumerate(rest, 1)]
        total = behind(own, others)
        for part in found:
            total = total + part.astype(F32)
        return total

    def owned(self, line):
        own = line.astype(BF16)
        other = flip(own, "y", 1, 2)
        first = lax.axis_index("y") == 0
        halves = [jnp.where(first, own, other), jnp.where(first, other, own)]
        return jnp.concatenate(halves, axis=1).astype(F32)


class Plain:
    axes = ("dp", "fsdp")
    shard_axes = ("fsdp",)

    sides = corners = ()

    def weights(self, low, x, back):
        full = lax.all_gather(low, "fsdp", axis=2, tiled=True)
        first, self.second = [Whole(array, low.shape[2]) for array in full]
        return first

    def second_weights(self, stats, gathered, *others):
        return self.second

    def turned_shape(self, canvas, channels):
        return ((channels, canvas.rows), BF16)

    def send(self, turned):
        return turned

    def chip_sum(self, canvas, turned, layer, channels, after):
        (full,) = call(
            functools.partial(kernel_grad_whole, canvas),
            (turned, layer[0]),
            (((TAPS, channels, channels), BF16),),
            (pltpu.VMEM((canvas.padded_rows, channels), F32),),
            after=after,
        )
        return (full,)

    def core_sum(self, chip, *others):
        return chip

    def line_sum(self, parts, *others):
        return lax.psum_scatter(parts[0], "fsdp", scatter_dimension=1, tiled=True)

    def owned(self, line):
        return lax.psum(line, "dp").astype(F32)


def local(
    ways,
    sizes,
    field_five,
    field_seven,
    field_nine,
    mask_five,
    mask_seven,
    mask_nine,
    back_five,
    back_seven,
    back_nine,
    kernels,
    norm_params,
    kernel_first,
    kernel_second,
    norm_first,
    norm_second,
):
    copies, shards = sizes
    fields = (field_five, field_seven, field_nine)
    masks = (mask_five, mask_seven, mask_nine)
    backs = (back_five, back_seven, back_nine)
    channels = field_five.shape[3]
    width = kernels.shape[4]
    canvas = Canvas([(field.shape[0], field.shape[1]) for field in fields])
    rows = canvas.rows
    count = copies * shards

    def turned(kernel):
        return jnp.transpose(kernel, (0, 1, 2, 4, 3)).reshape(2, TAPS, width, channels)

    def exchange(spread):
        return lax.all_to_all(spread, ways.axes, 0, 0, tiled=True)

    kernels_turned = turned(kernels)
    low = kernels_turned.astype(BF16)

    buffer = pltpu.VMEM((rows, channels), F32)
    weighted = (
        pltpu.VMEM((canvas.padded_rows, channels), F32),
        pltpu.VMEM((TAPS, channels, channels), BF16),
        pltpu.SemaphoreType.DMA((3,)),
    )
    flat32 = ((rows, channels), F32)
    flat16 = ((rows, channels), BF16)
    two = ((count, 2, channels), F32)
    norm = ((4, channels), F32)
    sums = ((2, channels), F32)
    turned_shape = ways.turned_shape(canvas, channels)

    full = ((TAPS, channels, channels), BF16)

    def conv_call(body, source, inputs, outputs, after=(), kept=()):
        return call(
            functools.partial(body, canvas, source),
            inputs,
            outputs,
            weighted,
            source.arrays,
            after,
            kept=kept,
        )

    x, mask, info = call(
        functools.partial(prepare, canvas),
        (*[jnp.transpose(field, (1, 2, 0, 3)) for field in fields], norm_params),
        (((canvas.sent_rows, channels), BF16), ((rows, LANES), F32), ((2, LANES), F32)),
        (buffer,),
        scalars=[jnp.transpose(mask, (1, 0, 2)) for mask in masks],
    )
    (back,) = call(
        functools.partial(prepare_back, canvas),
        [jnp.transpose(field, (1, 2, 0, 3)) for field in backs],
        (flat16,),
        (buffer,),
    )
    weight_one = ways.weights(low, x, back)
    sides = ways.sides
    hidden, stats = conv_call(
        forward_one,
        weight_one,
        (x, mask, info),
        (flat32, ((count, 2, channels + LANES), F32)),
        after=sides,
    )
    gathered = exchange(stats)
    sent_image = pltpu.VMEM((canvas.sent_rows, channels), BF16)
    side = ()
    if sides:
        *side, full_one = call(
            functools.partial(side_hidden, canvas, weight_one),
            (),
            (flat32,),
            (*weighted, sent_image, pltpu.SemaphoreType.DMA),
            (*weight_one.arrays, sides[1]),
            (stats,),
            kept=(full,),
        )
        weight_one = Whole(full_one, weight_one.width)
    weight_two = ways.second_weights(stats, gathered, *side)
    active, second, norm_one, params, counts, stats = conv_call(
        forward_two,
        weight_two,
        (hidden, gathered, mask),
        (flat16, flat32, norm, norm, ((count, channels), F32), two),
        after=side,
    )
    gathered = exchange(stats)
    actives = (active,)

    def side_call(known, sent, after):
        return call(
            functools.partial(side_active, canvas, weight_one, len(known)),
            (norm_one, params, *known),
            (flat16,) * (1 + len(known)),
            (
                *weighted,
                pltpu.VMEM((rows, channels), F32),
                sent_image,
                pltpu.VMEM((16, channels), BF16),
                pltpu.SemaphoreType.DMA((2,)),
            ),
            (*weight_one.arrays, *sent),
            after,
        )

    if sides:
        actives += tuple(side_call(side, sides, (stats,)))
    result, grad_sum, norm_two, stats = call(
        turn,
        (second, gathered, counts, params, mask, x, back),
        (flat16, flat32, norm, two),
        after=actives[1:],
    )
    gathered = exchange(stats)
    if sides:
        actives += tuple(side_call((), ways.corners, (stats,)))
    inner_two, sums_two, turned_two = call(
        functools.partial(norm_back, 2),
        (grad_sum, second, norm_two, gathered, params, mask),
        (flat16, sums, turned_shape),
        after=actives[3:],
    )
    moved_two = ways.send(turned_two)
    grad_hidden, stats = conv_call(
        backward_middle, weight_two, (inner_two, hidden, norm_one, params, mask), (flat32, two)
    )
    gathered = exchange(stats)
    chip_two = ways.chip_sum(canvas, moved_two, actives, channels, (grad_hidden,))
    layer_x = (x, *sides, *ways.corners)
    inner_one, sums_one, turned_one = call(
        functools.partial(norm_back, 0),
        (grad_hidden, hidden, norm_one, gathered, params, mask),
        (flat16, sums, turned_shape),
        after=chip_two,
    )
    moved_one = ways.send(turned_one)
    core_two = ways.core_sum(chip_two, gathered)
    line_two = ways.line_sum(core_two)
    chip_one = ways.chip_sum(canvas, moved_one, layer_x, channels, core_two[1:])
    core_one = ways.core_sum(chip_one, line_two)
    (grad_input,) = conv_call(
        backward_input, weight_one, (inner_one, grad_sum, mask), (flat32,), after=core_one
    )
    owned_two = ways.owned(line_two)
    owned_one = ways.owned(ways.line_sum(core_one, grad_input))

    results = adamw(
        kernels_turned,
        jnp.stack([owned_one, owned_two]),
        turned(kernel_first),
        turned(kernel_second),
        KERNEL_RATE,
        KERNEL_DECAY,
    )
    kernel_results = [
        jnp.transpose(value.reshape(2, 3, 3, width, channels), (0, 1, 2, 4, 3))
        for value in results
    ]
    norm_full = jnp.concatenate([sums_one, sums_two], axis=0)
    place = lax.axis_index(ways.shard_axes) * width
    norm_grads = lax.dynamic_slice_in_dim(norm_full, place, width, 1)
    norm_results = adamw(norm_params, norm_grads, norm_first, norm_second, NORM_RATE, 0.0)
    return (
        *canvas.unflatten(result),
        *canvas.unflatten(grad_input),
        *kernel_results,
        *norm_results,
    )


def solution(mesh):
    sizes = (mesh.shape["dp"], mesh.shape["fsdp"])
    if sizes == (2, 16):
        ways = Grid()
        mesh = Mesh(mesh.devices.reshape(2, 4, 2, 2), ways.axes)
    else:
        ways = Plain()
    images = P(ways.axes, None, None, None)
    maps = P(ways.axes, None, None)
    weights = P(None, None, None, None, ways.shard_axes)
    norms = P(None, ways.shard_axes)
    in_specs = (
        (images,) * 3 + (maps,) * 3 + (images,) * 3 + (weights, norms, weights, weights, norms, norms)
    )
    out_specs = (images,) * 6 + (weights,) * 3 + (norms,) * 3
    body = functools.partial(local, ways, sizes)
    return jax.shard_map(body, mesh=mesh, in_specs=in_specs, out_specs=out_specs, check_vma=False)
```

```python
import functools

import jax
import jax.numpy as jnp
from jax import lax
from jax.experimental import pallas as pl
from jax.experimental.pallas import tpu as pltpu
from jax.sharding import Mesh, PartitionSpec as P

STEP = 5
NORM_EPS = 1e-05
BETA_ONE = 0.5
BETA_TWO = 0.5
KERNEL_RATE = 0.03
NORM_RATE = 0.4
KERNEL_DECAY = 0.01
ADAM_EPS = 1e-08
TAPS = 9
LANES = 128
CELL = 2
VMEM_BYTES = 53 * 1024 * 1024
F32, BF16 = jnp.float32, jnp.bfloat16


def round_up(value, step):
    return (value + step - 1) // step * step


class Canvas:
    def __init__(self, shapes):
        self.shapes = shapes
        cells = [
            (side, group, first)
            for group, (count, side) in enumerate(shapes)
            for first in range(0, count, CELL)
        ]
        limit = max(
            sum(side + 1 for side, group, _ in cells if group == wanted)
            for wanted in range(len(shapes))
        )
        self.bands = []
        for side, group, first in sorted(cells, reverse=True):
            used = sum(cell[0] + 1 for cell in self.bands[-1]) if self.bands else limit
            if used + side + 1 > limit:
                self.bands.append([])
            self.bands[-1].append((side, group, first))
        self.width = limit
        self.right = CELL
        self.down = limit * CELL
        self.heights = [band[0][0] for band in self.bands]
        used_rows = (sum(self.heights) + len(self.bands) - 1) * self.down
        self.rows = round_up(used_rows, 16)
        self.halo = round_up(self.down + self.right, 8)
        self.lanes = round_up(self.rows + self.down + self.right, LANES)
        self.padded_rows = self.rows + 2 * self.halo
        self.sent_rows = self.rows + 16

    def cells(self):
        start = 0
        for band, height in zip(self.bands, self.heights):
            column = 0
            for side, group, first in band:
                yield side, group, first, start * self.down + column * CELL
                column += side + 1
            start += height + 1

    def shift(self, tap):
        return (tap // 3 - 1) * self.down + (tap % 3 - 1) * self.right

    def place(self, buffer, value):
        edge = jnp.zeros((self.halo, value.shape[1]), F32)
        buffer[0 : self.halo, :] = edge
        buffer[self.halo : self.halo + self.rows, :] = value
        buffer[self.halo + self.rows :, :] = edge

    def shifted(self, buffer, tap, sign):
        start = self.halo + sign * self.shift(tap)
        return buffer[start : start + self.rows, :].astype(BF16)


def wide(mask_ref, channels):
    return jnp.concatenate([mask_ref[...]] * (channels // LANES), axis=1)


def multiply(left, right, left_dim, right_dim):
    return lax.dot_general(
        left, right, (((left_dim,), (right_dim,)), ((), ())), preferred_element_type=F32
    )


def column_sum(value):
    return jnp.sum(value, axis=0, keepdims=True)


def spread_rows(rows, ref):
    ref[...] = jnp.broadcast_to(jnp.concatenate(rows, axis=0)[None], ref.shape)


def local_statistics(hidden, valid, *refs):
    total = column_sum(hidden * valid)
    centre = total / jnp.maximum(column_sum(valid), 1.0)
    squares = column_sum(jnp.square(hidden - centre) * valid)
    rows = jnp.concatenate([total, squares], axis=0)
    *info, ref = [ref[...] for ref in refs[:-1]] + [refs[-1]]
    rows = jnp.concatenate([rows, *info], axis=1)
    ref[...] = jnp.broadcast_to(rows[None], ref.shape)


def global_statistics(gathered, counts):
    channels = counts.shape[1]
    totals, squares = gathered[:, 0, :channels], gathered[:, 1, :channels]
    total = column_sum(counts)
    centre = column_sum(totals) / total
    between = column_sum(counts * jnp.square(totals / jnp.maximum(counts, 1.0) - centre))
    spread = (column_sum(squares) + between) / total
    return centre, lax.rsqrt(spread + NORM_EPS), total


def lay_out(canvas, field_refs, buffer):
    buffer[...] = jnp.zeros_like(buffer)
    for side, group, first, start in canvas.cells():
        for down in range(side):
            for right in range(side):
                row = start + down * canvas.down + right * CELL
                pair = field_refs[group][down, right, first : first + CELL, :]
                buffer[row : row + CELL, :] = pair.astype(F32)


def prepare(canvas, *refs):
    *field_refs, param_ref = refs[:4]
    mask_refs = refs[4:7]
    x_ref, mask_ref, info_ref, buffer = refs[7:]
    rows, channels = buffer.shape
    mask_ref[...] = jnp.zeros_like(mask_ref)
    for side, group, first, start in canvas.cells():
        for down in range(side):
            for right in range(side):
                for image in range(CELL):
                    row = start + down * canvas.down + right * CELL + image
                    value = mask_refs[group][down, first + image, right].astype(F32)
                    mask_ref[row : row + 1, :] = jnp.full((1, LANES), value, F32)
    lay_out(canvas, field_refs, buffer)
    x_ref[0:rows, :] = (buffer[...] * wide(mask_ref, channels)).astype(BF16)
    line = jnp.transpose(mask_ref[...])[0:1]
    rest = jnp.zeros((1, channels * 2 - rows), F32)
    lines = [line[:, :channels], jnp.concatenate([line[:, channels:], rest], axis=1)]
    lines.append(jnp.zeros((14, channels), F32))
    x_ref[rows:, :] = jnp.concatenate(lines, axis=0).astype(BF16)
    params = param_ref[...].astype(BF16).astype(F32)
    rows = [params[index : index + 1] for index in range(4)]
    if params.size < LANES:
        rows.append(jnp.zeros((1, LANES - params.size), F32))
    row = jnp.concatenate(rows, axis=1)
    info_ref[...] = jnp.concatenate([row, column_sum(mask_ref[...])], axis=0)


def sent_mask(canvas, lines):
    channels = lines.shape[1]
    turned = jnp.transpose(lines)
    column = jnp.concatenate([turned[:, 0:1], turned[: canvas.rows - channels, 1:2]], axis=0)
    return jnp.broadcast_to(column, (canvas.rows, channels))


def prepare_back(canvas, *refs):
    *field_refs, back_ref, buffer = refs
    lay_out(canvas, field_refs, buffer)
    back_ref[...] = buffer[...].astype(BF16)


def sigmoid(value):
    return 1.0 / (1.0 + jnp.exp(-value))


def swish_slope(value):
    logistic = sigmoid(value)
    return logistic * (1.0 + value * (1.0 - logistic))


class Whole:
    def __init__(self, array, width):
        self.arrays = self.last = [array]
        self.width = width

    @staticmethod
    def start(refs, weight, sems):
        for part in range(3):
            taps = pl.ds(3 * part, 3)
            pltpu.make_async_copy(refs[0].at[taps], weight.at[taps], sems.at[part]).start()


class Pieces:
    width = 32

    def __init__(self, pieces):
        self.arrays = [array for array, _, _ in pieces]
        self.last = self.arrays[-4:]
        self.places = [(slots, first) for _, slots, first in pieces]

    def start(self, refs, weight, sems):
        y, z, x, c = (lax.axis_index(name) for name in ("y", "z", "x", "c"))
        moves = []
        for ref, (slots, first) in zip(refs, self.places):
            _, _, rows, lanes = ref.shape
            for slot, (dy, dz, dx, dc) in enumerate(slots):
                shard = ((z ^ dz) * 2 + (x ^ dx)) * 2 + (c ^ dc)
                row = pl.multiple_of(shard * self.width + first, 16)
                lane = 0 if dy is None else pl.multiple_of((y ^ dy) * lanes, lanes)
                moves.append((ref.at[slot], pl.ds(row, rows), pl.ds(lane, lanes)))
        for part in range(3):
            taps = pl.ds(3 * part, 3)
            for source, row, lane in moves:
                target = weight.at[taps, row, lane]
                pltpu.make_async_copy(source.at[taps], target, sems.at[part]).start()


class Fetch:
    def __init__(self, source, refs, weight, sems, target=None):
        self.weight, self.sems, self.target = weight, sems, target
        self.waiting = [0, 1, 2]
        source.start(refs, weight, sems)

    def ready(self, tap):
        if tap % 3 == 0 and self.waiting:
            part = self.waiting.pop(0)
            taps = self.weight.at[pl.ds(3 * part, 3)]
            pltpu.make_async_copy(taps, taps, self.sems.at[part]).wait()
            if not self.waiting and self.target is not None:
                self.store = pltpu.make_async_copy(self.weight, self.target, self.sems.at[0])
                self.store.start()


def convolve(canvas, value, fetch, buffer, out_ref, sign):
    canvas.place(buffer, value)
    for tap in range(TAPS):
        part = canvas.shifted(buffer, tap, sign)
        fetch.ready(tap)
        product = multiply(part, fetch.weight[tap], 1, 1 if sign > 0 else 0)
        out_ref[...] = product if tap == 0 else out_ref[...] + product


def activate(hidden, norm_ref, param_ref, valid):
    normed = (hidden - norm_ref[0:1, :]) * norm_ref[1:2, :]
    value = normed * param_ref[0:1, :] + param_ref[1:2, :]
    return value * sigmoid(value) * valid


def side_hidden(canvas, source, *refs):
    *weights, sent_hbm, hidden_ref, full_ref, buffer, weight, sems, sent, sent_sem = refs
    copy = pltpu.make_async_copy(sent_hbm, sent, sent_sem)
    copy.start()
    fetch = Fetch(source, weights, weight, sems, full_ref)
    copy.wait()
    convolve(canvas, sent[0 : canvas.rows, :].astype(F32), fetch, buffer, hidden_ref, 1)
    fetch.store.wait()


def side_active(canvas, source, known, *refs):
    norm_ref, param_ref, *refs = refs
    hidden_refs, refs = refs[:known], refs[known:]
    weights, refs = refs[: len(source.arrays)], refs[len(source.arrays) :]
    sent_hbm, refs = refs[: 1 + known], refs[1 + known :]
    active_refs, refs = refs[: 1 + known], refs[1 + known :]
    buffer, weight, sems, hidden, sent, lines, sent_sems = refs
    copies = [pltpu.make_async_copy(sent_hbm[0], sent, sent_sems.at[0])]
    for other in sent_hbm[1:]:
        tail = other.at[pl.ds(canvas.rows, 16)]
        copies.append(pltpu.make_async_copy(tail, lines, sent_sems.at[1]))
    for copy in copies:
        copy.start()
    fetch = Fetch(source, weights, weight, sems)
    for hidden_ref, active_ref in zip(hidden_refs, active_refs[1:]):
        copies[1].wait()
        valid = sent_mask(canvas, lines[...].astype(F32))
        active_ref[...] = activate(hidden_ref[...], norm_ref, param_ref, valid).astype(BF16)
    copies[0].wait()
    convolve(canvas, sent[0 : canvas.rows, :].astype(F32), fetch, buffer, hidden, 1)
    valid = sent_mask(canvas, sent[canvas.rows :, :].astype(F32))
    active_refs[0][...] = activate(hidden[...], norm_ref, param_ref, valid).astype(BF16)


def forward_one(canvas, source, x_ref, mask_ref, info_ref, *refs):
    *weights, hidden_ref, stats_ref, buffer, weight, sem = refs
    fetch = Fetch(source, weights, weight, sem)
    convolve(canvas, x_ref[0 : canvas.rows, :].astype(F32), fetch, buffer, hidden_ref, 1)
    local_statistics(hidden_ref[...], wide(mask_ref, x_ref.shape[1]), info_ref, stats_ref)


def forward_two(canvas, source, hidden_ref, gathered_ref, mask_ref, *refs):
    *weights, active_ref, second_ref, norm_ref, param_ref, count_ref, stats_ref = refs[:-3]
    buffer, weight, sem = refs[-3:]
    fetch = Fetch(source, weights, weight, sem)
    channels = hidden_ref.shape[1]
    valid = wide(mask_ref, channels)
    width = source.width
    rows = []
    for index in range(4):
        start = channels + index * width
        rows.append(
            jnp.concatenate(
                [gathered_ref[shard, 0:1, start : start + width] for shard in range(channels // width)],
                axis=1,
            )
        )
    param_ref[...] = jnp.concatenate(rows, axis=0)
    counts = gathered_ref[:, 1, channels : channels + LANES]
    count_ref[...] = jnp.concatenate([counts] * (channels // LANES), axis=1)

    centre, inv, total = global_statistics(gathered_ref, count_ref[...])
    norm_ref[...] = jnp.concatenate([centre, inv, total, total], axis=0)
    value = activate(hidden_ref[...], norm_ref, param_ref, valid)
    active_ref[...] = value.astype(BF16)
    convolve(canvas, value, fetch, buffer, second_ref, 1)
    local_statistics(second_ref[...], valid, stats_ref)


def turn(
    second_ref,
    gathered_ref,
    count_ref,
    param_ref,
    mask_ref,
    x_ref,
    back_ref,
    result_ref,
    grad_ref,
    norm_ref,
    stats_ref,
):
    valid = wide(mask_ref, second_ref.shape[1])
    centre, inv, total = global_statistics(gathered_ref, count_ref[...])
    norm_ref[...] = jnp.concatenate([centre, inv, total, total], axis=0)
    normed = (second_ref[...] - centre) * inv
    rows = second_ref.shape[0]
    summed = normed * param_ref[2:3, :] + param_ref[3:4, :] + x_ref[0:rows, :].astype(F32)
    logistic = sigmoid(summed)
    result_ref[...] = (summed * logistic * valid).astype(BF16)
    slope = logistic * (1.0 + summed * (1.0 - logistic))
    grad = back_ref[...].astype(F32) * valid * slope
    grad_ref[...] = grad
    spread_rows([column_sum(grad), column_sum(grad * normed)], stats_ref)


def norm_back(
    row,
    grad_ref,
    hidden_ref,
    norm_ref,
    gathered_ref,
    param_ref,
    mask_ref,
    inner_ref,
    sums_ref,
    *turned_refs,
):
    valid = wide(mask_ref, grad_ref.shape[1])
    shift_grad = column_sum(gathered_ref[:, 0, :])
    gain_grad = column_sum(gathered_ref[:, 1, :])
    sums_ref[...] = jnp.concatenate([gain_grad, shift_grad], axis=0)
    centre, inv, total = norm_ref[0:1, :], norm_ref[1:2, :], norm_ref[2:3, :]
    normed = (hidden_ref[...] - centre) * inv
    grad = grad_ref[...] - shift_grad / total - normed * (gain_grad / total)
    inner = valid * (param_ref[row : row + 1, :] * inv) * grad
    inner_ref[...] = inner.astype(BF16)
    turned = jnp.transpose(inner).astype(BF16)
    if len(turned_refs) == 1:
        turned_refs[0][...] = turned
        return
    rows, channels = inner.shape
    *turned_refs, full = turned_refs
    full[:, 0:rows] = turned
    full[:, rows:] = jnp.zeros((channels, full.shape[1] - rows), BF16)
    y, x = lax.axis_index("y"), lax.axis_index("x")
    half = channels // 32
    for index, turned_ref in enumerate(turned_refs):
        for c in range(2):
            for z in range(4):
                shard = (z * 2 + (x ^ (index % 2))) * 2 + c
                start = pl.multiple_of((shard * 2 + (y ^ (index // 2))) * half, half)
                turned_ref[c, z * half : (z + 1) * half, :] = full[pl.ds(start, half), :]


def backward_middle(canvas, source, inner_ref, hidden_ref, norm_ref, param_ref, mask_ref, *refs):
    *weights, grad_ref, stats_ref, buffer, weight, sem = refs
    valid = wide(mask_ref, hidden_ref.shape[1])
    fetch = Fetch(source, weights, weight, sem)
    convolve(canvas, inner_ref[...].astype(F32), fetch, buffer, grad_ref, -1)
    normed = (hidden_ref[...] - norm_ref[0:1, :]) * norm_ref[1:2, :]
    value = normed * param_ref[0:1, :] + param_ref[1:2, :]
    grad = grad_ref[...] * valid * swish_slope(value)
    grad_ref[...] = grad
    spread_rows([column_sum(grad), column_sum(grad * normed)], stats_ref)


def lay_back(canvas, flat, refs):
    for side, group, first, start in canvas.cells():
        for down in range(side):
            for right in range(side):
                row = start + down * canvas.down + right * CELL
                pair = flat[row : row + CELL, :].astype(refs[group].dtype)
                refs[group][down, right, first : first + CELL, :] = pair


def backward_input(canvas, source, inner_ref, residual_ref, mask_ref, result_ref, *refs):
    weights, refs = refs[: len(source.arrays)], refs[len(source.arrays) :]
    result_refs, grad_refs, (buffer, weight, sem, flat) = refs[:3], refs[3:6], refs[6:]
    fetch = Fetch(source, weights, weight, sem)
    convolve(canvas, inner_ref[...].astype(F32), fetch, buffer, flat, -1)
    flat[...] = residual_ref[...] + wide(mask_ref, flat.shape[1]) * flat[...]
    lay_back(canvas, flat, grad_refs)
    flat[...] = result_ref[...].astype(F32)
    lay_back(canvas, flat, result_refs)


def kernel_grad_whole(canvas, turned_ref, active_ref, out_ref, buffer):
    canvas.place(buffer, active_ref[0 : canvas.rows, :].astype(F32))
    for tap in range(TAPS):
        product = multiply(turned_ref[...], canvas.shifted(buffer, tap, 1), 1, 0)
        out_ref[tap] = product.astype(out_ref.dtype)


def kernel_grad_layer(canvas, *refs):
    turned_hbm, active_hbm, (send_hbm, keep_hbm) = refs[:4], refs[4:8], refs[8:10]
    turned_ref, active_ref, left, total, send_ref, keep_ref, sems = refs[10:]
    z, c = lax.axis_index("z"), lax.axis_index("c")
    rows, part = canvas.rows, turned_ref.shape[2]
    half = part // 4
    turns, copies = [], []
    for index, hbm in enumerate(turned_hbm):
        turns.append(pltpu.make_async_copy(hbm, turned_ref.at[index], sems.at[index]))
    for index, hbm in enumerate(active_hbm):
        target = active_ref.at[index, pl.ds(0, hbm.shape[0])]
        copies.append(pltpu.make_async_copy(hbm, target, sems.at[4 + index]))
    for pair in zip(turns, copies):
        for copy in pair:
            copy.start()
    stores = []
    for core, ref, hbm in ((1, send_ref, send_hbm), (0, keep_ref, keep_hbm)):
        for index in range(4):
            slot = index % 2
            if core:
                turns[index].wait()
            turned = turned_ref[index, c ^ core].astype(F32)
            for tap in range(TAPS):
                shift = canvas.shift(tap) % canvas.lanes
                moved = pltpu.roll(turned, shift, 1) if shift else turned
                left[slot, tap * part : (tap + 1) * part, :] = moved[:, :rows].astype(BF16)
            if core:
                copies[index].wait()
            product = multiply(left[slot], active_ref[index, 0:rows, :], 1, 0)
            total[...] = product if index == 0 else total[...] + product
        for tap in range(TAPS):
            for place in range(4):
                row = tap * part + (z ^ place) * half
                ref[place, tap] = total[pl.ds(row, half), :].astype(ref.dtype)
        stores.append(pltpu.make_async_copy(ref, hbm, sems.at[8 + core]))
        stores[-1].start()
    for store in stores:
        store.wait()


def call(body, inputs, outputs, scratch=(), weights=(), after=(), scalars=(), kept=()):
    whole = pl.BlockSpec(memory_space=pltpu.VMEM)
    anywhere = pl.BlockSpec(memory_space=pltpu.HBM)
    read = len(inputs) + len(scalars) + len(weights)

    def kernel(*refs):
        body(*refs[:read], *refs[read + len(after) :])

    return pl.pallas_call(
        kernel,
        out_shape=[jax.ShapeDtypeStruct(shape, dtype) for shape, dtype in (*outputs, *kept)],
        in_specs=[whole] * len(inputs)
        + [pl.BlockSpec(memory_space=pltpu.SMEM)] * len(scalars)
        + [anywhere] * (len(weights) + len(after)),
        out_specs=[whole] * len(outputs) + [anywhere] * len(kept),
        scratch_shapes=list(scratch),
        compiler_params=pltpu.CompilerParams(vmem_limit_bytes=VMEM_BYTES),
    )(*inputs, *scalars, *weights, *after)


def adamw(param, grad, first, second, rate, decay):
    first_new = BETA_ONE * first + (1.0 - BETA_ONE) * grad
    second_new = BETA_TWO * second + (1.0 - BETA_TWO) * grad * grad
    first_hat = first_new / (1.0 - BETA_ONE**STEP)
    second_hat = second_new / (1.0 - BETA_TWO**STEP)
    update = first_hat / (jnp.sqrt(second_hat) + ADAM_EPS)
    return (param - rate * (update + decay * param), first_new, second_new)


def flip(value, axis, bit, size):
    return lax.ppermute(value, axis, [(place, place ^ bit) for place in range(size)])


def diagonal(value):
    return lax.ppermute(value, ("y", "x"), [(place, place ^ 3) for place in range(4)])


def behind(value, others):
    return lax.optimization_barrier((value, *others))[0] if others else value


class Gather:
    def __init__(self, shard, half):
        self.shard, self.half = shard[None], half[None]

    def along_two(self, *others):
        self.second = flip(behind(self.half, others), "z", 2, 4)

    def beside(self, *others):
        self.nearest = flip(behind(self.shard, others), "x", 1, 2)

    def along_one(self, *others):
        both = jnp.concatenate([self.half, self.second], axis=0)
        self.line = flip(behind(both, others), "z", 1, 4)

    def across(self, *others):
        self.rest = jnp.concatenate([self.second, self.line], axis=0)
        rest = behind(self.rest, others)
        self.over = flip(rest, "x", 1, 2), flip(rest, "y", 1, 2)

    def corner(self, *others):
        rows = self.shard.shape[2] // 2
        over_x, over_y = self.over
        self.corners = (
            flip(behind(over_y[:, :, :rows], others), "x", 1, 2),
            flip(behind(over_x[:, :, rows:], others), "y", 1, 2),
        )

    def cores(self, early=(), late=()):
        rows = self.shard.shape[2] // 2
        deep = (2, 1, 3)
        pieces = [
            (self.shard, [(None, 0, 0)], 0),
            (self.nearest, [(None, 0, 1)], 0),
            (self.rest, [(0, dz, 0) for dz in deep], 0),
            (self.over[0], [(0, dz, 1) for dz in deep], 0),
            (self.over[1], [(1, dz, 0) for dz in deep], 0),
            (self.corners[0], [(1, dz, 1) for dz in deep], 0),
            (self.corners[1], [(1, dz, 1) for dz in deep], rows),
        ]
        self.found = []
        for index, (array, slots, first) in enumerate(pieces):
            others = late if index > 4 else early if index > 2 else ()
            other = flip(behind(array, others), "c", 1, 2)
            self.found.append((array, [slot + (0,) for slot in slots], first))
            self.found.append((other, [slot + (1,) for slot in slots], first))


class Grid:
    axes = ("y", "z", "x", "c")
    shard_axes = ("z", "x", "c")

    def weights(self, low, x, back):
        half = low.shape[3] // 2
        first, second = lax.dynamic_slice_in_dim(low, lax.axis_index("y") * half, half, 3)
        one, two = Gather(low[0], first), Gather(low[1], second)
        one.along_two()
        one.beside()
        self.pixels = x
        self.sides = flip(x, "x", 1, 2), flip(x, "y", 1, 2)
        one.along_one(x, one.nearest)
        two.along_two(one.line)
        one.across(back, *self.sides)
        two.along_one(*one.over)
        one.corner()
        one.cores()
        two.beside(*one.corners)
        two.across(*one.corners)
        self.second = two
        return Pieces(one.found)

    def second_weights(self, stats, gathered, *others):
        self.second.corner(stats)
        self.second.cores((stats,), (gathered, *others))
        self.corners = (diagonal(behind(self.pixels, self.second.corners)),)
        return Pieces(self.second.found)

    def turned_shapes(self, canvas, channels):
        return (((2, channels // 8, canvas.lanes), BF16),) * 4

    def turned_scratch(self, canvas, channels):
        return (pltpu.VMEM((channels, canvas.lanes), BF16),)

    def send(self, own, over_x, over_y, corner):
        return own, flip(over_x, "x", 1, 2), flip(over_y, "y", 1, 2), diagonal(corner)

    def chip_sum(self, canvas, moved, layer, channels, after):
        out = (4, TAPS, channels // 32, channels)
        part = moved[0].shape[1]
        send, keep = call(
            functools.partial(kernel_grad_layer, canvas),
            (),
            (),
            (
                pltpu.VMEM((4, *moved[0].shape), BF16),
                pltpu.VMEM((4, canvas.sent_rows, channels), BF16),
                pltpu.VMEM((2, TAPS * part, canvas.rows), BF16),
                pltpu.VMEM((TAPS * part, channels), F32),
                pltpu.VMEM(out, BF16),
                pltpu.VMEM(out, F32),
                pltpu.SemaphoreType.DMA((10,)),
            ),
            (*moved, *layer),
            after,
            kept=((out, BF16), (out, F32)),
        )
        return send, keep

    def core_sum(self, chip, *others):
        send, keep = chip
        chip = keep + flip(behind(send, others), "c", 1, 2).astype(F32)
        return chip[0], *[chip[place].astype(BF16) for place in range(1, 4)]

    def line(self, parts):
        return [flip(part, "z", place, 4) for place, part in enumerate(parts[1:], 1)]

    def line_sum(self, parts, found, *others):
        total = behind(parts[0], others)
        for part in found:
            total = total + part.astype(F32)
        return total

    def owned(self, line):
        own = line.astype(BF16)
        other = flip(own, "y", 1, 2)
        first = lax.axis_index("y") == 0
        halves = [jnp.where(first, own, other), jnp.where(first, other, own)]
        return jnp.concatenate(halves, axis=1).astype(F32)


class Plain:
    axes = ("dp", "fsdp")
    shard_axes = ("fsdp",)

    sides = corners = ()

    def weights(self, low, x, back):
        full = lax.all_gather(low, "fsdp", axis=2, tiled=True)
        first, self.second = [Whole(array, low.shape[2]) for array in full]
        return first

    def second_weights(self, stats, gathered, *others):
        return self.second

    def turned_shapes(self, canvas, channels):
        return (((channels, canvas.rows), BF16),)

    def turned_scratch(self, canvas, channels):
        return ()

    def send(self, turned):
        return (turned,)

    def chip_sum(self, canvas, moved, layer, channels, after):
        (full,) = call(
            functools.partial(kernel_grad_whole, canvas),
            (*moved, layer[0]),
            (((TAPS, channels, channels), BF16),),
            (pltpu.VMEM((canvas.padded_rows, channels), F32),),
            after=after,
        )
        return (full,)

    def core_sum(self, chip, *others):
        return chip

    def line(self, parts):
        return ()

    def line_sum(self, parts, found, *others):
        return lax.psum_scatter(parts[0], "fsdp", scatter_dimension=1, tiled=True)

    def owned(self, line):
        return lax.psum(line, "dp").astype(F32)


def local(
    ways,
    sizes,
    field_five,
    field_seven,
    field_nine,
    mask_five,
    mask_seven,
    mask_nine,
    back_five,
    back_seven,
    back_nine,
    kernels,
    norm_params,
    kernel_first,
    kernel_second,
    norm_first,
    norm_second,
):
    copies, shards = sizes
    fields = (field_five, field_seven, field_nine)
    masks = (mask_five, mask_seven, mask_nine)
    backs = (back_five, back_seven, back_nine)
    channels = field_five.shape[3]
    width = kernels.shape[4]
    canvas = Canvas([(field.shape[0], field.shape[1]) for field in fields])
    rows = canvas.rows
    count = copies * shards

    def turned(kernel):
        return jnp.transpose(kernel, (0, 1, 2, 4, 3)).reshape(2, TAPS, width, channels)

    def exchange(spread):
        return lax.all_to_all(spread, ways.axes, 0, 0, tiled=True)

    kernels_turned = turned(kernels)
    low = kernels_turned.astype(BF16)

    buffer = pltpu.VMEM((rows, channels), F32)
    weighted = (
        pltpu.VMEM((canvas.padded_rows, channels), F32),
        pltpu.VMEM((TAPS, channels, channels), BF16),
        pltpu.SemaphoreType.DMA((3,)),
    )
    flat32 = ((rows, channels), F32)
    flat16 = ((rows, channels), BF16)
    two = ((count, 2, channels), F32)
    norm = ((4, channels), F32)
    sums = ((2, channels), F32)
    turned_shapes = ways.turned_shapes(canvas, channels)
    turned_scratch = ways.turned_scratch(canvas, channels)

    full = ((TAPS, channels, channels), BF16)

    def conv_call(body, source, inputs, outputs, after=(), kept=()):
        return call(
            functools.partial(body, canvas, source),
            inputs,
            outputs,
            weighted,
            source.arrays,
            after,
            kept=kept,
        )

    x, mask, info = call(
        functools.partial(prepare, canvas),
        (*[jnp.transpose(field, (1, 2, 0, 3)) for field in fields], norm_params),
        (((canvas.sent_rows, channels), BF16), ((rows, LANES), F32), ((2, LANES), F32)),
        (buffer,),
        scalars=[jnp.transpose(mask, (1, 0, 2)) for mask in masks],
    )
    (back,) = call(
        functools.partial(prepare_back, canvas),
        [jnp.transpose(field, (1, 2, 0, 3)) for field in backs],
        (flat16,),
        (buffer,),
    )
    weight_one = ways.weights(low, x, back)
    sides = ways.sides
    hidden, stats = conv_call(
        forward_one,
        weight_one,
        (x, mask, info),
        (flat32, ((count, 2, channels + LANES), F32)),
        after=sides,
    )
    gathered = exchange(stats)
    sent_image = pltpu.VMEM((canvas.sent_rows, channels), BF16)
    side = ()
    if sides:
        *side, full_one = call(
            functools.partial(side_hidden, canvas, weight_one),
            (),
            (flat32,),
            (*weighted, sent_image, pltpu.SemaphoreType.DMA),
            (*weight_one.arrays, sides[1]),
            (stats,),
            kept=(full,),
        )
        weight_one = Whole(full_one, weight_one.width)
    weight_two = ways.second_weights(stats, gathered, *side)
    active, second, norm_one, params, counts, stats = conv_call(
        forward_two,
        weight_two,
        (hidden, gathered, mask),
        (flat16, flat32, norm, norm, ((count, channels), F32), two),
        after=side,
    )
    gathered = exchange(stats)
    actives = (active,)

    def side_call(known, sent, after):
        return call(
            functools.partial(side_active, canvas, weight_one, len(known)),
            (norm_one, params, *known),
            (flat16,) * (1 + len(known)),
            (
                *weighted,
                pltpu.VMEM((rows, channels), F32),
                sent_image,
                pltpu.VMEM((16, channels), BF16),
                pltpu.SemaphoreType.DMA((2,)),
            ),
            (*weight_one.arrays, *sent),
            after,
        )

    if sides:
        actives += tuple(side_call(side, sides, (stats,)))
    result, grad_sum, norm_two, stats = call(
        turn,
        (second, gathered, counts, params, mask, x, back),
        (flat16, flat32, norm, two),
        after=actives[1:],
    )
    gathered = exchange(stats)
    if sides:
        actives += tuple(side_call((), ways.corners, (stats,)))
    inner_two, sums_two, *turned_two = call(
        functools.partial(norm_back, 2),
        (grad_sum, second, norm_two, gathered, params, mask),
        (flat16, sums, *turned_shapes),
        turned_scratch,
        after=actives[3:],
    )
    moved_two = ways.send(*turned_two)
    grad_hidden, stats = conv_call(
        backward_middle, weight_two, (inner_two, hidden, norm_one, params, mask), (flat32, two)
    )
    gathered = exchange(behind(stats, moved_two[1:]))
    chip_two = ways.chip_sum(canvas, moved_two, actives, channels, (grad_hidden,))
    layer_x = (x, *sides, *ways.corners)
    inner_one, sums_one, *turned_one = call(
        functools.partial(norm_back, 0),
        (grad_hidden, hidden, norm_one, gathered, params, mask),
        (flat16, sums, *turned_shapes),
        turned_scratch,
        after=chip_two,
    )
    moved_one = ways.send(*turned_one)
    core_two = ways.core_sum(chip_two, gathered)
    line_two = ways.line(core_two)
    chip_one = ways.chip_sum(canvas, moved_one, layer_x, channels, core_two[1:])
    core_one = ways.core_sum(chip_one, *line_two)
    shapes = [(side, side, images, channels) for images, side in canvas.shapes]
    finished = call(
        functools.partial(backward_input, canvas, weight_one),
        (inner_one, grad_sum, mask, result),
        [(shape, BF16) for shape in shapes] + [(shape, F32) for shape in shapes],
        (*weighted, buffer),
        weight_one.arrays,
        core_one,
    )
    owned_two = ways.owned(ways.line_sum(core_two, line_two, finished[0]))
    owned_one = ways.owned(ways.line_sum(core_one, ways.line(core_one), finished[0]))

    results = adamw(
        kernels_turned,
        jnp.stack([owned_one, owned_two]),
        turned(kernel_first),
        turned(kernel_second),
        KERNEL_RATE,
        KERNEL_DECAY,
    )
    kernel_results = [
        jnp.transpose(value.reshape(2, 3, 3, width, channels), (0, 1, 2, 4, 3))
        for value in results
    ]
    norm_full = jnp.concatenate([behind(sums_one, finished[:1]), sums_two], axis=0)
    place = lax.axis_index(ways.shard_axes) * width
    norm_grads = lax.dynamic_slice_in_dim(norm_full, place, width, 1)
    norm_results = adamw(norm_params, norm_grads, norm_first, norm_second, NORM_RATE, 0.0)
    return (
        *[jnp.transpose(array, (2, 0, 1, 3)) for array in finished],
        *kernel_results,
        *norm_results,
    )


def solution(mesh):
    sizes = (mesh.shape["dp"], mesh.shape["fsdp"])
    if sizes == (2, 16):
        ways = Grid()
        mesh = Mesh(mesh.devices.reshape(2, 4, 2, 2), ways.axes)
    else:
        ways = Plain()
    images = P(ways.axes, None, None, None)
    maps = P(ways.axes, None, None)
    weights = P(None, None, None, None, ways.shard_axes)
    norms = P(None, ways.shard_axes)
    in_specs = (
        (images,) * 3 + (maps,) * 3 + (images,) * 3 + (weights, norms, weights, weights, norms, norms)
    )
    out_specs = (images,) * 6 + (weights,) * 3 + (norms,) * 3
    body = functools.partial(local, ways, sizes)
    return jax.shard_map(body, mesh=mesh, in_specs=in_specs, out_specs=out_specs, check_vma=False)
```

```python
import functools

import jax
import jax.numpy as jnp
from jax import lax
from jax.experimental import pallas as pl
from jax.experimental.pallas import tpu as pltpu
from jax.sharding import Mesh, PartitionSpec as P

STEP = 5
NORM_EPS = 1e-05
BETA_ONE = 0.5
BETA_TWO = 0.5
KERNEL_RATE = 0.03
NORM_RATE = 0.4
KERNEL_DECAY = 0.01
ADAM_EPS = 1e-08
TAPS = 9
LANES = 128
CELL = 2
VMEM_BYTES = 53 * 1024 * 1024
F32, BF16 = jnp.float32, jnp.bfloat16


def round_up(value, step):
    return (value + step - 1) // step * step


class Canvas:
    def __init__(self, shapes):
        self.shapes = shapes
        cells = [
            (side, group, first)
            for group, (count, side) in enumerate(shapes)
            for first in range(0, count, CELL)
        ]
        limit = max(
            sum(side + 1 for side, group, _ in cells if group == wanted)
            for wanted in range(len(shapes))
        )
        self.bands = []
        for side, group, first in sorted(cells, reverse=True):
            used = sum(cell[0] + 1 for cell in self.bands[-1]) if self.bands else limit
            if used + side + 1 > limit:
                self.bands.append([])
            self.bands[-1].append((side, group, first))
        self.width = limit
        self.right = CELL
        self.down = limit * CELL
        self.heights = [band[0][0] for band in self.bands]
        used_rows = (sum(self.heights) + len(self.bands) - 1) * self.down
        self.rows = round_up(used_rows, 16)
        self.halo = round_up(self.down + self.right, 8)
        self.lanes = round_up(self.rows + self.down + self.right, LANES)
        self.padded_rows = self.rows + 2 * self.halo
        self.sent_rows = self.rows + 16

    def cells(self):
        start = 0
        for band, height in zip(self.bands, self.heights):
            column = 0
            for side, group, first in band:
                yield side, group, first, start * self.down + column * CELL
                column += side + 1
            start += height + 1

    def shift(self, tap):
        return (tap // 3 - 1) * self.down + (tap % 3 - 1) * self.right

    def place(self, buffer, value):
        edge = jnp.zeros((self.halo, value.shape[1]), F32)
        buffer[0 : self.halo, :] = edge
        buffer[self.halo : self.halo + self.rows, :] = value
        buffer[self.halo + self.rows :, :] = edge

    def shifted(self, buffer, tap, sign):
        start = self.halo + sign * self.shift(tap)
        return buffer[start : start + self.rows, :].astype(BF16)


def wide(mask, channels):
    return jnp.concatenate([mask[...]] * (channels // LANES), axis=1)


def multiply(left, right, left_dim, right_dim):
    return lax.dot_general(
        left, right, (((left_dim,), (right_dim,)), ((), ())), preferred_element_type=F32
    )


def column_sum(value):
    return jnp.sum(value, axis=0, keepdims=True)


def spread_rows(rows, ref):
    ref[...] = jnp.broadcast_to(jnp.concatenate(rows, axis=0)[None], ref.shape)


def local_statistics(hidden, valid, *refs):
    total = column_sum(hidden * valid)
    centre = total / jnp.maximum(column_sum(valid), 1.0)
    squares = column_sum(jnp.square(hidden - centre) * valid)
    rows = jnp.concatenate([total, squares], axis=0)
    *info, ref = [ref[...] for ref in refs[:-1]] + [refs[-1]]
    rows = jnp.concatenate([rows, *info], axis=1)
    ref[...] = jnp.broadcast_to(rows[None], ref.shape)


def global_statistics(gathered, counts):
    channels = counts.shape[1]
    totals, squares = gathered[:, 0, :channels], gathered[:, 1, :channels]
    total = column_sum(counts)
    centre = column_sum(totals) / total
    between = column_sum(counts * jnp.square(totals / jnp.maximum(counts, 1.0) - centre))
    spread = (column_sum(squares) + between) / total
    return centre, lax.rsqrt(spread + NORM_EPS), total


def lay_out(canvas, field_refs, buffer):
    buffer[...] = jnp.zeros_like(buffer)
    for side, group, first, start in canvas.cells():
        for down in range(side):
            for right in range(side):
                row = start + down * canvas.down + right * CELL
                pair = field_refs[group][down, right, first : first + CELL, :]
                buffer[row : row + CELL, :] = pair.astype(F32)


def prepare(canvas, *refs):
    *field_refs, param_ref = refs[:4]
    mask_refs = refs[4:7]
    x_ref, mask_ref, info_ref, buffer = refs[7:]
    rows, channels = buffer.shape
    mask_ref[...] = jnp.zeros_like(mask_ref)
    for side, group, first, start in canvas.cells():
        for down in range(side):
            for right in range(side):
                for image in range(CELL):
                    row = start + down * canvas.down + right * CELL + image
                    value = mask_refs[group][down, first + image, right].astype(F32)
                    mask_ref[row : row + 1, :] = jnp.full((1, LANES), value, F32)
    lay_out(canvas, field_refs, buffer)
    x_ref[0:rows, :] = (buffer[...] * wide(mask_ref, channels)).astype(BF16)
    line = jnp.transpose(mask_ref[...])[0:1]
    rest = jnp.zeros((1, channels * 2 - rows), F32)
    lines = [line[:, :channels], jnp.concatenate([line[:, channels:], rest], axis=1)]
    lines.append(jnp.zeros((14, channels), F32))
    x_ref[rows:, :] = jnp.concatenate(lines, axis=0).astype(BF16)
    params = param_ref[...].astype(BF16).astype(F32)
    rows = [params[index : index + 1] for index in range(4)]
    if params.size < LANES:
        rows.append(jnp.zeros((1, LANES - params.size), F32))
    row = jnp.concatenate(rows, axis=1)
    info_ref[...] = jnp.concatenate([row, column_sum(mask_ref[...])], axis=0)


def sent_mask(canvas, lines):
    channels = lines.shape[1]
    turned = jnp.transpose(lines)
    column = jnp.concatenate([turned[:, 0:1], turned[: canvas.rows - channels, 1:2]], axis=0)
    return jnp.broadcast_to(column, (canvas.rows, channels))


def prepare_back(canvas, *refs):
    *field_refs, back_ref, buffer = refs
    lay_out(canvas, field_refs, buffer)
    back_ref[...] = buffer[...].astype(BF16)


def sigmoid(value):
    return 1.0 / (1.0 + jnp.exp(-value))


def swish_slope(value):
    logistic = sigmoid(value)
    return logistic * (1.0 + value * (1.0 - logistic))


class Whole:
    def __init__(self, array, width):
        self.arrays = self.last = [array]
        self.width = width

    @staticmethod
    def start(refs, weight, sems):
        for part in range(3):
            taps = pl.ds(3 * part, 3)
            pltpu.make_async_copy(refs[0].at[taps], weight.at[taps], sems.at[part]).start()


class Pieces:
    width = 32

    def __init__(self, pieces):
        self.arrays = [array for array, _, _ in pieces]
        self.last = self.arrays[-4:]
        self.places = [(slots, first) for _, slots, first in pieces]

    def start(self, refs, weight, sems):
        y, z, x, c = (lax.axis_index(name) for name in ("y", "z", "x", "c"))
        moves = []
        for ref, (slots, first) in zip(refs, self.places):
            _, _, rows, lanes = ref.shape
            for slot, (dy, dz, dx, dc) in enumerate(slots):
                shard = ((z ^ dz) * 2 + (x ^ dx)) * 2 + (c ^ dc)
                row = pl.multiple_of(shard * self.width + first, 16)
                lane = 0 if dy is None else pl.multiple_of((y ^ dy) * lanes, lanes)
                moves.append((ref.at[slot], pl.ds(row, rows), pl.ds(lane, lanes)))
        for part in range(3):
            taps = pl.ds(3 * part, 3)
            for source, row, lane in moves:
                target = weight.at[taps, row, lane]
                pltpu.make_async_copy(source.at[taps], target, sems.at[part]).start()


class Fetch:
    def __init__(self, source, refs, weight, sems, target=None):
        self.weight, self.sems, self.target = weight, sems, target
        self.waiting = [0, 1, 2]
        source.start(refs, weight, sems)

    def ready(self, tap, when=None):
        if tap % 3 or not self.waiting:
            return
        part = self.waiting.pop(0)

        def wait():
            taps = self.weight.at[pl.ds(3 * part, 3)]
            pltpu.make_async_copy(taps, taps, self.sems.at[part]).wait()
            if not self.waiting and self.target is not None:
                pltpu.make_async_copy(self.weight, self.target, self.sems.at[0]).start()

        wait() if when is None else pl.when(when)(wait)

    def finish(self):
        pltpu.make_async_copy(self.weight, self.target, self.sems.at[0]).wait()


def convolve(canvas, value, fetch, buffer, out_ref, sign, halves=False, when=None):
    canvas.place(buffer, value)
    if not halves:
        for tap in range(TAPS):
            part = canvas.shifted(buffer, tap, sign)
            fetch.ready(tap, when)
            product = multiply(part, fetch.weight[tap], 1, 1 if sign > 0 else 0)
            out_ref[...] = product if tap == 0 else out_ref[...] + product
        return
    for tap in range(TAPS):
        fetch.ready(tap)
    width = out_ref.shape[1] // 2

    def half(index, carry):
        columns = pl.ds(pl.multiple_of(index * width, width), width)
        for tap in range(TAPS):
            part = canvas.shifted(buffer, tap, sign)
            weight = fetch.weight[tap, columns] if sign > 0 else fetch.weight[tap, :, columns]
            product = multiply(part, weight, 1, 1 if sign > 0 else 0)
            out_ref[:, columns] = product if tap == 0 else out_ref[:, columns] + product
        return carry

    lax.fori_loop(0, 2, half, 0)


def activate(hidden, norm_ref, param_ref, valid):
    normed = (hidden - norm_ref[0:1, :]) * norm_ref[1:2, :]
    value = normed * param_ref[0:1, :] + param_ref[1:2, :]
    return value * sigmoid(value) * valid


def side_active(canvas, source, count, *refs):
    norm_ref, param_ref, *refs = refs
    weights, refs = refs[: len(source.arrays)], refs[len(source.arrays) :]
    sent_hbm, refs = refs[:count], refs[count:]
    active_ref, *full, buffer, weight, sems, hidden, sent, sent_sem = refs
    copies = [
        pltpu.make_async_copy(hbm, sent.at[index], sent_sem) for index, hbm in enumerate(sent_hbm)
    ]
    for copy in copies:
        copy.start()
    fetch = Fetch(source, weights, weight, sems, *full)
    for copy in copies:
        copy.wait()

    def image(index, carry):
        pixels = sent[index].astype(F32)
        convolve(canvas, pixels[: canvas.rows], fetch, buffer, hidden, 1, when=index == 0)
        valid = sent_mask(canvas, pixels[canvas.rows :])
        active = activate(hidden[...], norm_ref, param_ref, valid)
        active_ref[index] = active.astype(BF16)
        return carry

    lax.fori_loop(0, count, image, 0)
    if full:
        fetch.finish()


def forward_one(canvas, source, x_ref, mask_ref, info_ref, *refs):
    *weights, hidden_ref, stats_ref, buffer, weight, sem = refs
    fetch = Fetch(source, weights, weight, sem)
    convolve(canvas, x_ref[0 : canvas.rows, :].astype(F32), fetch, buffer, hidden_ref, 1)
    local_statistics(hidden_ref[...], wide(mask_ref, x_ref.shape[1]), info_ref, stats_ref)


def forward_two(canvas, source, hidden_ref, gathered_ref, mask_ref, *refs):
    *weights, active_ref, second_ref, norm_ref, param_ref, count_ref, stats_ref = refs[:-3]
    buffer, weight, sem = refs[-3:]
    fetch = Fetch(source, weights, weight, sem)
    channels = hidden_ref.shape[1]
    valid = wide(mask_ref, channels)
    width = source.width
    rows = []
    for index in range(4):
        start = channels + index * width
        rows.append(
            jnp.concatenate(
                [gathered_ref[shard, 0:1, start : start + width] for shard in range(channels // width)],
                axis=1,
            )
        )
    param_ref[...] = jnp.concatenate(rows, axis=0)
    counts = gathered_ref[:, 1, channels : channels + LANES]
    count_ref[...] = jnp.concatenate([counts] * (channels // LANES), axis=1)

    centre, inv, total = global_statistics(gathered_ref, count_ref[...])
    norm_ref[...] = jnp.concatenate([centre, inv, total, total], axis=0)
    value = activate(hidden_ref[...], norm_ref, param_ref, valid)
    active_ref[...] = value.astype(BF16)
    convolve(canvas, value, fetch, buffer, second_ref, 1)
    local_statistics(second_ref[...], valid, stats_ref)


def turn(
    second_ref,
    gathered_ref,
    count_ref,
    param_ref,
    mask_ref,
    x_ref,
    back_ref,
    result_ref,
    grad_ref,
    norm_ref,
    stats_ref,
):
    valid = wide(mask_ref, second_ref.shape[1])
    centre, inv, total = global_statistics(gathered_ref, count_ref[...])
    norm_ref[...] = jnp.concatenate([centre, inv, total, total], axis=0)
    normed = (second_ref[...] - centre) * inv
    rows = second_ref.shape[0]
    summed = normed * param_ref[2:3, :] + param_ref[3:4, :] + x_ref[0:rows, :].astype(F32)
    logistic = sigmoid(summed)
    result_ref[...] = (summed * logistic * valid).astype(BF16)
    slope = logistic * (1.0 + summed * (1.0 - logistic))
    grad = back_ref[...].astype(F32) * valid * slope
    grad_ref[...] = grad
    spread_rows([column_sum(grad), column_sum(grad * normed)], stats_ref)


def norm_back(row, norm_ref, gathered_ref, param_ref, sums_ref, *turned_refs, moving):
    grad_in, hidden, mask, inner_out = moving
    channels = norm_ref.shape[1]
    shift_grad = column_sum(gathered_ref[:, 0, :])
    gain_grad = column_sum(gathered_ref[:, 1, :])
    sums_ref[...] = jnp.concatenate([gain_grad, shift_grad], axis=0)
    centre, inv, total = norm_ref[0:1, :], norm_ref[1:2, :], norm_ref[2:3, :]
    gain = param_ref[row : row + 1, :] * inv
    full = turned_refs[-1]
    for part, (start, stop) in enumerate(inner_out.spans):
        normed = (hidden.part(part) - centre) * inv
        grad = grad_in.part(part) - shift_grad / total - normed * (gain_grad / total)
        inner = wide(mask.part(part), channels) * gain * grad
        inner_out.put(part, inner.astype(BF16))
        full[:, start:stop] = jnp.transpose(inner).astype(BF16)
    if len(turned_refs) == 1:
        return
    rows = inner_out.spans[-1][1]
    full[:, rows:] = jnp.zeros((channels, full.shape[1] - rows), BF16)
    y, x = lax.axis_index("y"), lax.axis_index("x")
    half = channels // 32
    for index, turned_ref in enumerate(turned_refs[:-1]):
        for c in range(2):
            for z in range(4):
                shard = (z * 2 + (x ^ (index % 2))) * 2 + c
                start = pl.multiple_of((shard * 2 + (y ^ (index // 2))) * half, half)
                turned_ref[c, z * half : (z + 1) * half, :] = full[pl.ds(start, half), :]


def backward_middle(canvas, source, inner_ref, hidden_ref, norm_ref, param_ref, mask_ref, *refs):
    *weights, grad_ref, stats_ref, buffer, weight, sem = refs
    valid = wide(mask_ref, hidden_ref.shape[1])
    fetch = Fetch(source, weights, weight, sem)
    convolve(canvas, inner_ref[...].astype(F32), fetch, buffer, grad_ref, -1)
    normed = (hidden_ref[...] - norm_ref[0:1, :]) * norm_ref[1:2, :]
    value = normed * param_ref[0:1, :] + param_ref[1:2, :]
    grad = grad_ref[...] * valid * swish_slope(value)
    grad_ref[...] = grad
    spread_rows([column_sum(grad), column_sum(grad * normed)], stats_ref)


def lay_back(canvas, flat, refs):
    for side, group, first, start in canvas.cells():
        for down in range(side):
            for right in range(side):
                row = start + down * canvas.down + right * CELL
                pair = flat[row : row + CELL, :].astype(refs[group].dtype)
                refs[group][down, right, first : first + CELL, :] = pair


def backward_input(canvas, source, inner_ref, residual_ref, mask_ref, result_ref, *refs):
    weights, refs = refs[: len(source.arrays)], refs[len(source.arrays) :]
    result_refs, grad_refs, (buffer, weight, sem, flat) = refs[:3], refs[3:6], refs[6:]
    fetch = Fetch(source, weights, weight, sem)
    convolve(canvas, inner_ref[...].astype(F32), fetch, buffer, flat, -1, True)
    flat[...] = residual_ref[...] + wide(mask_ref, flat.shape[1]) * flat[...]
    lay_back(canvas, flat, grad_refs)
    flat[...] = result_ref[...].astype(F32)
    lay_back(canvas, flat, result_refs)


def kernel_grad_whole(canvas, turned_ref, active_ref, out_ref, buffer):
    canvas.place(buffer, active_ref[0 : canvas.rows, :].astype(F32))
    for tap in range(TAPS):
        product = multiply(turned_ref[...], canvas.shifted(buffer, tap, 1), 1, 0)
        out_ref[tap] = product.astype(out_ref.dtype)


def kernel_grad_layer(canvas, *refs):
    turned_hbm, refs = refs[:4], refs[4:]
    active_hbm, (send_hbm, keep_hbm) = refs[:-9], refs[-9:-7]
    turned_ref, active_ref, left, total, send_ref, keep_ref, sems = refs[-7:]
    if len(active_hbm) < 4:
        own, pair, last = active_hbm
        active_hbm = (own, pair.at[0], pair.at[1], last.at[0])
    z, c = lax.axis_index("z"), lax.axis_index("c")
    rows, part = canvas.rows, turned_ref.shape[2]
    half = part // 4
    turns, copies = [], []
    for index, hbm in enumerate(turned_hbm):
        turns.append(pltpu.make_async_copy(hbm, turned_ref.at[index], sems.at[index]))
    for index, hbm in enumerate(active_hbm):
        target = active_ref.at[index, pl.ds(0, hbm.shape[0])]
        copies.append(pltpu.make_async_copy(hbm, target, sems.at[4 + index]))
    for pair in zip(turns, copies):
        for copy in pair:
            copy.start()
    def half_sum(core, wait):
        for index in range(4):
            slot = index % 2
            if wait:
                pl.when(core == 1)(turns[index].wait)
            turned = turned_ref[index, c ^ core].astype(F32)
            for tap in range(TAPS):
                shift = canvas.shift(tap) % canvas.lanes
                moved = pltpu.roll(turned, shift, 1) if shift else turned
                left[slot, tap * part : (tap + 1) * part, :] = moved[:, :rows].astype(BF16)
            if wait:
                pl.when(core == 1)(copies[index].wait)
            product = multiply(left[slot], active_ref[index, 0:rows, :], 1, 0)
            total[...] = product if index == 0 else total[...] + product

    def spread(ref):
        for tap in range(TAPS):
            for place in range(4):
                row = tap * part + (z ^ place) * half
                ref[place, tap] = total[pl.ds(row, half), :].astype(ref.dtype)

    send = pltpu.make_async_copy(send_ref, send_hbm, sems.at[8])
    keep = pltpu.make_async_copy(keep_ref, keep_hbm, sems.at[9])

    def both(step, carry):
        half_sum(1 - step, True)

        @pl.when(step == 0)
        def _():
            spread(send_ref)
            send.start()

        return carry

    lax.fori_loop(0, 2, both, 0)
    spread(keep_ref)
    keep.start()
    send.wait()
    keep.wait()


class Moving:
    def __init__(self, hbm, ref, sems, bounds, inward):
        self.ref, self.spans = ref, list(zip(bounds[:-1], bounds[1:]))
        self.copies, self.waited = [], set()
        for index, (start, stop) in enumerate(self.spans):
            far, near = hbm.at[pl.ds(start, stop - start)], ref.at[pl.ds(start, stop - start)]
            ends = (far, near) if inward else (near, far)
            self.copies.append(pltpu.make_async_copy(*ends, sems.at[index]))

    def start(self, index):
        self.copies[index].start()

    def part(self, index):
        if index not in self.waited:
            self.waited.add(index)
            self.copies[index].wait()
        start, stop = self.spans[index]
        return self.ref[start:stop, :]

    def put(self, index, value):
        start, stop = self.spans[index]
        self.ref[start:stop, :] = value
        self.copies[index].start()


def call(
    body,
    inputs,
    outputs,
    scratch=(),
    weights=(),
    after=(),
    scalars=(),
    kept=(),
    late=(),
    streams=(),
    bounds=(),
):
    whole = pl.BlockSpec(memory_space=pltpu.VMEM)
    anywhere = pl.BlockSpec(memory_space=pltpu.HBM)
    read = len(inputs) + len(scalars) + len(weights)
    moved = [(array.shape, array.dtype) for array in late] + list(streams)
    results = (*outputs, *kept, *streams)

    def split(refs, *counts):
        groups = []
        for count in counts:
            groups.append(refs[:count])
            refs = refs[count:]
        return groups

    def kernel(*refs):
        ins, far, _, outs, out_far, scratch_refs, near, sems = split(
            refs,
            read,
            len(late),
            len(after),
            len(outputs) + len(kept),
            len(streams),
            len(scratch),
            len(moved),
            len(moved),
        )
        if not moved:
            return body(*ins, *outs, *scratch_refs)
        moving = [
            Moving(hbm, ref, sem, bounds, index < len(late))
            for index, (hbm, ref, sem) in enumerate(zip((*far, *out_far), near, sems))
        ]
        for part in range(len(bounds) - 1 if len(bounds) > 2 else 0):
            for mover in moving[: len(late)]:
                mover.start(part)
        body(*ins, *outs, *scratch_refs, moving=moving)
        for mover in moving[len(late) :]:
            for copy in mover.copies:
                copy.wait()

    return pl.pallas_call(
        kernel,
        out_shape=[jax.ShapeDtypeStruct(shape, dtype) for shape, dtype in results],
        in_specs=[whole] * len(inputs)
        + [pl.BlockSpec(memory_space=pltpu.SMEM)] * len(scalars)
        + [anywhere] * (len(weights) + len(late) + len(after)),
        out_specs=[whole] * len(outputs) + [anywhere] * (len(kept) + len(streams)),
        scratch_shapes=list(scratch)
        + [pltpu.VMEM(shape, dtype) for shape, dtype in moved]
        + [pltpu.SemaphoreType.DMA((len(bounds) - 1,)) for _ in moved],
        compiler_params=pltpu.CompilerParams(vmem_limit_bytes=VMEM_BYTES),
    )(*inputs, *scalars, *weights, *late, *after)


def adamw(param, grad, first, second, rate, decay):
    first_new = BETA_ONE * first + (1.0 - BETA_ONE) * grad
    second_new = BETA_TWO * second + (1.0 - BETA_TWO) * grad * grad
    first_hat = first_new / (1.0 - BETA_ONE**STEP)
    second_hat = second_new / (1.0 - BETA_TWO**STEP)
    update = first_hat / (jnp.sqrt(second_hat) + ADAM_EPS)
    return (param - rate * (update + decay * param), first_new, second_new)


def flip(value, axis, bit, size):
    return lax.ppermute(value, axis, [(place, place ^ bit) for place in range(size)])


def diagonal(value):
    return lax.ppermute(value, ("y", "x"), [(place, place ^ 3) for place in range(4)])


def behind(value, others):
    return lax.optimization_barrier((value, *others))[0] if others else value


class Gather:
    def __init__(self, shard, half):
        self.shard, self.half = shard[None], half[None]

    def along_two(self, *others):
        self.second = flip(behind(self.half, others), "z", 2, 4)

    def beside(self, *others):
        self.nearest = flip(behind(self.shard, others), "x", 1, 2)

    def along_one(self, *others):
        both = jnp.concatenate([self.half, self.second], axis=0)
        self.line = flip(behind(both, others), "z", 1, 4)

    def across(self, *others):
        self.rest = rest = behind(jnp.concatenate([self.second, self.line], axis=0), others)
        self.over = flip(rest, "x", 1, 2), flip(rest, "y", 1, 2)

    def direct(self):
        self.corners = (diagonal(self.rest),)

    def corner(self, *others):
        rows = self.shard.shape[2] // 2
        over_x, over_y = self.over
        corners = (
            flip(behind(over_y[:, :, :rows], others), "x", 1, 2),
            flip(behind(over_x[:, :, rows:], others), "y", 1, 2),
        )
        self.corners = lax.optimization_barrier(corners)

    def cores(self, early=(), late=()):
        rows = self.shard.shape[2] // 2
        deep = (2, 1, 3)
        pieces = [
            (self.shard, [(None, 0, 0)], 0),
            (self.nearest, [(None, 0, 1)], 0),
            (self.rest, [(0, dz, 0) for dz in deep], 0),
            (self.over[0], [(0, dz, 1) for dz in deep], 0),
            (self.over[1], [(1, dz, 0) for dz in deep], 0),
        ]
        for index, array in enumerate(self.corners):
            pieces.append((array, [(1, dz, 1) for dz in deep], index * rows))
        self.found = []
        for index, (array, slots, first) in enumerate(pieces):
            others = late if index > 4 else early if index > 2 else ()
            other = flip(behind(array, others), "c", 1, 2)
            self.found.append((array, [slot + (0,) for slot in slots], first))
            self.found.append((other, [slot + (1,) for slot in slots], first))


class Grid:
    axes = ("y", "z", "x", "c")
    shard_axes = ("z", "x", "c")

    def weights(self, low, x, back):
        half = low.shape[3] // 2
        first, second = lax.dynamic_slice_in_dim(low, lax.axis_index("y") * half, half, 3)
        one, two = Gather(low[0], first), Gather(low[1], second)
        one.along_two()
        one.beside()
        self.pixels = x
        self.sides = flip(x, "x", 1, 2), flip(x, "y", 1, 2)
        one.along_one(x, one.nearest)
        two.along_two(one.line)
        one.across(back, *self.sides)
        two.along_one(*one.over)
        two.beside(*self.sides)
        one.corner()
        one.cores()
        two.across(two.nearest, *one.corners)
        two.direct()
        self.second = two
        return Pieces(one.found)

    def second_weights(self, stats, gathered, *others):
        self.second.cores((stats,), (gathered, *others))
        self.corners = (diagonal(behind(self.pixels, (stats,))),)
        return Pieces(self.second.found)

    def turned_shapes(self, canvas, channels):
        return (((2, channels // 8, canvas.lanes), BF16),) * 4

    def turned_scratch(self, canvas, channels):
        return (pltpu.VMEM((channels, canvas.lanes), BF16),)

    def send(self, own, over_x, over_y, corner):
        return own, flip(over_x, "x", 1, 2), flip(over_y, "y", 1, 2), diagonal(corner)

    def chip_sum(self, canvas, moved, layer, channels, after):
        out = (4, TAPS, channels // 32, channels)
        part = moved[0].shape[1]
        send, keep = call(
            functools.partial(kernel_grad_layer, canvas),
            (),
            (),
            (
                pltpu.VMEM((4, *moved[0].shape), BF16),
                pltpu.VMEM((4, canvas.sent_rows, channels), BF16),
                pltpu.VMEM((2, TAPS * part, canvas.rows), BF16),
                pltpu.VMEM((TAPS * part, channels), F32),
                pltpu.VMEM(out, BF16),
                pltpu.VMEM(out, F32),
                pltpu.SemaphoreType.DMA((10,)),
            ),
            (*moved, *layer),
            after,
            kept=((out, BF16), (out, F32)),
        )
        return send, keep

    def core_sum(self, chip, *others):
        send, keep = chip
        chip = keep + flip(behind(send, others), "c", 1, 2).astype(F32)
        return chip[0], *[chip[place].astype(BF16) for place in range(1, 4)]

    def line(self, parts):
        return [flip(part, "z", place, 4) for place, part in enumerate(parts[1:], 1)]

    def line_sum(self, parts, found, *others):
        total = behind(parts[0], others)
        for part in found:
            total = total + part.astype(F32)
        return total

    def owned(self, line):
        own = line.astype(BF16)
        other = flip(own, "y", 1, 2)
        first = lax.axis_index("y") == 0
        halves = [jnp.where(first, own, other), jnp.where(first, other, own)]
        return jnp.concatenate(halves, axis=1).astype(F32)


class Plain:
    axes = ("dp", "fsdp")
    shard_axes = ("fsdp",)

    sides = corners = ()

    def weights(self, low, x, back):
        full = lax.all_gather(low, "fsdp", axis=2, tiled=True)
        first, self.second = [Whole(array, low.shape[2]) for array in full]
        return first

    def second_weights(self, stats, gathered, *others):
        return self.second

    def turned_shapes(self, canvas, channels):
        return (((channels, canvas.rows), BF16),)

    def turned_scratch(self, canvas, channels):
        return ()

    def send(self, turned):
        return (turned,)

    def chip_sum(self, canvas, moved, layer, channels, after):
        (full,) = call(
            functools.partial(kernel_grad_whole, canvas),
            (*moved, layer[0]),
            (((TAPS, channels, channels), BF16),),
            (pltpu.VMEM((canvas.padded_rows, channels), F32),),
            after=after,
        )
        return (full,)

    def core_sum(self, chip, *others):
        return chip

    def line(self, parts):
        return ()

    def line_sum(self, parts, found, *others):
        return lax.psum_scatter(parts[0], "fsdp", scatter_dimension=1, tiled=True)

    def owned(self, line):
        return lax.psum(line, "dp").astype(F32)


def local(
    ways,
    sizes,
    field_five,
    field_seven,
    field_nine,
    mask_five,
    mask_seven,
    mask_nine,
    back_five,
    back_seven,
    back_nine,
    kernels,
    norm_params,
    kernel_first,
    kernel_second,
    norm_first,
    norm_second,
):
    copies, shards = sizes
    fields = (field_five, field_seven, field_nine)
    masks = (mask_five, mask_seven, mask_nine)
    backs = (back_five, back_seven, back_nine)
    channels = field_five.shape[3]
    width = kernels.shape[4]
    canvas = Canvas([(field.shape[0], field.shape[1]) for field in fields])
    rows = canvas.rows
    count = copies * shards

    def turned(kernel):
        return jnp.transpose(kernel, (0, 1, 2, 4, 3)).reshape(2, TAPS, width, channels)

    def exchange(spread):
        return lax.all_to_all(spread, ways.axes, 0, 0, tiled=True)

    kernels_turned = turned(kernels)
    low = kernels_turned.astype(BF16)

    buffer = pltpu.VMEM((rows, channels), F32)
    weighted = (
        pltpu.VMEM((canvas.padded_rows, channels), F32),
        pltpu.VMEM((TAPS, channels, channels), BF16),
        pltpu.SemaphoreType.DMA((3,)),
    )
    flat32 = ((rows, channels), F32)
    flat16 = ((rows, channels), BF16)
    two = ((count, 2, channels), F32)
    norm = ((4, channels), F32)
    sums = ((2, channels), F32)
    turned_shapes = ways.turned_shapes(canvas, channels)
    turned_scratch = ways.turned_scratch(canvas, channels)

    full = ((TAPS, channels, channels), BF16)

    bounds = (*range(0, rows - LANES, LANES), rows)

    bounds = (*range(0, rows - LANES, LANES), rows)

    def conv_call(body, source, inputs, outputs, after=()):
        return call(
            functools.partial(body, canvas, source),
            inputs,
            outputs,
            weighted,
            source.arrays,
            after,
        )

    x, mask, info = call(
        functools.partial(prepare, canvas),
        (*[jnp.transpose(field, (1, 2, 0, 3)) for field in fields], norm_params),
        (((canvas.sent_rows, channels), BF16), ((rows, LANES), F32), ((2, LANES), F32)),
        (buffer,),
        scalars=[jnp.transpose(mask, (1, 0, 2)) for mask in masks],
    )
    (back,) = call(
        functools.partial(prepare_back, canvas),
        [jnp.transpose(field, (1, 2, 0, 3)) for field in backs],
        (flat16,),
        (buffer,),
    )
    weight_one = ways.weights(low, x, back)
    sides = ways.sides
    hidden, stats = conv_call(
        forward_one,
        weight_one,
        (x, mask, info),
        (flat32, ((count, 2, channels + LANES), F32)),
        after=sides,
    )
    gathered = exchange(stats)
    side = ()
    weight_two = ways.second_weights(stats, gathered, *side)
    active, second, norm_one, params, counts, stats = conv_call(
        forward_two,
        weight_two,
        (hidden, gathered, mask),
        (flat16, flat32, norm, norm, ((count, channels), F32), two),
        after=side,
    )
    gathered = exchange(stats)
    actives = (active,)

    def side_call(sent, after, kept=()):
        return call(
            functools.partial(side_active, canvas, weight_one, len(sent)),
            (norm_one, params),
            (((len(sent), rows, channels), BF16),),
            (
                *weighted,
                pltpu.VMEM((rows, channels), F32),
                pltpu.VMEM((len(sent), canvas.sent_rows, channels), BF16),
                pltpu.SemaphoreType.DMA,
            ),
            (*weight_one.arrays, *sent),
            after,
            kept=kept,
        )

    if sides:
        found, full_one = side_call(sides, (stats,), (full,))
        weight_one = Whole(full_one, weight_one.width)
        actives += (found,)
    result, grad_sum, norm_two, stats = call(
        turn,
        (second, gathered, counts, params, mask, x, back),
        (flat16, flat32, norm, two),
        after=actives[1:],
    )
    gathered = exchange(stats)
    if sides:
        actives += tuple(side_call(ways.corners, (stats,)))
    sums_two, *turned_two, inner_two = call(
        functools.partial(norm_back, 2),
        (norm_two, gathered, params),
        (sums, *turned_shapes),
        turned_scratch,
        late=(grad_sum, second, mask),
        streams=(flat16,),
        bounds=bounds,
        after=actives[2:],
    )
    moved_two = ways.send(*turned_two)
    grad_hidden, stats = conv_call(
        backward_middle, weight_two, (inner_two, hidden, norm_one, params, mask), (flat32, two)
    )
    gathered = exchange(behind(stats, moved_two[1:]))
    chip_two = ways.chip_sum(canvas, moved_two, actives, channels, (grad_hidden,))
    layer_x = (x, *sides, *ways.corners)
    sums_one, *turned_one, inner_one = call(
        functools.partial(norm_back, 0),
        (norm_one, gathered, params),
        (sums, *turned_shapes),
        turned_scratch,
        late=(grad_hidden, hidden, mask),
        streams=(flat16,),
        bounds=bounds,
        after=chip_two,
    )
    moved_one = ways.send(*turned_one)
    core_two = ways.core_sum(chip_two, gathered)
    line_two = ways.line(core_two)
    chip_one = ways.chip_sum(canvas, moved_one, layer_x, channels, core_two[1:])
    core_one = ways.core_sum(chip_one, *line_two)
    shapes = [(side, side, images, channels) for images, side in canvas.shapes]
    finished = call(
        functools.partial(backward_input, canvas, weight_one),
        (inner_one, grad_sum, mask, result),
        [(shape, BF16) for shape in shapes] + [(shape, F32) for shape in shapes],
        (*weighted, buffer),
        weight_one.arrays,
        core_one,
    )
    owned_two = ways.owned(ways.line_sum(core_two, line_two, finished[0]))
    owned_one = ways.owned(ways.line_sum(core_one, ways.line(core_one), finished[0]))

    results = adamw(
        kernels_turned,
        jnp.stack([owned_one, owned_two]),
        turned(kernel_first),
        turned(kernel_second),
        KERNEL_RATE,
        KERNEL_DECAY,
    )
    kernel_results = [
        jnp.transpose(value.reshape(2, 3, 3, width, channels), (0, 1, 2, 4, 3))
        for value in results
    ]
    norm_full = jnp.concatenate([behind(sums_one, finished[:1]), sums_two], axis=0)
    place = lax.axis_index(ways.shard_axes) * width
    norm_grads = lax.dynamic_slice_in_dim(norm_full, place, width, 1)
    norm_results = adamw(norm_params, norm_grads, norm_first, norm_second, NORM_RATE, 0.0)
    return (
        *[jnp.transpose(array, (2, 0, 1, 3)) for array in finished],
        *kernel_results,
        *norm_results,
    )


def solution(mesh):
    sizes = (mesh.shape["dp"], mesh.shape["fsdp"])
    if sizes == (2, 16):
        ways = Grid()
        mesh = Mesh(mesh.devices.reshape(2, 4, 2, 2), ways.axes)
    else:
        ways = Plain()
    images = P(ways.axes, None, None, None)
    maps = P(ways.axes, None, None)
    weights = P(None, None, None, None, ways.shard_axes)
    norms = P(None, ways.shard_axes)
    in_specs = (
        (images,) * 3 + (maps,) * 3 + (images,) * 3 + (weights, norms, weights, weights, norms, norms)
    )
    out_specs = (images,) * 6 + (weights,) * 3 + (norms,) * 3
    body = functools.partial(local, ways, sizes)
    return jax.shard_map(body, mesh=mesh, in_specs=in_specs, out_specs=out_specs, check_vma=False)
```

```python
import functools

import jax
import jax.numpy as jnp
from jax import lax
from jax.experimental import pallas as pl
from jax.experimental.pallas import tpu as pltpu
from jax.sharding import Mesh, PartitionSpec as P

STEP = 5
NORM_EPS = 1e-05
BETA_ONE = 0.5
BETA_TWO = 0.5
KERNEL_RATE = 0.03
NORM_RATE = 0.4
KERNEL_DECAY = 0.01
ADAM_EPS = 1e-08
TAPS = 9
LANES = 128
CELL = 2
VMEM_BYTES = 53 * 1024 * 1024
F32, BF16 = jnp.float32, jnp.bfloat16


def round_up(value, step):
    return (value + step - 1) // step * step


class Canvas:
    def __init__(self, shapes):
        self.shapes = shapes
        cells = [
            (side, group, first)
            for group, (count, side) in enumerate(shapes)
            for first in range(0, count, CELL)
        ]
        limit = max(
            sum(side + 1 for side, group, _ in cells if group == wanted)
            for wanted in range(len(shapes))
        )
        self.bands = []
        for side, group, first in sorted(cells, reverse=True):
            used = sum(cell[0] + 1 for cell in self.bands[-1]) if self.bands else limit
            if used + side + 1 > limit:
                self.bands.append([])
            self.bands[-1].append((side, group, first))
        self.width = limit
        self.right = CELL
        self.down = limit * CELL
        self.heights = [band[0][0] for band in self.bands]
        used_rows = (sum(self.heights) + len(self.bands) - 1) * self.down
        self.rows = round_up(used_rows, 16)
        self.halo = round_up(self.down + self.right, 8)
        self.lanes = round_up(self.rows + self.down + self.right, LANES)
        self.padded_rows = self.rows + 2 * self.halo
        self.sent_rows = self.rows + 16

    def cells(self):
        start = 0
        for band, height in zip(self.bands, self.heights):
            column = 0
            for side, group, first in band:
                yield side, group, first, start * self.down + column * CELL
                column += side + 1
            start += height + 1

    def shift(self, tap):
        return (tap // 3 - 1) * self.down + (tap % 3 - 1) * self.right

    def place(self, buffer, value):
        edge = jnp.zeros((self.halo, value.shape[1]), F32)
        buffer[0 : self.halo, :] = edge
        buffer[self.halo : self.halo + self.rows, :] = value
        buffer[self.halo + self.rows :, :] = edge

    def shifted(self, buffer, tap, sign):
        start = self.halo + sign * self.shift(tap)
        return buffer[start : start + self.rows, :].astype(BF16)


def wide(mask, channels):
    return jnp.concatenate([mask[...]] * (channels // LANES), axis=1)


def multiply(left, right, left_dim, right_dim):
    return lax.dot_general(
        left, right, (((left_dim,), (right_dim,)), ((), ())), preferred_element_type=F32
    )


def column_sum(value):
    return jnp.sum(value, axis=0, keepdims=True)


def spread_rows(rows, ref):
    ref[...] = jnp.broadcast_to(jnp.concatenate(rows, axis=0)[None], ref.shape)


def local_statistics(hidden, valid, *refs):
    total = column_sum(hidden * valid)
    centre = total / jnp.maximum(column_sum(valid), 1.0)
    squares = column_sum(jnp.square(hidden - centre) * valid)
    rows = jnp.concatenate([total, squares], axis=0)
    *info, ref = [ref[...] for ref in refs[:-1]] + [refs[-1]]
    rows = jnp.concatenate([rows, *info], axis=1)
    ref[...] = jnp.broadcast_to(rows[None], ref.shape)


def global_statistics(gathered, counts):
    channels = counts.shape[1]
    totals, squares = gathered[:, 0, :channels], gathered[:, 1, :channels]
    total = column_sum(counts)
    centre = column_sum(totals) / total
    between = column_sum(counts * jnp.square(totals / jnp.maximum(counts, 1.0) - centre))
    spread = (column_sum(squares) + between) / total
    return centre, lax.rsqrt(spread + NORM_EPS), total


def lay_out(canvas, field_refs, buffer):
    buffer[...] = jnp.zeros_like(buffer)
    for side, group, first, start in canvas.cells():
        for down in range(side):
            for right in range(side):
                row = start + down * canvas.down + right * CELL
                pair = field_refs[group][down, right, first : first + CELL, :]
                buffer[row : row + CELL, :] = pair.astype(F32)


def prepare(canvas, *refs):
    *field_refs, param_ref = refs[:4]
    mask_refs = refs[4:7]
    x_ref, mask_ref, info_ref, buffer = refs[7:]
    rows, channels = buffer.shape
    mask_ref[...] = jnp.zeros_like(mask_ref)
    for side, group, first, start in canvas.cells():
        for down in range(side):
            for right in range(side):
                for image in range(CELL):
                    row = start + down * canvas.down + right * CELL + image
                    value = mask_refs[group][down, first + image, right].astype(F32)
                    mask_ref[row : row + 1, :] = jnp.full((1, LANES), value, F32)
    lay_out(canvas, field_refs, buffer)
    x_ref[0:rows, :] = (buffer[...] * wide(mask_ref, channels)).astype(BF16)
    line = jnp.transpose(mask_ref[...])[0:1]
    rest = jnp.zeros((1, channels * 2 - rows), F32)
    lines = [line[:, :channels], jnp.concatenate([line[:, channels:], rest], axis=1)]
    lines.append(jnp.zeros((14, channels), F32))
    x_ref[rows:, :] = jnp.concatenate(lines, axis=0).astype(BF16)
    params = param_ref[...].astype(BF16).astype(F32)
    rows = [params[index : index + 1] for index in range(4)]
    if params.size < LANES:
        rows.append(jnp.zeros((1, LANES - params.size), F32))
    row = jnp.concatenate(rows, axis=1)
    info_ref[...] = jnp.concatenate([row, column_sum(mask_ref[...])], axis=0)


def sent_mask(canvas, lines):
    channels = lines.shape[1]
    turned = jnp.transpose(lines)
    column = jnp.concatenate([turned[:, 0:1], turned[: canvas.rows - channels, 1:2]], axis=0)
    return jnp.broadcast_to(column, (canvas.rows, channels))


def prepare_back(canvas, *refs):
    *field_refs, back_ref, buffer = refs
    lay_out(canvas, field_refs, buffer)
    back_ref[...] = buffer[...].astype(BF16)


def sigmoid(value):
    return 1.0 / (1.0 + jnp.exp(-value))


def swish_slope(value):
    logistic = sigmoid(value)
    return logistic * (1.0 + value * (1.0 - logistic))


class Whole:
    def __init__(self, array, width):
        self.arrays = self.last = [array]
        self.width = width

    @staticmethod
    def start(refs, weight, sems):
        for part in range(3):
            taps = pl.ds(3 * part, 3)
            pltpu.make_async_copy(refs[0].at[taps], weight.at[taps], sems.at[part]).start()


class Pieces:
    width = 32

    def __init__(self, pieces):
        self.arrays = [array for array, _, _ in pieces]
        self.last = self.arrays[-4:]
        self.places = [(slots, first) for _, slots, first in pieces]

    def start(self, refs, weight, sems):
        y, z, x, c = (lax.axis_index(name) for name in ("y", "z", "x", "c"))
        moves = []
        for ref, (slots, first) in zip(refs, self.places):
            _, _, rows, lanes = ref.shape
            for slot, (dy, dz, dx, dc) in enumerate(slots):
                shard = ((z ^ dz) * 2 + (x ^ dx)) * 2 + (c ^ dc)
                row = pl.multiple_of(shard * self.width + first, 16)
                lane = 0 if dy is None else pl.multiple_of((y ^ dy) * lanes, lanes)
                moves.append((ref.at[slot], pl.ds(row, rows), pl.ds(lane, lanes)))
        for part in range(3):
            taps = pl.ds(3 * part, 3)
            for source, row, lane in moves:
                target = weight.at[taps, row, lane]
                pltpu.make_async_copy(source.at[taps], target, sems.at[part]).start()


class Fetch:
    def __init__(self, source, refs, weight, sems, target=None):
        self.weight, self.sems, self.target = weight, sems, target
        self.waiting = [0, 1, 2]
        source.start(refs, weight, sems)

    def ready(self, tap, when=None):
        if tap % 3 or not self.waiting:
            return
        part = self.waiting.pop(0)

        def wait():
            taps = self.weight.at[pl.ds(3 * part, 3)]
            pltpu.make_async_copy(taps, taps, self.sems.at[part]).wait()
            if not self.waiting and self.target is not None:
                pltpu.make_async_copy(self.weight, self.target, self.sems.at[0]).start()

        wait() if when is None else pl.when(when)(wait)

    def finish(self):
        pltpu.make_async_copy(self.weight, self.target, self.sems.at[0]).wait()


def convolve(canvas, value, fetch, buffer, out_ref, sign, halves=False, when=None):
    canvas.place(buffer, value)
    if not halves:
        for tap in range(TAPS):
            part = canvas.shifted(buffer, tap, sign)
            fetch.ready(tap, when)
            product = multiply(part, fetch.weight[tap], 1, 1 if sign > 0 else 0)
            out_ref[...] = product if tap == 0 else out_ref[...] + product
        return
    for tap in range(TAPS):
        fetch.ready(tap)
    width = out_ref.shape[1] // 2

    def half(index, carry):
        columns = pl.ds(pl.multiple_of(index * width, width), width)
        for tap in range(TAPS):
            part = canvas.shifted(buffer, tap, sign)
            weight = fetch.weight[tap, columns] if sign > 0 else fetch.weight[tap, :, columns]
            product = multiply(part, weight, 1, 1 if sign > 0 else 0)
            out_ref[:, columns] = product if tap == 0 else out_ref[:, columns] + product
        return carry

    lax.fori_loop(0, 2, half, 0)


def activate(hidden, norm_ref, param_ref, valid):
    normed = (hidden - norm_ref[0:1, :]) * norm_ref[1:2, :]
    value = normed * param_ref[0:1, :] + param_ref[1:2, :]
    return value * sigmoid(value) * valid


def side_active(canvas, source, count, *refs):
    norm_ref, param_ref, *refs = refs
    weights, refs = refs[: len(source.arrays)], refs[len(source.arrays) :]
    sent_hbm, refs = refs[:count], refs[count:]
    active_ref, *full, buffer, weight, sems, hidden, sent, sent_sem = refs
    copies = [
        pltpu.make_async_copy(hbm, sent.at[index], sent_sem) for index, hbm in enumerate(sent_hbm)
    ]
    for copy in copies:
        copy.start()
    fetch = Fetch(source, weights, weight, sems, *full)
    for copy in copies:
        copy.wait()

    def image(index, carry):
        pixels = sent[index].astype(F32)
        convolve(canvas, pixels[: canvas.rows], fetch, buffer, hidden, 1, when=index == 0)
        valid = sent_mask(canvas, pixels[canvas.rows :])
        active = activate(hidden[...], norm_ref, param_ref, valid)
        active_ref[index] = active.astype(BF16)
        return carry

    lax.fori_loop(0, count, image, 0)
    if full:
        fetch.finish()


def forward_one(canvas, source, x_ref, mask_ref, info_ref, *refs):
    *weights, hidden_ref, stats_ref, buffer, weight, sem = refs
    fetch = Fetch(source, weights, weight, sem)
    convolve(canvas, x_ref[0 : canvas.rows, :].astype(F32), fetch, buffer, hidden_ref, 1)
    local_statistics(hidden_ref[...], wide(mask_ref, x_ref.shape[1]), info_ref, stats_ref)


def forward_two(canvas, source, hidden_ref, gathered_ref, mask_ref, *refs):
    *weights, active_ref, second_ref, norm_ref, param_ref, count_ref, stats_ref = refs[:-3]
    buffer, weight, sem = refs[-3:]
    fetch = Fetch(source, weights, weight, sem)
    channels = hidden_ref.shape[1]
    valid = wide(mask_ref, channels)
    width = source.width
    rows = []
    for index in range(4):
        start = channels + index * width
        rows.append(
            jnp.concatenate(
                [gathered_ref[shard, 0:1, start : start + width] for shard in range(channels // width)],
                axis=1,
            )
        )
    param_ref[...] = jnp.concatenate(rows, axis=0)
    counts = gathered_ref[:, 1, channels : channels + LANES]
    count_ref[...] = jnp.concatenate([counts] * (channels // LANES), axis=1)

    centre, inv, total = global_statistics(gathered_ref, count_ref[...])
    norm_ref[...] = jnp.concatenate([centre, inv, total, total], axis=0)
    value = activate(hidden_ref[...], norm_ref, param_ref, valid)
    active_ref[...] = value.astype(BF16)
    convolve(canvas, value, fetch, buffer, second_ref, 1)
    local_statistics(second_ref[...], valid, stats_ref)


def turn(
    second_ref,
    gathered_ref,
    count_ref,
    param_ref,
    mask_ref,
    x_ref,
    back_ref,
    result_ref,
    grad_ref,
    norm_ref,
    stats_ref,
):
    valid = wide(mask_ref, second_ref.shape[1])
    centre, inv, total = global_statistics(gathered_ref, count_ref[...])
    norm_ref[...] = jnp.concatenate([centre, inv, total, total], axis=0)
    normed = (second_ref[...] - centre) * inv
    rows = second_ref.shape[0]
    summed = normed * param_ref[2:3, :] + param_ref[3:4, :] + x_ref[0:rows, :].astype(F32)
    logistic = sigmoid(summed)
    result_ref[...] = (summed * logistic * valid).astype(BF16)
    slope = logistic * (1.0 + summed * (1.0 - logistic))
    grad = back_ref[...].astype(F32) * valid * slope
    grad_ref[...] = grad
    spread_rows([column_sum(grad), column_sum(grad * normed)], stats_ref)


def norm_back(row, norm_ref, gathered_ref, param_ref, sums_ref, *turned_refs, moving):
    grad_in, hidden, mask, inner_out = moving
    channels = norm_ref.shape[1]
    shift_grad = column_sum(gathered_ref[:, 0, :])
    gain_grad = column_sum(gathered_ref[:, 1, :])
    sums_ref[...] = jnp.concatenate([gain_grad, shift_grad], axis=0)
    centre, inv, total = norm_ref[0:1, :], norm_ref[1:2, :], norm_ref[2:3, :]
    gain = param_ref[row : row + 1, :] * inv
    full = turned_refs[-1]
    for part, (start, stop) in enumerate(inner_out.spans):
        normed = (hidden.part(part) - centre) * inv
        grad = grad_in.part(part) - shift_grad / total - normed * (gain_grad / total)
        inner = wide(mask.part(part), channels) * gain * grad
        inner_out.put(part, inner.astype(BF16))
        full[:, start:stop] = jnp.transpose(inner).astype(BF16)
    if len(turned_refs) == 1:
        return
    rows = inner_out.spans[-1][1]
    full[:, rows:] = jnp.zeros((channels, full.shape[1] - rows), BF16)
    y, x = lax.axis_index("y"), lax.axis_index("x")
    half = channels // 32
    for index, turned_ref in enumerate(turned_refs[:-1]):
        for c in range(2):
            for z in range(4):
                shard = (z * 2 + (x ^ (index % 2))) * 2 + c
                start = pl.multiple_of((shard * 2 + (y ^ (index // 2))) * half, half)
                turned_ref[c, z * half : (z + 1) * half, :] = full[pl.ds(start, half), :]


def backward_middle(canvas, source, inner_ref, hidden_ref, norm_ref, param_ref, mask_ref, *refs):
    *weights, grad_ref, stats_ref, buffer, weight, sem = refs
    valid = wide(mask_ref, hidden_ref.shape[1])
    fetch = Fetch(source, weights, weight, sem)
    convolve(canvas, inner_ref[...].astype(F32), fetch, buffer, grad_ref, -1)
    normed = (hidden_ref[...] - norm_ref[0:1, :]) * norm_ref[1:2, :]
    value = normed * param_ref[0:1, :] + param_ref[1:2, :]
    grad = grad_ref[...] * valid * swish_slope(value)
    grad_ref[...] = grad
    spread_rows([column_sum(grad), column_sum(grad * normed)], stats_ref)


def lay_back(canvas, flat, refs):
    for side, group, first, start in canvas.cells():
        for down in range(side):
            for right in range(side):
                row = start + down * canvas.down + right * CELL
                pair = flat[row : row + CELL, :].astype(refs[group].dtype)
                refs[group][down, right, first : first + CELL, :] = pair


def backward_input(canvas, source, inner_ref, residual_ref, mask_ref, result_ref, *refs):
    weights, refs = refs[: len(source.arrays)], refs[len(source.arrays) :]
    result_refs, grad_refs, (buffer, weight, sem, flat) = refs[:3], refs[3:6], refs[6:]
    fetch = Fetch(source, weights, weight, sem)
    convolve(canvas, inner_ref[...].astype(F32), fetch, buffer, flat, -1, True)
    flat[...] = residual_ref[...] + wide(mask_ref, flat.shape[1]) * flat[...]
    lay_back(canvas, flat, grad_refs)
    flat[...] = result_ref[...].astype(F32)
    lay_back(canvas, flat, result_refs)


def kernel_grad_whole(canvas, turned_ref, active_ref, out_ref, buffer):
    canvas.place(buffer, active_ref[0 : canvas.rows, :].astype(F32))
    for tap in range(TAPS):
        product = multiply(turned_ref[...], canvas.shifted(buffer, tap, 1), 1, 0)
        out_ref[tap] = product.astype(out_ref.dtype)


def kernel_grad_layer(canvas, *refs):
    turned_hbm, refs = refs[:4], refs[4:]
    active_hbm, (send_hbm, keep_hbm) = refs[:-9], refs[-9:-7]
    turned_ref, active_ref, left, total, send_ref, keep_ref, sems = refs[-7:]
    if len(active_hbm) < 4:
        own, pair, last = active_hbm
        active_hbm = (own, pair.at[0], pair.at[1], last.at[0])
    z, c = lax.axis_index("z"), lax.axis_index("c")
    rows, part = canvas.rows, turned_ref.shape[2]
    half = part // 4
    turns, copies = [], []
    for index, hbm in enumerate(turned_hbm):
        turns.append(pltpu.make_async_copy(hbm, turned_ref.at[index], sems.at[index]))
    for index, hbm in enumerate(active_hbm):
        target = active_ref.at[index, pl.ds(0, hbm.shape[0])]
        copies.append(pltpu.make_async_copy(hbm, target, sems.at[4 + index]))
    for pair in zip(turns, copies):
        for copy in pair:
            copy.start()
    def half_sum(core, wait):
        for index in range(4):
            slot = index % 2
            turned = turned_ref[index, c ^ core].astype(F32)
            for tap in range(TAPS):
                shift = canvas.shift(tap) % canvas.lanes
                moved = pltpu.roll(turned, shift, 1) if shift else turned
                left[slot, tap * part : (tap + 1) * part, :] = moved[:, :rows].astype(BF16)
            if wait:
                pl.when(core == 1)(copies[index].wait)
            product = multiply(left[slot], active_ref[index, 0:rows, :], 1, 0)
            total[...] = product if index == 0 else total[...] + product

    def spread(ref):
        for tap in range(TAPS):
            for place in range(4):
                row = tap * part + (z ^ place) * half
                ref[place, tap] = total[pl.ds(row, half), :].astype(ref.dtype)

    send = pltpu.make_async_copy(send_ref, send_hbm, sems.at[8])
    keep = pltpu.make_async_copy(keep_ref, keep_hbm, sems.at[9])

    for turn in turns:
        turn.wait()

    def both(step, carry):
        half_sum(1 - step, True)

        @pl.when(step == 0)
        def _():
            spread(send_ref)
            send.start()

        return carry

    lax.fori_loop(0, 2, both, 0)
    spread(keep_ref)
    keep.start()
    send.wait()
    keep.wait()


class Moving:
    def __init__(self, hbm, ref, sems, bounds, inward):
        self.ref, self.spans = ref, list(zip(bounds[:-1], bounds[1:]))
        self.copies, self.waited = [], set()
        for index, (start, stop) in enumerate(self.spans):
            far, near = hbm.at[pl.ds(start, stop - start)], ref.at[pl.ds(start, stop - start)]
            ends = (far, near) if inward else (near, far)
            self.copies.append(pltpu.make_async_copy(*ends, sems.at[index]))

    def start(self, index):
        self.copies[index].start()

    def part(self, index):
        if index not in self.waited:
            self.waited.add(index)
            self.copies[index].wait()
        start, stop = self.spans[index]
        return self.ref[start:stop, :]

    def put(self, index, value):
        start, stop = self.spans[index]
        self.ref[start:stop, :] = value
        self.copies[index].start()


def call(
    body,
    inputs,
    outputs,
    scratch=(),
    weights=(),
    after=(),
    scalars=(),
    kept=(),
    late=(),
    streams=(),
    bounds=(),
):
    whole = pl.BlockSpec(memory_space=pltpu.VMEM)
    anywhere = pl.BlockSpec(memory_space=pltpu.HBM)
    read = len(inputs) + len(scalars) + len(weights)
    moved = [(array.shape, array.dtype) for array in late] + list(streams)
    results = (*outputs, *kept, *streams)

    def split(refs, *counts):
        groups = []
        for count in counts:
            groups.append(refs[:count])
            refs = refs[count:]
        return groups

    def kernel(*refs):
        ins, far, _, outs, out_far, scratch_refs, near, sems = split(
            refs,
            read,
            len(late),
            len(after),
            len(outputs) + len(kept),
            len(streams),
            len(scratch),
            len(moved),
            len(moved),
        )
        if not moved:
            return body(*ins, *outs, *scratch_refs)
        moving = [
            Moving(hbm, ref, sem, bounds, index < len(late))
            for index, (hbm, ref, sem) in enumerate(zip((*far, *out_far), near, sems))
        ]
        for part in range(len(bounds) - 1 if len(bounds) > 2 else 0):
            for mover in moving[: len(late)]:
                mover.start(part)
        body(*ins, *outs, *scratch_refs, moving=moving)
        for mover in moving[len(late) :]:
            for copy in mover.copies:
                copy.wait()

    return pl.pallas_call(
        kernel,
        out_shape=[jax.ShapeDtypeStruct(shape, dtype) for shape, dtype in results],
        in_specs=[whole] * len(inputs)
        + [pl.BlockSpec(memory_space=pltpu.SMEM)] * len(scalars)
        + [anywhere] * (len(weights) + len(late) + len(after)),
        out_specs=[whole] * len(outputs) + [anywhere] * (len(kept) + len(streams)),
        scratch_shapes=list(scratch)
        + [pltpu.VMEM(shape, dtype) for shape, dtype in moved]
        + [pltpu.SemaphoreType.DMA((len(bounds) - 1,)) for _ in moved],
        compiler_params=pltpu.CompilerParams(vmem_limit_bytes=VMEM_BYTES),
    )(*inputs, *scalars, *weights, *late, *after)


def adamw(param, grad, first, second, rate, decay):
    first_new = BETA_ONE * first + (1.0 - BETA_ONE) * grad
    second_new = BETA_TWO * second + (1.0 - BETA_TWO) * grad * grad
    first_hat = first_new / (1.0 - BETA_ONE**STEP)
    second_hat = second_new / (1.0 - BETA_TWO**STEP)
    update = first_hat / (jnp.sqrt(second_hat) + ADAM_EPS)
    return (param - rate * (update + decay * param), first_new, second_new)


def flip(value, axis, bit, size):
    return lax.ppermute(value, axis, [(place, place ^ bit) for place in range(size)])


def diagonal(value):
    return lax.ppermute(value, ("y", "x"), [(place, place ^ 3) for place in range(4)])


def behind(value, others):
    return lax.optimization_barrier((value, *others))[0] if others else value


class Gather:
    def __init__(self, shard, half):
        self.shard, self.half = shard[None], half[None]

    def along_two(self, *others):
        self.second = flip(behind(self.half, others), "z", 2, 4)

    def beside(self, *others):
        self.nearest = flip(behind(self.shard, others), "x", 1, 2)

    def along_one(self, *others):
        both = jnp.concatenate([self.half, self.second], axis=0)
        self.line = flip(behind(both, others), "z", 1, 4)

    def across(self, *others):
        self.rest = rest = behind(jnp.concatenate([self.second, self.line], axis=0), others)
        self.over = flip(rest, "x", 1, 2), flip(rest, "y", 1, 2)

    def direct(self):
        self.corners = (diagonal(self.rest),)

    def corner(self, *others):
        rows = self.shard.shape[2] // 2
        over_x, over_y = self.over
        corners = (
            flip(behind(over_y[:, :, :rows], others), "x", 1, 2),
            flip(behind(over_x[:, :, rows:], others), "y", 1, 2),
        )
        self.corners = lax.optimization_barrier(corners)

    def cores(self, early=(), late=()):
        rows = self.shard.shape[2] // 2
        deep = (2, 1, 3)
        pieces = [
            (self.shard, [(None, 0, 0)], 0),
            (self.nearest, [(None, 0, 1)], 0),
            (self.rest, [(0, dz, 0) for dz in deep], 0),
            (self.over[0], [(0, dz, 1) for dz in deep], 0),
            (self.over[1], [(1, dz, 0) for dz in deep], 0),
        ]
        for index, array in enumerate(self.corners):
            pieces.append((array, [(1, dz, 1) for dz in deep], index * rows))
        self.found = []
        for index, (array, slots, first) in enumerate(pieces):
            others = late if index > 4 else early if index > 2 else ()
            other = flip(behind(array, others), "c", 1, 2)
            self.found.append((array, [slot + (0,) for slot in slots], first))
            self.found.append((other, [slot + (1,) for slot in slots], first))


class Grid:
    axes = ("y", "z", "x", "c")
    shard_axes = ("z", "x", "c")

    def weights(self, low, x, back):
        half = low.shape[3] // 2
        first, second = lax.dynamic_slice_in_dim(low, lax.axis_index("y") * half, half, 3)
        one, two = Gather(low[0], first), Gather(low[1], second)
        one.along_two()
        one.beside()
        self.pixels = x
        self.sides = flip(x, "x", 1, 2), flip(x, "y", 1, 2)
        one.along_one(x, one.nearest)
        two.along_two(one.line)
        one.across(back, *self.sides)
        two.along_one(*one.over)
        two.beside(*self.sides)
        one.corner()
        one.cores()
        two.across(two.nearest, *one.corners)
        two.direct()
        self.second = two
        return Pieces(one.found)

    def second_weights(self, stats, gathered, *others):
        self.second.cores((stats,), (gathered, *others))
        self.corners = (diagonal(behind(self.pixels, (stats,))),)
        return Pieces(self.second.found)

    def turned_shapes(self, canvas, channels):
        return (((2, channels // 8, canvas.lanes), BF16),) * 4

    def turned_scratch(self, canvas, channels):
        return (pltpu.VMEM((channels, canvas.lanes), BF16),)

    def send(self, own, over_x, over_y, corner):
        return own, flip(over_x, "x", 1, 2), flip(over_y, "y", 1, 2), diagonal(corner)

    def chip_sum(self, canvas, moved, layer, channels, after):
        out = (4, TAPS, channels // 32, channels)
        part = moved[0].shape[1]
        send, keep = call(
            functools.partial(kernel_grad_layer, canvas),
            (),
            (),
            (
                pltpu.VMEM((4, *moved[0].shape), BF16),
                pltpu.VMEM((4, canvas.sent_rows, channels), BF16),
                pltpu.VMEM((2, TAPS * part, canvas.rows), BF16),
                pltpu.VMEM((TAPS * part, channels), F32),
                pltpu.VMEM(out, BF16),
                pltpu.VMEM(out, F32),
                pltpu.SemaphoreType.DMA((10,)),
            ),
            (*moved, *layer),
            after,
            kept=((out, BF16), (out, F32)),
        )
        return send, keep

    def core_sum(self, chip, *others):
        send, keep = chip
        other = flip(behind(send, others), "c", 1, 2)
        parts = [(keep[place] + other[place].astype(F32)).astype(BF16) for place in range(1, 4)]
        return (keep[0], other[0]), *parts

    def line(self, parts):
        return [flip(part, "z", place, 4) for place, part in enumerate(parts[1:], 1)]

    def line_sum(self, parts, found, *others):
        keep, other = lax.optimization_barrier((*parts[0], *others))[:2]
        total = keep + other.astype(F32)
        for part in found:
            total = total + part.astype(F32)
        return total

    def owned(self, line):
        own = line.astype(BF16)
        other = flip(own, "y", 1, 2)
        first = lax.axis_index("y") == 0
        halves = [jnp.where(first, own, other), jnp.where(first, other, own)]
        return jnp.concatenate(halves, axis=1).astype(F32)


class Plain:
    axes = ("dp", "fsdp")
    shard_axes = ("fsdp",)

    sides = corners = ()

    def weights(self, low, x, back):
        full = lax.all_gather(low, "fsdp", axis=2, tiled=True)
        first, self.second = [Whole(array, low.shape[2]) for array in full]
        return first

    def second_weights(self, stats, gathered, *others):
        return self.second

    def turned_shapes(self, canvas, channels):
        return (((channels, canvas.rows), BF16),)

    def turned_scratch(self, canvas, channels):
        return ()

    def send(self, turned):
        return (turned,)

    def chip_sum(self, canvas, moved, layer, channels, after):
        (full,) = call(
            functools.partial(kernel_grad_whole, canvas),
            (*moved, layer[0]),
            (((TAPS, channels, channels), BF16),),
            (pltpu.VMEM((canvas.padded_rows, channels), F32),),
            after=after,
        )
        return (full,)

    def core_sum(self, chip, *others):
        return chip

    def line(self, parts):
        return ()

    def line_sum(self, parts, found, *others):
        return lax.psum_scatter(parts[0], "fsdp", scatter_dimension=1, tiled=True)

    def owned(self, line):
        return lax.psum(line, "dp").astype(F32)


def local(
    ways,
    sizes,
    field_five,
    field_seven,
    field_nine,
    mask_five,
    mask_seven,
    mask_nine,
    back_five,
    back_seven,
    back_nine,
    kernels,
    norm_params,
    kernel_first,
    kernel_second,
    norm_first,
    norm_second,
):
    copies, shards = sizes
    fields = (field_five, field_seven, field_nine)
    masks = (mask_five, mask_seven, mask_nine)
    backs = (back_five, back_seven, back_nine)
    channels = field_five.shape[3]
    width = kernels.shape[4]
    canvas = Canvas([(field.shape[0], field.shape[1]) for field in fields])
    rows = canvas.rows
    count = copies * shards

    def turned(kernel):
        return jnp.transpose(kernel, (0, 1, 2, 4, 3)).reshape(2, TAPS, width, channels)

    def exchange(spread):
        return lax.all_to_all(spread, ways.axes, 0, 0, tiled=True)

    kernels_turned = turned(kernels)
    low = kernels_turned.astype(BF16)

    buffer = pltpu.VMEM((rows, channels), F32)
    weighted = (
        pltpu.VMEM((canvas.padded_rows, channels), F32),
        pltpu.VMEM((TAPS, channels, channels), BF16),
        pltpu.SemaphoreType.DMA((3,)),
    )
    flat32 = ((rows, channels), F32)
    flat16 = ((rows, channels), BF16)
    two = ((count, 2, channels), F32)
    norm = ((4, channels), F32)
    sums = ((2, channels), F32)
    turned_shapes = ways.turned_shapes(canvas, channels)
    turned_scratch = ways.turned_scratch(canvas, channels)

    full = ((TAPS, channels, channels), BF16)

    bounds = (*range(0, rows - LANES, LANES), rows)

    bounds = (*range(0, rows - LANES, LANES), rows)

    def conv_call(body, source, inputs, outputs, after=()):
        return call(
            functools.partial(body, canvas, source),
            inputs,
            outputs,
            weighted,
            source.arrays,
            after,
        )

    x, mask, info = call(
        functools.partial(prepare, canvas),
        (*[jnp.transpose(field, (1, 2, 0, 3)) for field in fields], norm_params),
        (((canvas.sent_rows, channels), BF16), ((rows, LANES), F32), ((2, LANES), F32)),
        (buffer,),
        scalars=[jnp.transpose(mask, (1, 0, 2)) for mask in masks],
    )
    (back,) = call(
        functools.partial(prepare_back, canvas),
        [jnp.transpose(field, (1, 2, 0, 3)) for field in backs],
        (flat16,),
        (buffer,),
    )
    weight_one = ways.weights(low, x, back)
    sides = ways.sides
    hidden, stats = conv_call(
        forward_one,
        weight_one,
        (x, mask, info),
        (flat32, ((count, 2, channels + LANES), F32)),
        after=sides,
    )
    gathered = exchange(stats)
    side = ()
    weight_two = ways.second_weights(stats, gathered, *side)
    active, second, norm_one, params, counts, stats = conv_call(
        forward_two,
        weight_two,
        (hidden, gathered, mask),
        (flat16, flat32, norm, norm, ((count, channels), F32), two),
        after=side,
    )
    gathered = exchange(stats)
    actives = (active,)

    def side_call(sent, after, kept=()):
        return call(
            functools.partial(side_active, canvas, weight_one, len(sent)),
            (norm_one, params),
            (((len(sent), rows, channels), BF16),),
            (
                *weighted,
                pltpu.VMEM((rows, channels), F32),
                pltpu.VMEM((len(sent), canvas.sent_rows, channels), BF16),
                pltpu.SemaphoreType.DMA,
            ),
            (*weight_one.arrays, *sent),
            after,
            kept=kept,
        )

    if sides:
        found, full_one = side_call(sides, (stats,), (full,))
        weight_one = Whole(full_one, weight_one.width)
        actives += (found,)
    result, grad_sum, norm_two, stats = call(
        turn,
        (second, gathered, counts, params, mask, x, back),
        (flat16, flat32, norm, two),
        after=actives[1:],
    )
    gathered = exchange(stats)
    if sides:
        actives += tuple(side_call(ways.corners, (stats,)))
    sums_two, *turned_two, inner_two = call(
        functools.partial(norm_back, 2),
        (norm_two, gathered, params),
        (sums, *turned_shapes),
        turned_scratch,
        late=(grad_sum, second, mask),
        streams=(flat16,),
        bounds=bounds,
        after=actives[2:],
    )
    moved_two = ways.send(*turned_two)
    grad_hidden, stats = conv_call(
        backward_middle, weight_two, (inner_two, hidden, norm_one, params, mask), (flat32, two)
    )
    gathered = exchange(behind(stats, moved_two[1:]))
    chip_two = ways.chip_sum(canvas, moved_two, actives, channels, (grad_hidden,))
    layer_x = (x, *sides, *ways.corners)
    sums_one, *turned_one, inner_one = call(
        functools.partial(norm_back, 0),
        (norm_one, gathered, params),
        (sums, *turned_shapes),
        turned_scratch,
        late=(grad_hidden, hidden, mask),
        streams=(flat16,),
        bounds=bounds,
        after=chip_two,
    )
    moved_one = ways.send(*turned_one)
    core_two = ways.core_sum(chip_two, gathered)
    line_two = ways.line(core_two)
    chip_one = ways.chip_sum(canvas, moved_one, layer_x, channels, core_two[1:])
    core_one = ways.core_sum(chip_one, *line_two)
    shapes = [(side, side, images, channels) for images, side in canvas.shapes]
    finished = call(
        functools.partial(backward_input, canvas, weight_one),
        (inner_one, grad_sum, mask, result),
        [(shape, BF16) for shape in shapes] + [(shape, F32) for shape in shapes],
        (*weighted, buffer),
        weight_one.arrays,
        core_one[1:],
    )
    owned_two = ways.owned(ways.line_sum(core_two, line_two, finished[0]))
    owned_one = ways.owned(ways.line_sum(core_one, ways.line(core_one), finished[0]))

    results = adamw(
        kernels_turned,
        jnp.stack([owned_one, owned_two]),
        turned(kernel_first),
        turned(kernel_second),
        KERNEL_RATE,
        KERNEL_DECAY,
    )
    kernel_results = [
        jnp.transpose(value.reshape(2, 3, 3, width, channels), (0, 1, 2, 4, 3))
        for value in results
    ]
    norm_full = jnp.concatenate([behind(sums_one, finished[:1]), sums_two], axis=0)
    place = lax.axis_index(ways.shard_axes) * width
    norm_grads = lax.dynamic_slice_in_dim(norm_full, place, width, 1)
    norm_results = adamw(norm_params, norm_grads, norm_first, norm_second, NORM_RATE, 0.0)
    return (
        *[jnp.transpose(array, (2, 0, 1, 3)) for array in finished],
        *kernel_results,
        *norm_results,
    )


def solution(mesh):
    sizes = (mesh.shape["dp"], mesh.shape["fsdp"])
    if sizes == (2, 16):
        ways = Grid()
        mesh = Mesh(mesh.devices.reshape(2, 4, 2, 2), ways.axes)
    else:
        ways = Plain()
    images = P(ways.axes, None, None, None)
    maps = P(ways.axes, None, None)
    weights = P(None, None, None, None, ways.shard_axes)
    norms = P(None, ways.shard_axes)
    in_specs = (
        (images,) * 3 + (maps,) * 3 + (images,) * 3 + (weights, norms, weights, weights, norms, norms)
    )
    out_specs = (images,) * 6 + (weights,) * 3 + (norms,) * 3
    body = functools.partial(local, ways, sizes)
    return jax.shard_map(body, mesh=mesh, in_specs=in_specs, out_specs=out_specs, check_vma=False)
```

```python
import functools

import jax
import jax.numpy as jnp
from jax import lax
from jax.experimental import pallas as pl
from jax.experimental.pallas import tpu as pltpu
from jax.sharding import Mesh, PartitionSpec as P

STEP = 5
NORM_EPS = 1e-05
BETA_ONE = 0.5
BETA_TWO = 0.5
KERNEL_RATE = 0.03
NORM_RATE = 0.4
KERNEL_DECAY = 0.01
ADAM_EPS = 1e-08
TAPS = 9
LANES = 128
CELL = 2
VMEM_BYTES = 53 * 1024 * 1024
F32, BF16 = jnp.float32, jnp.bfloat16


def round_up(value, step):
    return (value + step - 1) // step * step


class Canvas:
    def __init__(self, shapes):
        self.shapes = shapes
        cells = [
            (side, group, first)
            for group, (count, side) in enumerate(shapes)
            for first in range(0, count, CELL)
        ]
        limit = max(
            sum(side + 1 for side, group, _ in cells if group == wanted)
            for wanted in range(len(shapes))
        )
        self.bands = []
        for side, group, first in sorted(cells, reverse=True):
            used = sum(cell[0] + 1 for cell in self.bands[-1]) if self.bands else limit
            if used + side + 1 > limit:
                self.bands.append([])
            self.bands[-1].append((side, group, first))
        self.width = limit
        self.right = CELL
        self.down = limit * CELL
        self.heights = [band[0][0] for band in self.bands]
        used_rows = (sum(self.heights) + len(self.bands) - 1) * self.down
        self.rows = round_up(used_rows, 16)
        self.halo = round_up(self.down + self.right, 8)
        self.lanes = round_up(self.rows + self.down + self.right, LANES)
        self.padded_rows = self.rows + 2 * self.halo
        self.sent_rows = self.rows + 16

    def cells(self):
        start = 0
        for band, height in zip(self.bands, self.heights):
            column = 0
            for side, group, first in band:
                yield side, group, first, start * self.down + column * CELL
                column += side + 1
            start += height + 1

    def shift(self, tap):
        return (tap // 3 - 1) * self.down + (tap % 3 - 1) * self.right

    def place(self, buffer, value):
        edge = jnp.zeros((self.halo, value.shape[1]), F32)
        buffer[0 : self.halo, :] = edge
        buffer[self.halo : self.halo + self.rows, :] = value
        buffer[self.halo + self.rows :, :] = edge

    def shifted(self, buffer, tap, sign):
        start = self.halo + sign * self.shift(tap)
        return buffer[start : start + self.rows, :].astype(BF16)


def wide(mask, channels):
    return jnp.concatenate([mask[...]] * (channels // LANES), axis=1)


def multiply(left, right, left_dim, right_dim):
    return lax.dot_general(
        left, right, (((left_dim,), (right_dim,)), ((), ())), preferred_element_type=F32
    )


def column_sum(value):
    return jnp.sum(value, axis=0, keepdims=True)


def spread_rows(rows, ref):
    ref[...] = jnp.broadcast_to(jnp.concatenate(rows, axis=0)[None], ref.shape)


def local_statistics(hidden, valid, *refs):
    total = column_sum(hidden * valid)
    centre = total / jnp.maximum(column_sum(valid), 1.0)
    squares = column_sum(jnp.square(hidden - centre) * valid)
    rows = jnp.concatenate([total, squares], axis=0)
    *info, ref = [ref[...] for ref in refs[:-1]] + [refs[-1]]
    rows = jnp.concatenate([rows, *info], axis=1)
    ref[...] = jnp.broadcast_to(rows[None], ref.shape)


def global_statistics(gathered, counts):
    channels = counts.shape[1]
    totals, squares = gathered[:, 0, :channels], gathered[:, 1, :channels]
    total = column_sum(counts)
    centre = column_sum(totals) / total
    between = column_sum(counts * jnp.square(totals / jnp.maximum(counts, 1.0) - centre))
    spread = (column_sum(squares) + between) / total
    return centre, lax.rsqrt(spread + NORM_EPS), total


def lay_out(canvas, field_refs, buffer):
    buffer[...] = jnp.zeros_like(buffer)
    for side, group, first, start in canvas.cells():
        for down in range(side):
            for right in range(side):
                row = start + down * canvas.down + right * CELL
                pair = field_refs[group][down, right, first : first + CELL, :]
                buffer[row : row + CELL, :] = pair.astype(F32)


def prepare(canvas, *refs):
    *field_refs, param_ref = refs[:4]
    mask_refs = refs[4:7]
    x_ref, mask_ref, info_ref, buffer = refs[7:]
    rows, channels = buffer.shape
    mask_ref[...] = jnp.zeros_like(mask_ref)
    for side, group, first, start in canvas.cells():
        for down in range(side):
            for right in range(side):
                for image in range(CELL):
                    row = start + down * canvas.down + right * CELL + image
                    value = mask_refs[group][down, first + image, right].astype(F32)
                    mask_ref[row : row + 1, :] = jnp.full((1, LANES), value, F32)
    lay_out(canvas, field_refs, buffer)
    x_ref[0:rows, :] = (buffer[...] * wide(mask_ref, channels)).astype(BF16)
    line = jnp.transpose(mask_ref[...])[0:1]
    rest = jnp.zeros((1, channels * 2 - rows), F32)
    lines = [line[:, :channels], jnp.concatenate([line[:, channels:], rest], axis=1)]
    lines.append(jnp.zeros((14, channels), F32))
    x_ref[rows:, :] = jnp.concatenate(lines, axis=0).astype(BF16)
    params = param_ref[...].astype(BF16).astype(F32)
    rows = [params[index : index + 1] for index in range(4)]
    if params.size < LANES:
        rows.append(jnp.zeros((1, LANES - params.size), F32))
    row = jnp.concatenate(rows, axis=1)
    info_ref[...] = jnp.concatenate([row, column_sum(mask_ref[...])], axis=0)


def sent_mask(canvas, lines):
    channels = lines.shape[1]
    turned = jnp.transpose(lines)
    column = jnp.concatenate([turned[:, 0:1], turned[: canvas.rows - channels, 1:2]], axis=0)
    return jnp.broadcast_to(column, (canvas.rows, channels))


def prepare_back(canvas, *refs):
    *field_refs, back_ref, buffer = refs
    lay_out(canvas, field_refs, buffer)
    back_ref[...] = buffer[...].astype(BF16)


def sigmoid(value):
    return 1.0 / (1.0 + jnp.exp(-value))


def swish_slope(value):
    logistic = sigmoid(value)
    return logistic * (1.0 + value * (1.0 - logistic))


class Whole:
    def __init__(self, array, width):
        self.arrays = self.last = [array]
        self.width = width

    @staticmethod
    def start(refs, weight, sems):
        for part in range(3):
            taps = pl.ds(3 * part, 3)
            pltpu.make_async_copy(refs[0].at[taps], weight.at[taps], sems.at[part]).start()


class Pieces:
    width = 32

    def __init__(self, pieces):
        self.arrays = [array for array, _, _ in pieces]
        self.last = self.arrays[-4:]
        self.places = [(slots, first) for _, slots, first in pieces]

    def start(self, refs, weight, sems):
        y, z, x, c = (lax.axis_index(name) for name in ("y", "z", "x", "c"))
        moves = []
        for ref, (slots, first) in zip(refs, self.places):
            _, _, rows, lanes = ref.shape
            for slot, (dy, dz, dx, dc) in enumerate(slots):
                shard = ((z ^ dz) * 2 + (x ^ dx)) * 2 + (c ^ dc)
                row = pl.multiple_of(shard * self.width + first, 16)
                lane = 0 if dy is None else pl.multiple_of((y ^ dy) * lanes, lanes)
                moves.append((ref.at[slot], pl.ds(row, rows), pl.ds(lane, lanes)))
        for part in range(3):
            taps = pl.ds(3 * part, 3)
            for source, row, lane in moves:
                target = weight.at[taps, row, lane]
                pltpu.make_async_copy(source.at[taps], target, sems.at[part]).start()


class Fetch:
    def __init__(self, source, refs, weight, sems, target=None):
        self.weight, self.sems, self.target = weight, sems, target
        self.waiting = [0, 1, 2]
        source.start(refs, weight, sems)

    def ready(self, tap, when=None):
        if tap % 3 or not self.waiting:
            return
        part = self.waiting.pop(0)

        def wait():
            taps = self.weight.at[pl.ds(3 * part, 3)]
            pltpu.make_async_copy(taps, taps, self.sems.at[part]).wait()
            if not self.waiting and self.target is not None:
                pltpu.make_async_copy(self.weight, self.target, self.sems.at[0]).start()

        wait() if when is None else pl.when(when)(wait)

    def finish(self):
        pltpu.make_async_copy(self.weight, self.target, self.sems.at[0]).wait()


def convolve(canvas, value, fetch, buffer, out_ref, sign, halves=False, when=None):
    canvas.place(buffer, value)
    if not halves:
        for tap in range(TAPS):
            part = canvas.shifted(buffer, tap, sign)
            fetch.ready(tap, when)
            product = multiply(part, fetch.weight[tap], 1, 1 if sign > 0 else 0)
            out_ref[...] = product if tap == 0 else out_ref[...] + product
        return
    for tap in range(TAPS):
        fetch.ready(tap)
    width = out_ref.shape[1] // 2

    def half(index, carry):
        columns = pl.ds(pl.multiple_of(index * width, width), width)
        for tap in range(TAPS):
            part = canvas.shifted(buffer, tap, sign)
            weight = fetch.weight[tap, columns] if sign > 0 else fetch.weight[tap, :, columns]
            product = multiply(part, weight, 1, 1 if sign > 0 else 0)
            out_ref[:, columns] = product if tap == 0 else out_ref[:, columns] + product
        return carry

    lax.fori_loop(0, 2, half, 0)


def activate(hidden, norm_ref, param_ref, valid):
    normed = (hidden - norm_ref[0:1, :]) * norm_ref[1:2, :]
    value = normed * param_ref[0:1, :] + param_ref[1:2, :]
    return value * sigmoid(value) * valid


def side_hidden(canvas, source, count, *refs):
    weights, refs = refs[: len(source.arrays)], refs[len(source.arrays) :]
    sent_hbm, refs = refs[:count], refs[count:]
    hidden_ref, full, buffer, weight, sems, sent, sent_sem = refs
    copies = [
        pltpu.make_async_copy(hbm, sent.at[index], sent_sem) for index, hbm in enumerate(sent_hbm)
    ]
    for copy in copies:
        copy.start()
    fetch = Fetch(source, weights, weight, sems, full)
    for copy in copies:
        copy.wait()

    def image(index, carry):
        pixels = sent[index, 0 : canvas.rows, :].astype(F32)
        convolve(canvas, pixels, fetch, buffer, hidden_ref.at[index], 1, when=index == 0)
        return carry

    lax.fori_loop(0, count, image, 0)
    fetch.finish()


def side_activate(canvas, hidden_ref, norm_ref, param_ref, *refs):
    *sent_hbm, active_ref, lines, sent_sem = refs
    copies = []
    for index, hbm in enumerate(sent_hbm):
        tail = hbm.at[pl.ds(canvas.rows, 16)]
        copies.append(pltpu.make_async_copy(tail, lines.at[index], sent_sem))
    for copy in copies:
        copy.start()
    for copy in copies:
        copy.wait()

    def image(index, carry):
        valid = sent_mask(canvas, lines[index].astype(F32))
        active = activate(hidden_ref[index], norm_ref, param_ref, valid)
        active_ref[index] = active.astype(BF16)
        return carry

    lax.fori_loop(0, len(sent_hbm), image, 0)


def side_active(canvas, source, count, *refs):
    norm_ref, param_ref, *refs = refs
    weights, refs = refs[: len(source.arrays)], refs[len(source.arrays) :]
    sent_hbm, refs = refs[:count], refs[count:]
    active_ref, buffer, weight, sems, hidden, sent, sent_sem = refs
    copies = [
        pltpu.make_async_copy(hbm, sent.at[index], sent_sem) for index, hbm in enumerate(sent_hbm)
    ]
    for copy in copies:
        copy.start()
    fetch = Fetch(source, weights, weight, sems)
    for copy in copies:
        copy.wait()

    def image(index, carry):
        pixels = sent[index].astype(F32)
        convolve(canvas, pixels[: canvas.rows], fetch, buffer, hidden, 1, when=index == 0)
        valid = sent_mask(canvas, pixels[canvas.rows :])
        active = activate(hidden[...], norm_ref, param_ref, valid)
        active_ref[index] = active.astype(BF16)
        return carry

    lax.fori_loop(0, count, image, 0)


def forward_one(canvas, source, x_ref, mask_ref, info_ref, *refs):
    *weights, hidden_ref, stats_ref, buffer, weight, sem = refs
    fetch = Fetch(source, weights, weight, sem)
    convolve(canvas, x_ref[0 : canvas.rows, :].astype(F32), fetch, buffer, hidden_ref, 1)
    local_statistics(hidden_ref[...], wide(mask_ref, x_ref.shape[1]), info_ref, stats_ref)


def forward_two(canvas, source, hidden_ref, gathered_ref, mask_ref, *refs):
    *weights, active_ref, second_ref, norm_ref, param_ref, count_ref, stats_ref = refs[:-3]
    buffer, weight, sem = refs[-3:]
    fetch = Fetch(source, weights, weight, sem)
    channels = hidden_ref.shape[1]
    valid = wide(mask_ref, channels)
    width = source.width
    rows = []
    for index in range(4):
        start = channels + index * width
        rows.append(
            jnp.concatenate(
                [gathered_ref[shard, 0:1, start : start + width] for shard in range(channels // width)],
                axis=1,
            )
        )
    param_ref[...] = jnp.concatenate(rows, axis=0)
    counts = gathered_ref[:, 1, channels : channels + LANES]
    count_ref[...] = jnp.concatenate([counts] * (channels // LANES), axis=1)

    centre, inv, total = global_statistics(gathered_ref, count_ref[...])
    norm_ref[...] = jnp.concatenate([centre, inv, total, total], axis=0)
    value = activate(hidden_ref[...], norm_ref, param_ref, valid)
    active_ref[...] = value.astype(BF16)
    convolve(canvas, value, fetch, buffer, second_ref, 1)
    local_statistics(second_ref[...], valid, stats_ref)


def turn(
    second_ref,
    gathered_ref,
    count_ref,
    param_ref,
    mask_ref,
    x_ref,
    back_ref,
    result_ref,
    grad_ref,
    norm_ref,
    stats_ref,
):
    valid = wide(mask_ref, second_ref.shape[1])
    centre, inv, total = global_statistics(gathered_ref, count_ref[...])
    norm_ref[...] = jnp.concatenate([centre, inv, total, total], axis=0)
    normed = (second_ref[...] - centre) * inv
    rows = second_ref.shape[0]
    summed = normed * param_ref[2:3, :] + param_ref[3:4, :] + x_ref[0:rows, :].astype(F32)
    logistic = sigmoid(summed)
    result_ref[...] = (summed * logistic * valid).astype(BF16)
    slope = logistic * (1.0 + summed * (1.0 - logistic))
    grad = back_ref[...].astype(F32) * valid * slope
    grad_ref[...] = grad
    spread_rows([column_sum(grad), column_sum(grad * normed)], stats_ref)


def norm_back(row, norm_ref, gathered_ref, param_ref, sums_ref, *turned_refs, moving):
    grad_in, hidden, mask, inner_out = moving
    channels = norm_ref.shape[1]
    shift_grad = column_sum(gathered_ref[:, 0, :])
    gain_grad = column_sum(gathered_ref[:, 1, :])
    sums_ref[...] = jnp.concatenate([gain_grad, shift_grad], axis=0)
    centre, inv, total = norm_ref[0:1, :], norm_ref[1:2, :], norm_ref[2:3, :]
    gain = param_ref[row : row + 1, :] * inv
    full = turned_refs[-1]
    for part, (start, stop) in enumerate(inner_out.spans):
        normed = (hidden.part(part) - centre) * inv
        grad = grad_in.part(part) - shift_grad / total - normed * (gain_grad / total)
        inner = wide(mask.part(part), channels) * gain * grad
        inner_out.put(part, inner.astype(BF16))
        full[:, start:stop] = jnp.transpose(inner).astype(BF16)
    if len(turned_refs) == 1:
        return
    rows = inner_out.spans[-1][1]
    full[:, rows:] = jnp.zeros((channels, full.shape[1] - rows), BF16)
    y, x = lax.axis_index("y"), lax.axis_index("x")
    half = channels // 32
    for index, turned_ref in enumerate(turned_refs[:-1]):
        for c in range(2):
            for z in range(4):
                shard = (z * 2 + (x ^ (index % 2))) * 2 + c
                start = pl.multiple_of((shard * 2 + (y ^ (index // 2))) * half, half)
                turned_ref[c, z * half : (z + 1) * half, :] = full[pl.ds(start, half), :]


def backward_middle(canvas, source, inner_ref, hidden_ref, norm_ref, param_ref, mask_ref, *refs):
    *weights, grad_ref, stats_ref, buffer, weight, sem = refs
    valid = wide(mask_ref, hidden_ref.shape[1])
    fetch = Fetch(source, weights, weight, sem)
    convolve(canvas, inner_ref[...].astype(F32), fetch, buffer, grad_ref, -1)
    normed = (hidden_ref[...] - norm_ref[0:1, :]) * norm_ref[1:2, :]
    value = normed * param_ref[0:1, :] + param_ref[1:2, :]
    grad = grad_ref[...] * valid * swish_slope(value)
    grad_ref[...] = grad
    spread_rows([column_sum(grad), column_sum(grad * normed)], stats_ref)


def lay_back(canvas, flat, refs):
    for side, group, first, start in canvas.cells():
        for down in range(side):
            for right in range(side):
                row = start + down * canvas.down + right * CELL
                pair = flat[row : row + CELL, :].astype(refs[group].dtype)
                refs[group][down, right, first : first + CELL, :] = pair


def backward_input(canvas, source, inner_ref, residual_ref, mask_ref, result_ref, *refs):
    weights, refs = refs[: len(source.arrays)], refs[len(source.arrays) :]
    result_refs, grad_refs, (buffer, weight, sem, flat) = refs[:3], refs[3:6], refs[6:]
    fetch = Fetch(source, weights, weight, sem)
    convolve(canvas, inner_ref[...].astype(F32), fetch, buffer, flat, -1, True)
    flat[...] = residual_ref[...] + wide(mask_ref, flat.shape[1]) * flat[...]
    lay_back(canvas, flat, grad_refs)
    flat[...] = result_ref[...].astype(F32)
    lay_back(canvas, flat, result_refs)


def kernel_grad_whole(canvas, turned_ref, active_ref, out_ref, buffer):
    canvas.place(buffer, active_ref[0 : canvas.rows, :].astype(F32))
    for tap in range(TAPS):
        product = multiply(turned_ref[...], canvas.shifted(buffer, tap, 1), 1, 0)
        out_ref[tap] = product.astype(out_ref.dtype)


def kernel_grad_layer(canvas, *refs):
    turned_hbm, refs = refs[:4], refs[4:]
    active_hbm, (send_hbm, keep_hbm) = refs[:-9], refs[-9:-7]
    turned_ref, active_ref, left, total, send_ref, keep_ref, sems = refs[-7:]
    if len(active_hbm) < 4:
        own, pair, last = active_hbm
        active_hbm = (own, pair.at[0], pair.at[1], last.at[0])
    z, c = lax.axis_index("z"), lax.axis_index("c")
    rows, part = canvas.rows, turned_ref.shape[2]
    half = part // 4
    turns, copies = [], []
    for index, hbm in enumerate(turned_hbm):
        turns.append(pltpu.make_async_copy(hbm, turned_ref.at[index], sems.at[index]))
    for index, hbm in enumerate(active_hbm):
        target = active_ref.at[index, pl.ds(0, hbm.shape[0])]
        copies.append(pltpu.make_async_copy(hbm, target, sems.at[4 + index]))
    for pair in zip(turns, copies):
        for copy in pair:
            copy.start()
    def half_sum(core, wait):
        for index in range(4):
            slot = index % 2
            turned = turned_ref[index, c ^ core].astype(F32)
            for tap in range(TAPS):
                shift = canvas.shift(tap) % canvas.lanes
                moved = pltpu.roll(turned, shift, 1) if shift else turned
                left[slot, tap * part : (tap + 1) * part, :] = moved[:, :rows].astype(BF16)
            if wait:
                pl.when(core == 1)(copies[index].wait)
            product = multiply(left[slot], active_ref[index, 0:rows, :], 1, 0)
            total[...] = product if index == 0 else total[...] + product

    def spread(ref):
        for tap in range(TAPS):
            for place in range(4):
                row = tap * part + (z ^ place) * half
                ref[place, tap] = total[pl.ds(row, half), :].astype(ref.dtype)

    send = pltpu.make_async_copy(send_ref, send_hbm, sems.at[8])
    keep = pltpu.make_async_copy(keep_ref, keep_hbm, sems.at[9])

    for turn in turns:
        turn.wait()

    def both(step, carry):
        half_sum(1 - step, True)

        @pl.when(step == 0)
        def _():
            spread(send_ref)
            send.start()

        return carry

    lax.fori_loop(0, 2, both, 0)
    spread(keep_ref)
    keep.start()
    send.wait()
    keep.wait()


class Moving:
    def __init__(self, hbm, ref, sems, bounds, inward):
        self.ref, self.spans = ref, list(zip(bounds[:-1], bounds[1:]))
        self.copies, self.waited = [], set()
        for index, (start, stop) in enumerate(self.spans):
            far, near = hbm.at[pl.ds(start, stop - start)], ref.at[pl.ds(start, stop - start)]
            ends = (far, near) if inward else (near, far)
            self.copies.append(pltpu.make_async_copy(*ends, sems.at[index]))

    def start(self, index):
        self.copies[index].start()

    def part(self, index):
        if index not in self.waited:
            self.waited.add(index)
            self.copies[index].wait()
        start, stop = self.spans[index]
        return self.ref[start:stop, :]

    def put(self, index, value):
        start, stop = self.spans[index]
        self.ref[start:stop, :] = value
        self.copies[index].start()


def call(
    body,
    inputs,
    outputs,
    scratch=(),
    weights=(),
    after=(),
    scalars=(),
    kept=(),
    late=(),
    streams=(),
    bounds=(),
):
    whole = pl.BlockSpec(memory_space=pltpu.VMEM)
    anywhere = pl.BlockSpec(memory_space=pltpu.HBM)
    read = len(inputs) + len(scalars) + len(weights)
    moved = [(array.shape, array.dtype) for array in late] + list(streams)
    results = (*outputs, *kept, *streams)

    def split(refs, *counts):
        groups = []
        for count in counts:
            groups.append(refs[:count])
            refs = refs[count:]
        return groups

    def kernel(*refs):
        ins, far, _, outs, out_far, scratch_refs, near, sems = split(
            refs,
            read,
            len(late),
            len(after),
            len(outputs) + len(kept),
            len(streams),
            len(scratch),
            len(moved),
            len(moved),
        )
        if not moved:
            return body(*ins, *outs, *scratch_refs)
        moving = [
            Moving(hbm, ref, sem, bounds, index < len(late))
            for index, (hbm, ref, sem) in enumerate(zip((*far, *out_far), near, sems))
        ]
        for part in range(len(bounds) - 1 if len(bounds) > 2 else 0):
            for mover in moving[: len(late)]:
                mover.start(part)
        body(*ins, *outs, *scratch_refs, moving=moving)
        for mover in moving[len(late) :]:
            for copy in mover.copies:
                copy.wait()

    return pl.pallas_call(
        kernel,
        out_shape=[jax.ShapeDtypeStruct(shape, dtype) for shape, dtype in results],
        in_specs=[whole] * len(inputs)
        + [pl.BlockSpec(memory_space=pltpu.SMEM)] * len(scalars)
        + [anywhere] * (len(weights) + len(late) + len(after)),
        out_specs=[whole] * len(outputs) + [anywhere] * (len(kept) + len(streams)),
        scratch_shapes=list(scratch)
        + [pltpu.VMEM(shape, dtype) for shape, dtype in moved]
        + [pltpu.SemaphoreType.DMA((len(bounds) - 1,)) for _ in moved],
        compiler_params=pltpu.CompilerParams(vmem_limit_bytes=VMEM_BYTES),
    )(*inputs, *scalars, *weights, *late, *after)


def adamw(param, grad, first, second, rate, decay):
    first_new = BETA_ONE * first + (1.0 - BETA_ONE) * grad
    second_new = BETA_TWO * second + (1.0 - BETA_TWO) * grad * grad
    first_hat = first_new / (1.0 - BETA_ONE**STEP)
    second_hat = second_new / (1.0 - BETA_TWO**STEP)
    update = first_hat / (jnp.sqrt(second_hat) + ADAM_EPS)
    return (param - rate * (update + decay * param), first_new, second_new)


def flip(value, axis, bit, size):
    return lax.ppermute(value, axis, [(place, place ^ bit) for place in range(size)])


def diagonal(value):
    return lax.ppermute(value, ("y", "x"), [(place, place ^ 3) for place in range(4)])


def behind(value, others):
    return lax.optimization_barrier((value, *others))[0] if others else value


class Gather:
    def __init__(self, shard, half):
        self.shard, self.half = shard[None], half[None]

    def along_two(self, *others):
        self.second = flip(behind(self.half, others), "z", 2, 4)

    def beside(self, *others):
        self.nearest = flip(behind(self.shard, others), "x", 1, 2)

    def along_one(self, *others):
        both = jnp.concatenate([self.half, self.second], axis=0)
        self.line = flip(behind(both, others), "z", 1, 4)

    def across(self, *others):
        self.rest = rest = behind(jnp.concatenate([self.second, self.line], axis=0), others)
        self.over = flip(rest, "x", 1, 2), flip(rest, "y", 1, 2)

    def direct(self):
        self.corners = (diagonal(self.rest),)

    def corner(self, *others):
        rows = self.shard.shape[2] // 2
        over_x, over_y = self.over
        corners = (
            flip(behind(over_y[:, :, :rows], others), "x", 1, 2),
            flip(behind(over_x[:, :, rows:], others), "y", 1, 2),
        )
        self.corners = lax.optimization_barrier(corners)

    def cores(self, early=(), late=()):
        rows = self.shard.shape[2] // 2
        deep = (2, 1, 3)
        pieces = [
            (self.shard, [(None, 0, 0)], 0),
            (self.nearest, [(None, 0, 1)], 0),
            (self.rest, [(0, dz, 0) for dz in deep], 0),
            (self.over[0], [(0, dz, 1) for dz in deep], 0),
            (self.over[1], [(1, dz, 0) for dz in deep], 0),
        ]
        for index, array in enumerate(self.corners):
            pieces.append((array, [(1, dz, 1) for dz in deep], index * rows))
        self.found = []
        for index, (array, slots, first) in enumerate(pieces):
            others = late if index > 4 else early if index > 2 else ()
            other = flip(behind(array, others), "c", 1, 2)
            self.found.append((array, [slot + (0,) for slot in slots], first))
            self.found.append((other, [slot + (1,) for slot in slots], first))


class Grid:
    axes = ("y", "z", "x", "c")
    shard_axes = ("z", "x", "c")

    def weights(self, low, x, back):
        half = low.shape[3] // 2
        first, second = lax.dynamic_slice_in_dim(low, lax.axis_index("y") * half, half, 3)
        one, two = Gather(low[0], first), Gather(low[1], second)
        one.along_two()
        one.beside()
        self.pixels = x
        self.sides = flip(x, "x", 1, 2), flip(x, "y", 1, 2)
        one.along_one(x, one.nearest)
        two.along_two(one.line)
        one.across(back, *self.sides)
        two.along_one(*one.over)
        two.beside(*self.sides)
        one.corner()
        one.cores()
        two.across(two.nearest, *one.corners)
        two.direct()
        self.second = two
        return Pieces(one.found)

    def second_weights(self, stats, gathered, *others):
        self.second.cores((stats,), (gathered, *others))
        self.corners = (diagonal(behind(self.pixels, (stats,))),)
        return Pieces(self.second.found)

    def turned_shapes(self, canvas, channels):
        return (((2, channels // 8, canvas.lanes), BF16),) * 4

    def turned_scratch(self, canvas, channels):
        return (pltpu.VMEM((channels, canvas.lanes), BF16),)

    def send(self, own, over_x, over_y, corner):
        return own, flip(over_x, "x", 1, 2), flip(over_y, "y", 1, 2), diagonal(corner)

    def chip_sum(self, canvas, moved, layer, channels, after):
        out = (4, TAPS, channels // 32, channels)
        part = moved[0].shape[1]
        send, keep = call(
            functools.partial(kernel_grad_layer, canvas),
            (),
            (),
            (
                pltpu.VMEM((4, *moved[0].shape), BF16),
                pltpu.VMEM((4, canvas.sent_rows, channels), BF16),
                pltpu.VMEM((2, TAPS * part, canvas.rows), BF16),
                pltpu.VMEM((TAPS * part, channels), F32),
                pltpu.VMEM(out, BF16),
                pltpu.VMEM(out, BF16),
                pltpu.SemaphoreType.DMA((10,)),
            ),
            (*moved, *layer),
            after,
            kept=((out, BF16), (out, BF16)),
        )
        return send, keep

    def core_sum(self, chip, *others):
        send, keep = chip
        other = flip(behind(send, others), "c", 1, 2)
        parts = [(keep[place].astype(F32) + other[place].astype(F32)).astype(BF16) for place in range(1, 4)]
        return (keep[0], other[0]), *parts

    def line(self, parts):
        return [flip(part, "z", place, 4) for place, part in enumerate(parts[1:], 1)]

    def line_sum(self, parts, found, *others):
        keep, other = lax.optimization_barrier((*parts[0], *others))[:2]
        total = keep.astype(F32) + other.astype(F32)
        for part in found:
            total = total + part.astype(F32)
        return total

    def owned(self, line):
        own = line.astype(BF16)
        other = flip(own, "y", 1, 2)
        first = lax.axis_index("y") == 0
        halves = [jnp.where(first, own, other), jnp.where(first, other, own)]
        return jnp.concatenate(halves, axis=1).astype(F32)


class Plain:
    axes = ("dp", "fsdp")
    shard_axes = ("fsdp",)

    sides = corners = ()

    def weights(self, low, x, back):
        full = lax.all_gather(low, "fsdp", axis=2, tiled=True)
        first, self.second = [Whole(array, low.shape[2]) for array in full]
        return first

    def second_weights(self, stats, gathered, *others):
        return self.second

    def turned_shapes(self, canvas, channels):
        return (((channels, canvas.rows), BF16),)

    def turned_scratch(self, canvas, channels):
        return ()

    def send(self, turned):
        return (turned,)

    def chip_sum(self, canvas, moved, layer, channels, after):
        (full,) = call(
            functools.partial(kernel_grad_whole, canvas),
            (*moved, layer[0]),
            (((TAPS, channels, channels), BF16),),
            (pltpu.VMEM((canvas.padded_rows, channels), F32),),
            after=after,
        )
        return (full,)

    def core_sum(self, chip, *others):
        return chip

    def line(self, parts):
        return ()

    def line_sum(self, parts, found, *others):
        return lax.psum_scatter(parts[0], "fsdp", scatter_dimension=1, tiled=True)

    def owned(self, line):
        return lax.psum(line, "dp").astype(F32)


def local(
    ways,
    sizes,
    field_five,
    field_seven,
    field_nine,
    mask_five,
    mask_seven,
    mask_nine,
    back_five,
    back_seven,
    back_nine,
    kernels,
    norm_params,
    kernel_first,
    kernel_second,
    norm_first,
    norm_second,
):
    copies, shards = sizes
    fields = (field_five, field_seven, field_nine)
    masks = (mask_five, mask_seven, mask_nine)
    backs = (back_five, back_seven, back_nine)
    channels = field_five.shape[3]
    width = kernels.shape[4]
    canvas = Canvas([(field.shape[0], field.shape[1]) for field in fields])
    rows = canvas.rows
    count = copies * shards

    def turned(kernel):
        return jnp.transpose(kernel, (0, 1, 2, 4, 3)).reshape(2, TAPS, width, channels)

    def exchange(spread):
        return lax.all_to_all(spread, ways.axes, 0, 0, tiled=True)

    kernels_turned = turned(kernels)
    low = kernels_turned.astype(BF16)

    buffer = pltpu.VMEM((rows, channels), F32)
    weighted = (
        pltpu.VMEM((canvas.padded_rows, channels), F32),
        pltpu.VMEM((TAPS, channels, channels), BF16),
        pltpu.SemaphoreType.DMA((3,)),
    )
    flat32 = ((rows, channels), F32)
    flat16 = ((rows, channels), BF16)
    two = ((count, 2, channels), F32)
    norm = ((4, channels), F32)
    sums = ((2, channels), F32)
    turned_shapes = ways.turned_shapes(canvas, channels)
    turned_scratch = ways.turned_scratch(canvas, channels)

    full = ((TAPS, channels, channels), BF16)

    bounds = (*range(0, rows - LANES, LANES), rows)

    bounds = (*range(0, rows - LANES, LANES), rows)

    def conv_call(body, source, inputs, outputs, after=()):
        return call(
            functools.partial(body, canvas, source),
            inputs,
            outputs,
            weighted,
            source.arrays,
            after,
        )

    x, mask, info = call(
        functools.partial(prepare, canvas),
        (*[jnp.transpose(field, (1, 2, 0, 3)) for field in fields], norm_params),
        (((canvas.sent_rows, channels), BF16), ((rows, LANES), F32), ((2, LANES), F32)),
        (buffer,),
        scalars=[jnp.transpose(mask, (1, 0, 2)) for mask in masks],
    )
    (back,) = call(
        functools.partial(prepare_back, canvas),
        [jnp.transpose(field, (1, 2, 0, 3)) for field in backs],
        (flat16,),
        (buffer,),
    )
    weight_one = ways.weights(low, x, back)
    sides = ways.sides
    hidden, stats = conv_call(
        forward_one,
        weight_one,
        (x, mask, info),
        (flat32, ((count, 2, channels + LANES), F32)),
        after=sides,
    )
    gathered = exchange(stats)
    side = ()
    if sides:
        sent_images = pltpu.VMEM((len(sides), canvas.sent_rows, channels), BF16)
        *side, full_one = call(
            functools.partial(side_hidden, canvas, weight_one, len(sides)),
            (),
            (((len(sides), rows, channels), F32),),
            (*weighted, sent_images, pltpu.SemaphoreType.DMA),
            (*weight_one.arrays, *sides),
            (stats,),
            kept=(full,),
        )
        weight_one = Whole(full_one, weight_one.width)
    weight_two = ways.second_weights(stats, gathered, *side)
    active, second, norm_one, params, counts, stats = conv_call(
        forward_two,
        weight_two,
        (hidden, gathered, mask),
        (flat16, flat32, norm, norm, ((count, channels), F32), two),
        after=side,
    )
    gathered = exchange(stats)
    actives = (active,)

    def side_call(sent, after):
        return call(
            functools.partial(side_active, canvas, weight_one, len(sent)),
            (norm_one, params),
            (((len(sent), rows, channels), BF16),),
            (
                *weighted,
                pltpu.VMEM((rows, channels), F32),
                pltpu.VMEM((len(sent), canvas.sent_rows, channels), BF16),
                pltpu.SemaphoreType.DMA,
            ),
            (*weight_one.arrays, *sent),
            after,
        )

    if sides:
        (found,) = call(
            functools.partial(side_activate, canvas),
            (*side, norm_one, params),
            (((len(sides), rows, channels), BF16),),
            (pltpu.VMEM((len(sides), 16, channels), BF16), pltpu.SemaphoreType.DMA),
            sides,
            (stats,),
        )
        actives += (found,)
    result, grad_sum, norm_two, stats = call(
        turn,
        (second, gathered, counts, params, mask, x, back),
        (flat16, flat32, norm, two),
        after=actives[1:],
    )
    gathered = exchange(stats)
    if sides:
        actives += tuple(side_call(ways.corners, (stats,)))
    sums_two, *turned_two, inner_two = call(
        functools.partial(norm_back, 2),
        (norm_two, gathered, params),
        (sums, *turned_shapes),
        turned_scratch,
        late=(grad_sum, second, mask),
        streams=(flat16,),
        bounds=bounds,
        after=actives[2:],
    )
    moved_two = ways.send(*turned_two)
    grad_hidden, stats = conv_call(
        backward_middle, weight_two, (inner_two, hidden, norm_one, params, mask), (flat32, two)
    )
    gathered = exchange(behind(stats, moved_two[1:]))
    chip_two = ways.chip_sum(canvas, moved_two, actives, channels, (grad_hidden,))
    layer_x = (x, *sides, *ways.corners)
    sums_one, *turned_one, inner_one = call(
        functools.partial(norm_back, 0),
        (norm_one, gathered, params),
        (sums, *turned_shapes),
        turned_scratch,
        late=(grad_hidden, hidden, mask),
        streams=(flat16,),
        bounds=bounds,
        after=chip_two,
    )
    moved_one = ways.send(*turned_one)
    core_two = ways.core_sum(chip_two, gathered)
    line_two = ways.line(core_two)
    chip_one = ways.chip_sum(canvas, moved_one, layer_x, channels, core_two[1:])
    core_one = ways.core_sum(chip_one, *line_two)
    shapes = [(side, side, images, channels) for images, side in canvas.shapes]
    finished = call(
        functools.partial(backward_input, canvas, weight_one),
        (inner_one, grad_sum, mask, result),
        [(shape, BF16) for shape in shapes] + [(shape, F32) for shape in shapes],
        (*weighted, buffer),
        weight_one.arrays,
        core_one[1:],
    )
    owned_two = ways.owned(ways.line_sum(core_two, line_two, finished[0]))
    owned_one = ways.owned(ways.line_sum(core_one, ways.line(core_one), finished[0]))

    results = adamw(
        kernels_turned,
        jnp.stack([owned_one, owned_two]),
        turned(kernel_first),
        turned(kernel_second),
        KERNEL_RATE,
        KERNEL_DECAY,
    )
    kernel_results = [
        jnp.transpose(value.reshape(2, 3, 3, width, channels), (0, 1, 2, 4, 3))
        for value in results
    ]
    norm_full = jnp.concatenate([behind(sums_one, finished[:1]), sums_two], axis=0)
    place = lax.axis_index(ways.shard_axes) * width
    norm_grads = lax.dynamic_slice_in_dim(norm_full, place, width, 1)
    norm_results = adamw(norm_params, norm_grads, norm_first, norm_second, NORM_RATE, 0.0)
    return (
        *[jnp.transpose(array, (2, 0, 1, 3)) for array in finished],
        *kernel_results,
        *norm_results,
    )


def solution(mesh):
    sizes = (mesh.shape["dp"], mesh.shape["fsdp"])
    if sizes == (2, 16):
        ways = Grid()
        mesh = Mesh(mesh.devices.reshape(2, 4, 2, 2), ways.axes)
    else:
        ways = Plain()
    images = P(ways.axes, None, None, None)
    maps = P(ways.axes, None, None)
    weights = P(None, None, None, None, ways.shard_axes)
    norms = P(None, ways.shard_axes)
    in_specs = (
        (images,) * 3 + (maps,) * 3 + (images,) * 3 + (weights, norms, weights, weights, norms, norms)
    )
    out_specs = (images,) * 6 + (weights,) * 3 + (norms,) * 3
    body = functools.partial(local, ways, sizes)
    return jax.shard_map(body, mesh=mesh, in_specs=in_specs, out_specs=out_specs, check_vma=False)
```

```python
import functools

import jax
import jax.numpy as jnp
from jax import lax
from jax.experimental import pallas as pl
from jax.experimental.pallas import tpu as pltpu
from jax.sharding import Mesh, PartitionSpec as P

STEP = 5
NORM_EPS = 1e-05
BETA_ONE = 0.5
BETA_TWO = 0.5
KERNEL_RATE = 0.03
NORM_RATE = 0.4
KERNEL_DECAY = 0.01
ADAM_EPS = 1e-08
TAPS = 9
LANES = 128
CELL = 2
VMEM_BYTES = 53 * 1024 * 1024
F32, BF16 = jnp.float32, jnp.bfloat16


def round_up(value, step):
    return (value + step - 1) // step * step


class Canvas:
    def __init__(self, shapes):
        self.shapes = shapes
        cells = [
            (side, group, first)
            for group, (count, side) in enumerate(shapes)
            for first in range(0, count, CELL)
        ]
        limit = max(
            sum(side + 1 for side, group, _ in cells if group == wanted)
            for wanted in range(len(shapes))
        )
        self.bands = []
        for side, group, first in sorted(cells, reverse=True):
            used = sum(cell[0] + 1 for cell in self.bands[-1]) if self.bands else limit
            if used + side + 1 > limit:
                self.bands.append([])
            self.bands[-1].append((side, group, first))
        self.width = limit
        self.right = CELL
        self.down = limit * CELL
        self.heights = [band[0][0] for band in self.bands]
        used_rows = (sum(self.heights) + len(self.bands) - 1) * self.down
        self.rows = round_up(used_rows, 16)
        self.halo = round_up(self.down + self.right, 8)
        self.lanes = round_up(self.rows + self.down + self.right, LANES)
        self.padded_rows = self.rows + 2 * self.halo
        self.sent_rows = self.rows + 16

    def cells(self):
        start = 0
        for band, height in zip(self.bands, self.heights):
            column = 0
            for side, group, first in band:
                yield side, group, first, start * self.down + column * CELL
                column += side + 1
            start += height + 1

    def shift(self, tap):
        return (tap // 3 - 1) * self.down + (tap % 3 - 1) * self.right

    def place(self, buffer, value):
        edge = jnp.zeros((self.halo, value.shape[1]), F32)
        buffer[0 : self.halo, :] = edge
        buffer[self.halo : self.halo + self.rows, :] = value
        buffer[self.halo + self.rows :, :] = edge

    def shifted(self, buffer, tap, sign):
        start = self.halo + sign * self.shift(tap)
        return buffer[start : start + self.rows, :].astype(BF16)


def wide(mask, channels):
    return jnp.concatenate([mask[...]] * (channels // LANES), axis=1)


def multiply(left, right, left_dim, right_dim):
    return lax.dot_general(
        left, right, (((left_dim,), (right_dim,)), ((), ())), preferred_element_type=F32
    )


def column_sum(value):
    return jnp.sum(value, axis=0, keepdims=True)


def spread_rows(rows, ref):
    ref[...] = jnp.broadcast_to(jnp.concatenate(rows, axis=0)[None], ref.shape)


def local_statistics(hidden, valid, *refs):
    total = column_sum(hidden * valid)
    centre = total / jnp.maximum(column_sum(valid), 1.0)
    squares = column_sum(jnp.square(hidden - centre) * valid)
    rows = jnp.concatenate([total, squares], axis=0)
    *info, ref = [ref[...] for ref in refs[:-1]] + [refs[-1]]
    rows = jnp.concatenate([rows, *info], axis=1)
    ref[...] = jnp.broadcast_to(rows[None], ref.shape)


def global_statistics(gathered, counts):
    channels = counts.shape[1]
    totals, squares = gathered[:, 0, :channels], gathered[:, 1, :channels]
    total = column_sum(counts)
    centre = column_sum(totals) / total
    between = column_sum(counts * jnp.square(totals / jnp.maximum(counts, 1.0) - centre))
    spread = (column_sum(squares) + between) / total
    return centre, lax.rsqrt(spread + NORM_EPS), total


def lay_out(canvas, field_refs, buffer):
    buffer[...] = jnp.zeros_like(buffer)
    for side, group, first, start in canvas.cells():
        for down in range(side):
            for right in range(side):
                row = start + down * canvas.down + right * CELL
                pair = field_refs[group][down, right, first : first + CELL, :]
                buffer[row : row + CELL, :] = pair.astype(F32)


def prepare(canvas, *refs):
    *field_refs, param_ref = refs[:4]
    mask_refs = refs[4:7]
    x_ref, mask_ref, info_ref, buffer = refs[7:]
    rows, channels = buffer.shape
    mask_ref[...] = jnp.zeros_like(mask_ref)
    for side, group, first, start in canvas.cells():
        for down in range(side):
            for right in range(side):
                for image in range(CELL):
                    row = start + down * canvas.down + right * CELL + image
                    value = mask_refs[group][down, first + image, right].astype(F32)
                    mask_ref[row : row + 1, :] = jnp.full((1, LANES), value, F32)
    lay_out(canvas, field_refs, buffer)
    x_ref[0:rows, :] = (buffer[...] * wide(mask_ref, channels)).astype(BF16)
    line = jnp.transpose(mask_ref[...])[0:1]
    rest = jnp.zeros((1, channels * 2 - rows), F32)
    lines = [line[:, :channels], jnp.concatenate([line[:, channels:], rest], axis=1)]
    lines.append(jnp.zeros((14, channels), F32))
    x_ref[rows:, :] = jnp.concatenate(lines, axis=0).astype(BF16)
    params = param_ref[...].astype(BF16).astype(F32)
    rows = [params[index : index + 1] for index in range(4)]
    if params.size < LANES:
        rows.append(jnp.zeros((1, LANES - params.size), F32))
    row = jnp.concatenate(rows, axis=1)
    info_ref[...] = jnp.concatenate([row, column_sum(mask_ref[...])], axis=0)


def sent_mask(canvas, lines):
    channels = lines.shape[1]
    turned = jnp.transpose(lines)
    column = jnp.concatenate([turned[:, 0:1], turned[: canvas.rows - channels, 1:2]], axis=0)
    return jnp.broadcast_to(column, (canvas.rows, channels))


def prepare_back(canvas, *refs):
    *field_refs, back_ref, buffer = refs
    lay_out(canvas, field_refs, buffer)
    back_ref[...] = buffer[...].astype(BF16)


def sigmoid(value):
    return 1.0 / (1.0 + jnp.exp(-value))


def swish_slope(value):
    logistic = sigmoid(value)
    return logistic * (1.0 + value * (1.0 - logistic))


class Whole:
    def __init__(self, array, width):
        self.arrays = self.last = [array]
        self.width = width

    @staticmethod
    def start(refs, weight, sems):
        for part in range(3):
            taps = pl.ds(3 * part, 3)
            pltpu.make_async_copy(refs[0].at[taps], weight.at[taps], sems.at[part]).start()


class Pieces:
    width = 32

    def __init__(self, pieces):
        self.arrays = [array for array, _, _ in pieces]
        self.last = self.arrays[-4:]
        self.places = [(slots, first) for _, slots, first in pieces]

    def start(self, refs, weight, sems):
        y, z, x, c = (lax.axis_index(name) for name in ("y", "z", "x", "c"))
        moves = []
        for ref, (slots, first) in zip(refs, self.places):
            _, _, rows, lanes = ref.shape
            for slot, (dy, dz, dx, dc) in enumerate(slots):
                shard = ((z ^ dz) * 2 + (x ^ dx)) * 2 + (c ^ dc)
                row = pl.multiple_of(shard * self.width + first, 16)
                lane = 0 if dy is None else pl.multiple_of((y ^ dy) * lanes, lanes)
                moves.append((ref.at[slot], pl.ds(row, rows), pl.ds(lane, lanes)))
        for part in range(3):
            taps = pl.ds(3 * part, 3)
            for source, row, lane in moves:
                target = weight.at[taps, row, lane]
                pltpu.make_async_copy(source.at[taps], target, sems.at[part]).start()


class Fetch:
    def __init__(self, source, refs, weight, sems, target=None):
        self.weight, self.sems, self.target = weight, sems, target
        self.waiting = [0, 1, 2]
        source.start(refs, weight, sems)

    def ready(self, tap, when=None):
        if tap % 3 or not self.waiting:
            return
        part = self.waiting.pop(0)

        def wait():
            taps = self.weight.at[pl.ds(3 * part, 3)]
            pltpu.make_async_copy(taps, taps, self.sems.at[part]).wait()
            if not self.waiting and self.target is not None:
                pltpu.make_async_copy(self.weight, self.target, self.sems.at[0]).start()

        wait() if when is None else pl.when(when)(wait)

    def finish(self):
        pltpu.make_async_copy(self.weight, self.target, self.sems.at[0]).wait()


def convolve(canvas, value, fetch, buffer, out_ref, sign, halves=False, when=None):
    canvas.place(buffer, value)
    if not halves:
        for tap in range(TAPS):
            part = canvas.shifted(buffer, tap, sign)
            fetch.ready(tap, when)
            product = multiply(part, fetch.weight[tap], 1, 1 if sign > 0 else 0)
            out_ref[...] = product if tap == 0 else out_ref[...] + product
        return
    for tap in range(TAPS):
        fetch.ready(tap)
    width = out_ref.shape[1] // 2

    def half(index, carry):
        columns = pl.ds(pl.multiple_of(index * width, width), width)
        for tap in range(TAPS):
            part = canvas.shifted(buffer, tap, sign)
            weight = fetch.weight[tap, columns] if sign > 0 else fetch.weight[tap, :, columns]
            product = multiply(part, weight, 1, 1 if sign > 0 else 0)
            out_ref[:, columns] = product if tap == 0 else out_ref[:, columns] + product
        return carry

    lax.fori_loop(0, 2, half, 0)


def activate(hidden, norm_ref, param_ref, valid):
    normed = (hidden - norm_ref[0:1, :]) * norm_ref[1:2, :]
    value = normed * param_ref[0:1, :] + param_ref[1:2, :]
    return value * sigmoid(value) * valid


def side_hidden(canvas, source, count, *refs):
    weights, refs = refs[: len(source.arrays)], refs[len(source.arrays) :]
    sent_hbm, refs = refs[:count], refs[count:]
    hidden_ref, full, buffer, weight, sems, sent, sent_sem = refs
    copies = [
        pltpu.make_async_copy(hbm, sent.at[index], sent_sem) for index, hbm in enumerate(sent_hbm)
    ]
    for copy in copies:
        copy.start()
    fetch = Fetch(source, weights, weight, sems, full)
    for copy in copies:
        copy.wait()

    def image(index, carry):
        pixels = sent[index, 0 : canvas.rows, :].astype(F32)
        convolve(canvas, pixels, fetch, buffer, hidden_ref.at[index], 1, when=index == 0)
        return carry

    lax.fori_loop(0, count, image, 0)
    fetch.finish()


def side_activate(canvas, hidden_ref, norm_ref, param_ref, *refs):
    *sent_hbm, active_ref, lines, sent_sem = refs
    copies = []
    for index, hbm in enumerate(sent_hbm):
        tail = hbm.at[pl.ds(canvas.rows, 16)]
        copies.append(pltpu.make_async_copy(tail, lines.at[index], sent_sem))
    for copy in copies:
        copy.start()
    for copy in copies:
        copy.wait()

    def image(index, carry):
        valid = sent_mask(canvas, lines[index].astype(F32))
        active = activate(hidden_ref[index], norm_ref, param_ref, valid)
        active_ref[index] = active.astype(BF16)
        return carry

    lax.fori_loop(0, len(sent_hbm), image, 0)


def side_active(canvas, source, count, *refs):
    norm_ref, param_ref, *refs = refs
    weights, refs = refs[: len(source.arrays)], refs[len(source.arrays) :]
    sent_hbm, refs = refs[:count], refs[count:]
    active_ref, buffer, weight, sems, hidden, sent, sent_sem = refs
    copies = [
        pltpu.make_async_copy(hbm, sent.at[index], sent_sem) for index, hbm in enumerate(sent_hbm)
    ]
    for copy in copies:
        copy.start()
    fetch = Fetch(source, weights, weight, sems)
    for copy in copies:
        copy.wait()

    def image(index, carry):
        pixels = sent[index].astype(F32)
        convolve(canvas, pixels[: canvas.rows], fetch, buffer, hidden, 1, when=index == 0)
        valid = sent_mask(canvas, pixels[canvas.rows :])
        active = activate(hidden[...], norm_ref, param_ref, valid)
        active_ref[index] = active.astype(BF16)
        return carry

    lax.fori_loop(0, count, image, 0)


def forward_one(canvas, source, x_ref, mask_ref, info_ref, *refs):
    *weights, hidden_ref, stats_ref, buffer, weight, sem = refs
    fetch = Fetch(source, weights, weight, sem)
    convolve(canvas, x_ref[0 : canvas.rows, :].astype(F32), fetch, buffer, hidden_ref, 1)
    local_statistics(hidden_ref[...], wide(mask_ref, x_ref.shape[1]), info_ref, stats_ref)


def forward_two(canvas, source, hidden_ref, gathered_ref, mask_ref, *refs):
    *weights, active_ref, second_ref, norm_ref, param_ref, count_ref, stats_ref = refs[:-3]
    buffer, weight, sem = refs[-3:]
    fetch = Fetch(source, weights, weight, sem)
    channels = hidden_ref.shape[1]
    valid = wide(mask_ref, channels)
    width = source.width
    rows = []
    for index in range(4):
        start = channels + index * width
        rows.append(
            jnp.concatenate(
                [gathered_ref[shard, 0:1, start : start + width] for shard in range(channels // width)],
                axis=1,
            )
        )
    param_ref[...] = jnp.concatenate(rows, axis=0)
    counts = gathered_ref[:, 1, channels : channels + LANES]
    count_ref[...] = jnp.concatenate([counts] * (channels // LANES), axis=1)

    centre, inv, total = global_statistics(gathered_ref, count_ref[...])
    norm_ref[...] = jnp.concatenate([centre, inv, total, total], axis=0)
    value = activate(hidden_ref[...], norm_ref, param_ref, valid)
    active_ref[...] = value.astype(BF16)
    convolve(canvas, value, fetch, buffer, second_ref, 1)
    local_statistics(second_ref[...], valid, stats_ref)


def turn(
    second_ref,
    gathered_ref,
    count_ref,
    param_ref,
    mask_ref,
    x_ref,
    back_ref,
    result_ref,
    grad_ref,
    norm_ref,
    stats_ref,
):
    valid = wide(mask_ref, second_ref.shape[1])
    centre, inv, total = global_statistics(gathered_ref, count_ref[...])
    norm_ref[...] = jnp.concatenate([centre, inv, total, total], axis=0)
    normed = (second_ref[...] - centre) * inv
    rows = second_ref.shape[0]
    summed = normed * param_ref[2:3, :] + param_ref[3:4, :] + x_ref[0:rows, :].astype(F32)
    logistic = sigmoid(summed)
    result_ref[...] = (summed * logistic * valid).astype(BF16)
    slope = logistic * (1.0 + summed * (1.0 - logistic))
    grad = back_ref[...].astype(F32) * valid * slope
    grad_ref[...] = grad
    spread_rows([column_sum(grad), column_sum(grad * normed)], stats_ref)


def norm_back(row, norm_ref, gathered_ref, param_ref, sums_ref, *turned_refs, moving):
    grad_in, hidden, mask, inner_out = moving
    channels = norm_ref.shape[1]
    shift_grad = column_sum(gathered_ref[:, 0, :])
    gain_grad = column_sum(gathered_ref[:, 1, :])
    sums_ref[...] = jnp.concatenate([gain_grad, shift_grad], axis=0)
    centre, inv, total = norm_ref[0:1, :], norm_ref[1:2, :], norm_ref[2:3, :]
    gain = param_ref[row : row + 1, :] * inv
    full = turned_refs[-1]
    for part, (start, stop) in enumerate(inner_out.spans):
        normed = (hidden.part(part) - centre) * inv
        grad = grad_in.part(part) - shift_grad / total - normed * (gain_grad / total)
        inner = wide(mask.part(part), channels) * gain * grad
        inner_out.put(part, inner.astype(BF16))
        full[:, start:stop] = jnp.transpose(inner).astype(BF16)
    if len(turned_refs) == 1:
        return
    rows = inner_out.spans[-1][1]
    full[:, rows:] = jnp.zeros((channels, full.shape[1] - rows), BF16)
    y, x = lax.axis_index("y"), lax.axis_index("x")
    half = channels // 32
    for index, turned_ref in enumerate(turned_refs[:-1]):
        for c in range(2):
            for z in range(4):
                shard = (z * 2 + (x ^ (index % 2))) * 2 + c
                start = pl.multiple_of((shard * 2 + (y ^ (index // 2))) * half, half)
                turned_ref[c, z * half : (z + 1) * half, :] = full[pl.ds(start, half), :]


def backward_middle(canvas, source, inner_ref, hidden_ref, norm_ref, param_ref, mask_ref, *refs):
    *weights, grad_ref, stats_ref, buffer, weight, sem = refs
    valid = wide(mask_ref, hidden_ref.shape[1])
    fetch = Fetch(source, weights, weight, sem)
    convolve(canvas, inner_ref[...].astype(F32), fetch, buffer, grad_ref, -1)
    normed = (hidden_ref[...] - norm_ref[0:1, :]) * norm_ref[1:2, :]
    value = normed * param_ref[0:1, :] + param_ref[1:2, :]
    grad = grad_ref[...] * valid * swish_slope(value)
    grad_ref[...] = grad
    spread_rows([column_sum(grad), column_sum(grad * normed)], stats_ref)


def lay_back(canvas, flat, refs):
    for side, group, first, start in canvas.cells():
        for down in range(side):
            for right in range(side):
                row = start + down * canvas.down + right * CELL
                pair = flat[row : row + CELL, :].astype(refs[group].dtype)
                refs[group][down, right, first : first + CELL, :] = pair


def backward_input(canvas, source, inner_ref, residual_ref, mask_ref, result_ref, *refs):
    weights, refs = refs[: len(source.arrays)], refs[len(source.arrays) :]
    result_refs, grad_refs, (buffer, weight, sem, flat) = refs[:3], refs[3:6], refs[6:]
    fetch = Fetch(source, weights, weight, sem)
    convolve(canvas, inner_ref[...].astype(F32), fetch, buffer, flat, -1, True)
    flat[...] = residual_ref[...] + wide(mask_ref, flat.shape[1]) * flat[...]
    lay_back(canvas, flat, grad_refs)
    flat[...] = result_ref[...].astype(F32)
    lay_back(canvas, flat, result_refs)


def kernel_grad_whole(canvas, turned_ref, active_ref, out_ref, buffer):
    canvas.place(buffer, active_ref[0 : canvas.rows, :].astype(F32))
    for tap in range(TAPS):
        product = multiply(turned_ref[...], canvas.shifted(buffer, tap, 1), 1, 0)
        out_ref[tap] = product.astype(out_ref.dtype)


def kernel_grad_layer(canvas, *refs):
    turned_hbm, refs = refs[:4], refs[4:]
    active_hbm, (send_hbm, keep_hbm) = refs[:-9], refs[-9:-7]
    turned_ref, active_ref, left, total, send_ref, keep_ref, sems = refs[-7:]
    if len(active_hbm) < 4:
        own, pair, last = active_hbm
        active_hbm = (own, pair.at[0], pair.at[1], last.at[0])
    z, c = lax.axis_index("z"), lax.axis_index("c")
    rows, part = canvas.rows, turned_ref.shape[2]
    half = part // 4
    turns, copies = [], []
    for index, hbm in enumerate(turned_hbm):
        turns.append(pltpu.make_async_copy(hbm, turned_ref.at[index], sems.at[index]))
    for index, hbm in enumerate(active_hbm):
        target = active_ref.at[index, pl.ds(0, hbm.shape[0])]
        copies.append(pltpu.make_async_copy(hbm, target, sems.at[4 + index]))
    for pair in zip(turns, copies):
        for copy in pair:
            copy.start()
    def half_sum(core, wait):
        for index in range(4):
            slot = index % 2
            turned = turned_ref[index, c ^ core].astype(F32)
            for tap in range(TAPS):
                shift = canvas.shift(tap) % canvas.lanes
                moved = pltpu.roll(turned, shift, 1) if shift else turned
                left[slot, tap * part : (tap + 1) * part, :] = moved[:, :rows].astype(BF16)
            if wait:
                pl.when(core == 1)(copies[index].wait)
            product = multiply(left[slot], active_ref[index, 0:rows, :], 1, 0)
            total[...] = product if index == 0 else total[...] + product

    def spread(ref):
        for tap in range(TAPS):
            for place in range(4):
                row = tap * part + (z ^ place) * half
                ref[place, tap] = total[pl.ds(row, half), :].astype(ref.dtype)

    send = pltpu.make_async_copy(send_ref, send_hbm, sems.at[8])
    keep = pltpu.make_async_copy(keep_ref, keep_hbm, sems.at[9])

    for turn in turns:
        turn.wait()

    def both(step, carry):
        half_sum(1 - step, True)

        @pl.when(step == 0)
        def _():
            spread(send_ref)
            send.start()

        return carry

    lax.fori_loop(0, 2, both, 0)
    spread(keep_ref)
    keep.start()
    send.wait()
    keep.wait()


class Moving:
    def __init__(self, hbm, ref, sems, bounds, inward):
        self.ref, self.spans = ref, list(zip(bounds[:-1], bounds[1:]))
        self.copies, self.waited = [], set()
        for index, (start, stop) in enumerate(self.spans):
            far, near = hbm.at[pl.ds(start, stop - start)], ref.at[pl.ds(start, stop - start)]
            ends = (far, near) if inward else (near, far)
            self.copies.append(pltpu.make_async_copy(*ends, sems.at[index]))

    def start(self, index):
        self.copies[index].start()

    def part(self, index):
        if index not in self.waited:
            self.waited.add(index)
            self.copies[index].wait()
        start, stop = self.spans[index]
        return self.ref[start:stop, :]

    def put(self, index, value):
        start, stop = self.spans[index]
        self.ref[start:stop, :] = value
        self.copies[index].start()


def call(
    body,
    inputs,
    outputs,
    scratch=(),
    weights=(),
    after=(),
    scalars=(),
    kept=(),
    late=(),
    streams=(),
    bounds=(),
):
    whole = pl.BlockSpec(memory_space=pltpu.VMEM)
    anywhere = pl.BlockSpec(memory_space=pltpu.HBM)
    read = len(inputs) + len(scalars) + len(weights)
    moved = [(array.shape, array.dtype) for array in late] + list(streams)
    results = (*outputs, *kept, *streams)

    def split(refs, *counts):
        groups = []
        for count in counts:
            groups.append(refs[:count])
            refs = refs[count:]
        return groups

    def kernel(*refs):
        ins, far, _, outs, out_far, scratch_refs, near, sems = split(
            refs,
            read,
            len(late),
            len(after),
            len(outputs) + len(kept),
            len(streams),
            len(scratch),
            len(moved),
            len(moved),
        )
        if not moved:
            return body(*ins, *outs, *scratch_refs)
        moving = [
            Moving(hbm, ref, sem, bounds, index < len(late))
            for index, (hbm, ref, sem) in enumerate(zip((*far, *out_far), near, sems))
        ]
        for part in range(len(bounds) - 1 if len(bounds) > 2 else 0):
            for mover in moving[: len(late)]:
                mover.start(part)
        body(*ins, *outs, *scratch_refs, moving=moving)
        for mover in moving[len(late) :]:
            for copy in mover.copies:
                copy.wait()

    return pl.pallas_call(
        kernel,
        out_shape=[jax.ShapeDtypeStruct(shape, dtype) for shape, dtype in results],
        in_specs=[whole] * len(inputs)
        + [pl.BlockSpec(memory_space=pltpu.SMEM)] * len(scalars)
        + [anywhere] * (len(weights) + len(late) + len(after)),
        out_specs=[whole] * len(outputs) + [anywhere] * (len(kept) + len(streams)),
        scratch_shapes=list(scratch)
        + [pltpu.VMEM(shape, dtype) for shape, dtype in moved]
        + [pltpu.SemaphoreType.DMA((len(bounds) - 1,)) for _ in moved],
        compiler_params=pltpu.CompilerParams(vmem_limit_bytes=VMEM_BYTES),
    )(*inputs, *scalars, *weights, *late, *after)


def adamw(param, grad, first, second, rate, decay):
    first_new = BETA_ONE * first + (1.0 - BETA_ONE) * grad
    second_new = BETA_TWO * second + (1.0 - BETA_TWO) * grad * grad
    first_hat = first_new / (1.0 - BETA_ONE**STEP)
    second_hat = second_new / (1.0 - BETA_TWO**STEP)
    update = first_hat / (jnp.sqrt(second_hat) + ADAM_EPS)
    return (param - rate * (update + decay * param), first_new, second_new)


def flip(value, axis, bit, size):
    return lax.ppermute(value, axis, [(place, place ^ bit) for place in range(size)])


def diagonal(value):
    return lax.ppermute(value, ("y", "x"), [(place, place ^ 3) for place in range(4)])


def behind(value, others):
    return lax.optimization_barrier((value, *others))[0] if others else value


class Gather:
    def __init__(self, shard, half):
        self.shard, self.half = shard[None], half[None]

    def along_two(self, *others):
        self.second = flip(behind(self.half, others), "z", 2, 4)

    def beside(self, *others):
        self.nearest = flip(behind(self.shard, others), "x", 1, 2)

    def along_one(self, *others):
        both = jnp.concatenate([self.half, self.second], axis=0)
        self.line = flip(behind(both, others), "z", 1, 4)

    def across(self, *others):
        self.rest = rest = behind(jnp.concatenate([self.second, self.line], axis=0), others)
        self.over = flip(rest, "x", 1, 2), flip(rest, "y", 1, 2)

    def direct(self):
        self.corners = (diagonal(self.rest),)

    def corner(self, *others):
        rows = self.shard.shape[2] // 2
        over_x, over_y = self.over
        corners = (
            flip(behind(over_y[:, :, :rows], others), "x", 1, 2),
            flip(behind(over_x[:, :, rows:], others), "y", 1, 2),
        )
        self.corners = lax.optimization_barrier(corners)

    def cores(self, early=(), late=()):
        rows = self.shard.shape[2] // 2
        deep = (2, 1, 3)
        pieces = [
            (self.shard, [(None, 0, 0)], 0),
            (self.nearest, [(None, 0, 1)], 0),
            (self.rest, [(0, dz, 0) for dz in deep], 0),
            (self.over[0], [(0, dz, 1) for dz in deep], 0),
            (self.over[1], [(1, dz, 0) for dz in deep], 0),
        ]
        for index, array in enumerate(self.corners):
            pieces.append((array, [(1, dz, 1) for dz in deep], index * rows))
        self.found = []
        for index, (array, slots, first) in enumerate(pieces):
            others = late if index > 4 else early if index > 2 else ()
            other = flip(behind(array, others), "c", 1, 2)
            self.found.append((array, [slot + (0,) for slot in slots], first))
            self.found.append((other, [slot + (1,) for slot in slots], first))


class Grid:
    axes = ("y", "z", "x", "c")
    shard_axes = ("z", "x", "c")

    def weights(self, kernels, x, back):
        half = kernels.shape[3] // 2
        start = lax.axis_index("y") * half
        low = [kernels[0].astype(BF16), behind(kernels[1], (x,)).astype(BF16)]
        one, two = (Gather(part, lax.dynamic_slice_in_dim(part, start, half, 2)) for part in low)
        one.along_two()
        one.beside()
        self.pixels = x
        self.sides = flip(x, "x", 1, 2), flip(x, "y", 1, 2)
        one.along_one(x, one.nearest)
        two.along_two(one.line)
        one.across(back, *self.sides)
        two.along_one(*one.over)
        two.beside(*self.sides)
        one.corner()
        one.cores()
        two.across(two.nearest, *one.corners)
        two.direct()
        self.second = two
        return Pieces(one.found)

    def second_weights(self, stats, gathered, *others):
        self.second.cores((stats,), (gathered, *others))
        self.corners = (diagonal(behind(self.pixels, (stats,))),)
        return Pieces(self.second.found)

    def turned_shapes(self, canvas, channels):
        return (((2, channels // 8, canvas.lanes), BF16),) * 4

    def turned_scratch(self, canvas, channels):
        return (pltpu.VMEM((channels, canvas.lanes), BF16),)

    def send(self, own, over_x, over_y, corner):
        return own, flip(over_x, "x", 1, 2), flip(over_y, "y", 1, 2), diagonal(corner)

    def chip_sum(self, canvas, moved, layer, channels, after):
        out = (4, TAPS, channels // 32, channels)
        part = moved[0].shape[1]
        send, keep = call(
            functools.partial(kernel_grad_layer, canvas),
            (),
            (),
            (
                pltpu.VMEM((4, *moved[0].shape), BF16),
                pltpu.VMEM((4, canvas.sent_rows, channels), BF16),
                pltpu.VMEM((2, TAPS * part, canvas.rows), BF16),
                pltpu.VMEM((TAPS * part, channels), F32),
                pltpu.VMEM(out, BF16),
                pltpu.VMEM(out, BF16),
                pltpu.SemaphoreType.DMA((10,)),
            ),
            (*moved, *layer),
            after,
            kept=((out, BF16), (out, BF16)),
        )
        return send, keep

    def core_sum(self, chip, *others):
        send, keep = chip
        other = flip(behind(send, others), "c", 1, 2)
        parts = [(keep[place].astype(F32) + other[place].astype(F32)).astype(BF16) for place in range(1, 4)]
        return (keep[0], other[0]), *parts

    def line(self, parts):
        return [flip(part, "z", place, 4) for place, part in enumerate(parts[1:], 1)]

    def line_sum(self, parts, found, *others):
        keep, other = lax.optimization_barrier((*parts[0], *others))[:2]
        total = keep.astype(F32) + other.astype(F32)
        for part in found:
            total = total + part.astype(F32)
        return total

    def owned(self, line):
        own = line.astype(BF16)
        other = flip(own, "y", 1, 2)
        first = lax.axis_index("y") == 0
        halves = [jnp.where(first, own, other), jnp.where(first, other, own)]
        return jnp.concatenate(halves, axis=1).astype(F32)


class Plain:
    axes = ("dp", "fsdp")
    shard_axes = ("fsdp",)

    sides = corners = ()

    def weights(self, kernels, x, back):
        low = kernels.astype(BF16)
        full = lax.all_gather(low, "fsdp", axis=2, tiled=True)
        first, self.second = [Whole(array, low.shape[2]) for array in full]
        return first

    def second_weights(self, stats, gathered, *others):
        return self.second

    def turned_shapes(self, canvas, channels):
        return (((channels, canvas.rows), BF16),)

    def turned_scratch(self, canvas, channels):
        return ()

    def send(self, turned):
        return (turned,)

    def chip_sum(self, canvas, moved, layer, channels, after):
        (full,) = call(
            functools.partial(kernel_grad_whole, canvas),
            (*moved, layer[0]),
            (((TAPS, channels, channels), BF16),),
            (pltpu.VMEM((canvas.padded_rows, channels), F32),),
            after=after,
        )
        return (full,)

    def core_sum(self, chip, *others):
        return chip

    def line(self, parts):
        return ()

    def line_sum(self, parts, found, *others):
        return lax.psum_scatter(parts[0], "fsdp", scatter_dimension=1, tiled=True)

    def owned(self, line):
        return lax.psum(line, "dp").astype(F32)


def local(
    ways,
    sizes,
    field_five,
    field_seven,
    field_nine,
    mask_five,
    mask_seven,
    mask_nine,
    back_five,
    back_seven,
    back_nine,
    kernels,
    norm_params,
    kernel_first,
    kernel_second,
    norm_first,
    norm_second,
):
    copies, shards = sizes
    fields = (field_five, field_seven, field_nine)
    masks = (mask_five, mask_seven, mask_nine)
    backs = (back_five, back_seven, back_nine)
    channels = field_five.shape[3]
    width = kernels.shape[4]
    canvas = Canvas([(field.shape[0], field.shape[1]) for field in fields])
    rows = canvas.rows
    count = copies * shards

    def turned(kernel):
        return jnp.transpose(kernel, (0, 1, 2, 4, 3)).reshape(2, TAPS, width, channels)

    def exchange(spread):
        return lax.all_to_all(spread, ways.axes, 0, 0, tiled=True)

    kernels_turned = turned(kernels)

    buffer = pltpu.VMEM((rows, channels), F32)
    weighted = (
        pltpu.VMEM((canvas.padded_rows, channels), F32),
        pltpu.VMEM((TAPS, channels, channels), BF16),
        pltpu.SemaphoreType.DMA((3,)),
    )
    flat32 = ((rows, channels), F32)
    flat16 = ((rows, channels), BF16)
    two = ((count, 2, channels), F32)
    norm = ((4, channels), F32)
    sums = ((2, channels), F32)
    turned_shapes = ways.turned_shapes(canvas, channels)
    turned_scratch = ways.turned_scratch(canvas, channels)

    full = ((TAPS, channels, channels), BF16)

    bounds = (*range(0, rows - LANES, LANES), rows)

    bounds = (*range(0, rows - LANES, LANES), rows)

    def conv_call(body, source, inputs, outputs, after=()):
        return call(
            functools.partial(body, canvas, source),
            inputs,
            outputs,
            weighted,
            source.arrays,
            after,
        )

    x, mask, info = call(
        functools.partial(prepare, canvas),
        (*[jnp.transpose(field, (1, 2, 0, 3)) for field in fields], norm_params),
        (((canvas.sent_rows, channels), BF16), ((rows, LANES), F32), ((2, LANES), F32)),
        (buffer,),
        scalars=[jnp.transpose(mask, (1, 0, 2)) for mask in masks],
    )
    (back,) = call(
        functools.partial(prepare_back, canvas),
        [jnp.transpose(field, (1, 2, 0, 3)) for field in backs],
        (flat16,),
        (buffer,),
    )
    weight_one = ways.weights(kernels_turned, x, back)
    sides = ways.sides
    hidden, stats = conv_call(
        forward_one,
        weight_one,
        (x, mask, info),
        (flat32, ((count, 2, channels + LANES), F32)),
        after=sides,
    )
    gathered = exchange(stats)
    side = ()
    if sides:
        sent_images = pltpu.VMEM((len(sides), canvas.sent_rows, channels), BF16)
        *side, full_one = call(
            functools.partial(side_hidden, canvas, weight_one, len(sides)),
            (),
            (((len(sides), rows, channels), F32),),
            (*weighted, sent_images, pltpu.SemaphoreType.DMA),
            (*weight_one.arrays, *sides),
            (stats,),
            kept=(full,),
        )
        weight_one = Whole(full_one, weight_one.width)
    weight_two = ways.second_weights(stats, gathered, *side)
    active, second, norm_one, params, counts, stats = conv_call(
        forward_two,
        weight_two,
        (hidden, gathered, mask),
        (flat16, flat32, norm, norm, ((count, channels), F32), two),
        after=side,
    )
    gathered = exchange(stats)
    actives = (active,)

    def side_call(sent, after):
        return call(
            functools.partial(side_active, canvas, weight_one, len(sent)),
            (norm_one, params),
            (((len(sent), rows, channels), BF16),),
            (
                *weighted,
                pltpu.VMEM((rows, channels), F32),
                pltpu.VMEM((len(sent), canvas.sent_rows, channels), BF16),
                pltpu.SemaphoreType.DMA,
            ),
            (*weight_one.arrays, *sent),
            after,
        )

    if sides:
        (found,) = call(
            functools.partial(side_activate, canvas),
            (*side, norm_one, params),
            (((len(sides), rows, channels), BF16),),
            (pltpu.VMEM((len(sides), 16, channels), BF16), pltpu.SemaphoreType.DMA),
            sides,
            (stats,),
        )
        actives += (found,)
    result, grad_sum, norm_two, stats = call(
        turn,
        (second, gathered, counts, params, mask, x, back),
        (flat16, flat32, norm, two),
        after=actives[1:],
    )
    gathered = exchange(stats)
    if sides:
        actives += tuple(side_call(ways.corners, (stats,)))
    sums_two, *turned_two, inner_two = call(
        functools.partial(norm_back, 2),
        (norm_two, gathered, params),
        (sums, *turned_shapes),
        turned_scratch,
        late=(grad_sum, second, mask),
        streams=(flat16,),
        bounds=bounds,
        after=actives[2:],
    )
    moved_two = ways.send(*turned_two)
    grad_hidden, stats = conv_call(
        backward_middle, weight_two, (inner_two, hidden, norm_one, params, mask), (flat32, two)
    )
    gathered = exchange(behind(stats, moved_two[1:]))
    chip_two = ways.chip_sum(canvas, moved_two, actives, channels, (grad_hidden,))
    layer_x = (x, *sides, *ways.corners)
    sums_one, *turned_one, inner_one = call(
        functools.partial(norm_back, 0),
        (norm_one, gathered, params),
        (sums, *turned_shapes),
        turned_scratch,
        late=(grad_hidden, hidden, mask),
        streams=(flat16,),
        bounds=bounds,
        after=chip_two,
    )
    moved_one = ways.send(*turned_one)
    core_two = ways.core_sum(chip_two, gathered)
    line_two = ways.line(core_two)
    chip_one = ways.chip_sum(canvas, moved_one, layer_x, channels, core_two[1:])
    core_one = ways.core_sum(chip_one, *line_two)
    shapes = [(side, side, images, channels) for images, side in canvas.shapes]
    finished = call(
        functools.partial(backward_input, canvas, weight_one),
        (inner_one, grad_sum, mask, result),
        [(shape, BF16) for shape in shapes] + [(shape, F32) for shape in shapes],
        (*weighted, buffer),
        weight_one.arrays,
        core_one[1:],
    )
    owned_two = ways.owned(ways.line_sum(core_two, line_two, finished[0]))
    owned_one = ways.owned(ways.line_sum(core_one, ways.line(core_one), finished[0]))

    results = adamw(
        kernels_turned,
        jnp.stack([owned_one, owned_two]),
        turned(kernel_first),
        turned(kernel_second),
        KERNEL_RATE,
        KERNEL_DECAY,
    )
    kernel_results = [
        jnp.transpose(value.reshape(2, 3, 3, width, channels), (0, 1, 2, 4, 3))
        for value in results
    ]
    norm_full = jnp.concatenate([behind(sums_one, finished[:1]), sums_two], axis=0)
    place = lax.axis_index(ways.shard_axes) * width
    norm_grads = lax.dynamic_slice_in_dim(norm_full, place, width, 1)
    norm_results = adamw(norm_params, norm_grads, norm_first, norm_second, NORM_RATE, 0.0)
    return (
        *[jnp.transpose(array, (2, 0, 1, 3)) for array in finished],
        *kernel_results,
        *norm_results,
    )


def solution(mesh):
    sizes = (mesh.shape["dp"], mesh.shape["fsdp"])
    if sizes == (2, 16):
        ways = Grid()
        mesh = Mesh(mesh.devices.reshape(2, 4, 2, 2), ways.axes)
    else:
        ways = Plain()
    images = P(ways.axes, None, None, None)
    maps = P(ways.axes, None, None)
    weights = P(None, None, None, None, ways.shard_axes)
    norms = P(None, ways.shard_axes)
    in_specs = (
        (images,) * 3 + (maps,) * 3 + (images,) * 3 + (weights, norms, weights, weights, norms, norms)
    )
    out_specs = (images,) * 6 + (weights,) * 3 + (norms,) * 3
    body = functools.partial(local, ways, sizes)
    return jax.shard_map(body, mesh=mesh, in_specs=in_specs, out_specs=out_specs, check_vma=False)
```
